32 devices in a mesh: dp: 4 (over y, x), expert: 8 (over z, core).
Axes of the slice: x: 2, y: 2, z: 4, core: 2. Of those that a mesh axis runs over, the one named last changes fastest.
Arguments:
- tokens: bfloat16 [20480, 1536], P(('dp', 'expert')), may hold values from -6 to 6
- cotangent: bfloat16 [20480, 1536], P(('dp', 'expert')), may hold values from -6 to 6
- norm_attn: float32 [1536], replicated, may hold values from 0.5 to 1.5
- norm_moe: float32 [1536], replicated, may hold values from 0.5 to 1.5
- w_query: bfloat16 [1536, 1536], P('dp'), may hold values from -0.15625 to 0.15625
- key_weight: bfloat16 [1536, 256], P('dp'), may hold values from -0.15625 to 0.15625
- value_weight: bfloat16 [1536, 256], P('dp'), may hold values from -0.15625 to 0.15625
- w_out: bfloat16 [1536, 1536], P('dp'), may hold values from -0.4375 to 0.4375
- w_router: bfloat16 [1536, 8], replicated, may hold values from -0.078125 to 0.078125
- w_gate: bfloat16 [8, 1536, 768], P('expert'), may hold values from -0.15625 to 0.15625
- w_up: bfloat16 [8, 1536, 768], P('expert'), may hold values from -0.15625 to 0.15625
- w_down: bfloat16 [8, 768, 1536], P('expert'), may hold values from -1.25 to 1.25
- document_index: int32 [32, 640], P(('dp', 'expert')), may hold values from 0 to 7, never falling along the last dimension, each value on 1 to 320 neighbouring positions
- padding_token_mask: int32 [32, 640], P(('dp', 'expert')), may hold values 0 or 1
- routes: int32 [20480, 4], P(('dp', 'expert')), may hold values from 0 to 7, all different within a row
- pair_order: int32 [32, 2560], P(('dp', 'expert')), may hold values from 0 to 2559, each once within a row
Outputs:
- block_out: bfloat16 [20480, 1536], P(('dp', 'expert'))
- grad_tokens: float32 [20480, 1536], P(('dp', 'expert'))
- grad_norm_attn: float32 [1536], replicated
- grad_norm_moe: float32 [1536], replicated
- grad_query: float32 [1536, 1536], P('dp')
- grad_key: float32 [1536, 256], P('dp')
- grad_value: float32 [1536, 256], P('dp')
- grad_out: float32 [1536, 1536], P('dp')
- grad_router: float32 [1536, 8], replicated
- grad_gate: float32 [8, 1536, 768], P('expert')
- grad_up: float32 [8, 1536, 768], P('expert')
- grad_down: float32 [8, 768, 1536], P('expert')
The draws below stay inside these ranges and needn't reach their ends.
Inputs may be any that keep to these rules, and one draw needn't show every extreme that they name: `routes`: each row names 4 different experts. `document_index`: within a sequence the ids never fall and start at 0; a document has at most 320 tokens. `pair_order`: each row holds every pair index of its sequence once.
All inputs are finite; a program needn't handle non-finite values. No bound on the sum of `padding_token_mask` on one device may be relied on, other than what follows from the above.
Results may differ from the reference program's by a relative error of at most 0.023.
Values may be sent and summed in bfloat16 or wider, within the bound.
No kernel may reach another device: no remote copies, remote signals or barrier semaphores. Data moves between devices by JAX's collectives and lax.ppermute only.
A program may use at most 320 MiB of HBM per device.

```python
import math
from functools import partial
import jax
import jax.numpy as jnp
import numpy as np
from jax import lax

MODEL_WIDTH = 1536
QUERY_HEADS = 12
KEY_VALUE_HEADS = 2
HEAD_SIZE = 128
FF = 768
TOP = 4
DEVICE_TOKENS = 640
SEG_COUNT = 8
SEG_MOST = 320
SEQUENCE_TOTAL = 32
TOKENS = 20480
EXPERTS = 8
CAP = 360


def with_ends(array, rng, smallest, top_value):
    extent = array.shape
    place = [jax.random.randint(jax.random.fold_in(rng, axis), (), 0, extent[axis]) for axis in range(len(extent))]
    array = array.at[tuple(place)].set(smallest)
    longest = extent.index(max(extent))
    place[longest] = (place[longest] + 1) % extent[longest]
    return array.at[tuple(place)].set(top_value)


def shard_levels(stream_key, dims, shards, low, largest):
    def one(dim, shards_of):
        heights = jax.random.uniform(jax.random.fold_in(jax.random.fold_in(stream_key, 6), dim), (shards_of,), jnp.float32, low / len(shards), largest / len(shards))
        return jnp.repeat(jnp.exp(heights), dims[dim] // shards_of).reshape((-1,) + (1,) * (len(dims) - dim - 1))

    loudness = one(*shards[0])
    for cut in shards[1:]:
        loudness = loudness * one(*cut)
    return loudness


def choose_distinct(rng, rows, amount, top, lift):
    sequence = jax.random.permutation(jax.random.fold_in(rng, 1), amount)
    boost = sequence
    for power in range(3):
        boost = boost * boost // amount
    boost = boost * lift // amount
    lots = jax.random.randint(jax.random.fold_in(rng, 2), (rows, amount), 0, 4096) + boost
    sure = jax.random.permutation(jax.random.fold_in(rng, 3), rows)[jnp.arange(amount) % rows]
    lots = jnp.where(jnp.arange(rows)[:, None] == sure[None, :], 1 << 14, lots)
    merit = lots * amount + jnp.arange(amount)
    return lax.top_k(merit.astype(jnp.int32), top)[1].astype(jnp.int32)


def profile(number_of, total, bound, skew):
    weights = [(1 << 20) // math.isqrt(standing ** skew) + 1 for standing in range(2, number_of + 1)]
    surplus, counts = total - bound - (number_of - 1), [1] * (number_of - 1)
    while surplus > 0:
        movable = [i for i in range(number_of - 1) if counts[i] < bound]
        pool, remaining = sum([weights[i] for i in movable]), surplus
        for i in movable:
            addition = min(bound - counts[i], max(1, remaining * weights[i] // pool), surplus)
            counts[i] = counts[i] + addition
            surplus = surplus - addition
    return np.array([bound] + counts)


def ragged(rng, count, total, reach, skew):
    if count == 2:
        one = jax.random.randint(rng, (), max(1, total - reach), min(reach, total - 1) + 1)
        return jnp.stack([one, total - one])
    lengths = jnp.asarray(profile(count, total, reach, skew), jnp.int32)
    pairs = (count - 1) // 2
    source_of, sink = lengths[1:1 + 2 * pairs:2], lengths[2:2 + 2 * pairs:2]
    slack = jnp.minimum(source_of - 1, reach - sink)
    shifted = jax.random.randint(jax.random.fold_in(rng, 1), (pairs,), 0, 1 << 20) % (slack + 1)
    lengths = lengths.at[1:1 + 2 * pairs:2].set(source_of - shifted).at[2:2 + 2 * pairs:2].set(sink + shifted)
    return lengths[jax.random.permutation(jax.random.fold_in(rng, 2), count)]


def noise(stream_key, shape, spread, most, pieces=(), kind=jnp.bfloat16):
    level = shard_levels(stream_key, shape, pieces, -0.22, 0.18) if pieces else 1.0
    values = jax.random.normal(stream_key, shape, jnp.float32) * spread * level
    return jnp.minimum(jnp.maximum(values, -most), most).astype(kind)


def setup_inputs(seed: int = 0) -> dict:
    streams_of = jax.random.split(jax.random.key(seed), 17)
    return {
        "tokens": noise(streams_of[0], (TOKENS, MODEL_WIDTH), 1.0, 6.0, ((0, 32),)),
        "cotangent": noise(streams_of[1], (TOKENS, MODEL_WIDTH), 1.0, 6.0, ((0, 32),)),
        "norm_attn": jnp.clip(1.0 + 0.1 * jax.random.normal(streams_of[2], (MODEL_WIDTH,), jnp.float32), 0.5, 1.5),
        "norm_moe": jnp.clip(1.0 + 0.1 * jax.random.normal(streams_of[3], (MODEL_WIDTH,), jnp.float32), 0.5, 1.5),
        "w_query": noise(streams_of[4], (MODEL_WIDTH, QUERY_HEADS * HEAD_SIZE), MODEL_WIDTH ** -0.5, 0.15625, ((0, 4),)),
        "key_weight": noise(streams_of[5], (MODEL_WIDTH, KEY_VALUE_HEADS * HEAD_SIZE), MODEL_WIDTH ** -0.5, 0.15625, ((0, 4),)),
        "value_weight": noise(streams_of[6], (MODEL_WIDTH, KEY_VALUE_HEADS * HEAD_SIZE), MODEL_WIDTH ** -0.5, 0.15625, ((0, 4),)),
        "w_out": noise(streams_of[7], (QUERY_HEADS * HEAD_SIZE, MODEL_WIDTH), (QUERY_HEADS * HEAD_SIZE // 8) ** -0.5, 0.4375, ((0, 4),)),
        "w_router": noise(streams_of[8], (MODEL_WIDTH, EXPERTS), (4 * MODEL_WIDTH) ** -0.5, 0.078125),
        "w_gate": noise(streams_of[9], (EXPERTS, MODEL_WIDTH, FF), MODEL_WIDTH ** -0.5, 0.15625, ((0, 8),)),
        "w_up": noise(streams_of[10], (EXPERTS, MODEL_WIDTH, FF), MODEL_WIDTH ** -0.5, 0.15625, ((0, 8),)),
        "w_down": noise(streams_of[11], (EXPERTS, FF, MODEL_WIDTH), (max(1, 2 * FF // (EXPERTS * EXPERTS))) ** -0.5, 1.25, ((0, 8),)),
        "document_index": jax.vmap(lambda own: jnp.searchsorted(jnp.cumsum(ragged(own, SEG_COUNT, DEVICE_TOKENS, SEG_MOST, 2)), jnp.arange(DEVICE_TOKENS), side="right"))(jax.random.split(streams_of[12], SEQUENCE_TOTAL)).reshape((SEQUENCE_TOTAL, DEVICE_TOKENS)).astype(jnp.int32),
        "padding_token_mask": with_ends((jax.random.randint(streams_of[13], (SEQUENCE_TOTAL, DEVICE_TOKENS), 0, 8) < 7).astype(jnp.int32), jax.random.fold_in(streams_of[13], 1), 0, 1),
        "routes": choose_distinct(streams_of[14], TOKENS, EXPERTS, TOP, 4096),
        "pair_order": jax.vmap(lambda own: jax.random.permutation(own, DEVICE_TOKENS * TOP))(jax.random.split(streams_of[15], SEQUENCE_TOTAL)).reshape((SEQUENCE_TOTAL, DEVICE_TOKENS * TOP)).astype(jnp.int32),
    }


@jax.custom_vjp
def low(v):
    return lax.optimization_barrier(v.astype(jnp.bfloat16)).astype(jnp.float32)

@jax.custom_vjp
def low_back(v):
    return v

def low_keep(v):
    return (low(v), None)

def low_pass(kept, grad):
    return (grad,)

def back_keep(v):
    return (v, None)

def back_low(kept, grad):
    return (low(grad),)
low.defvjp(low_keep, low_pass)
low_back.defvjp(back_keep, back_low)
epsilon = 1e-06
neg_fill = -1e+30
highest = lax.Precision.HIGHEST

def slot_table(route_rows, order_row, experts, capacity):
    pair_count = order_row.shape[0]
    flat_routes = route_rows.reshape(-1).astype(jnp.int32)
    order_idx = order_row.astype(jnp.int32)
    expert_at = jnp.take(flat_routes, order_idx).astype(jnp.int32)
    columns = jnp.arange(experts, dtype=jnp.int32)
    onehot = (expert_at[:, None] == columns[None, :]).astype(jnp.int32)
    running = jnp.cumsum(onehot, axis=0, dtype=jnp.int32).astype(jnp.int32)
    ranking = (jnp.take_along_axis(running, expert_at[:, None], axis=1)[:, 0] - 1).astype(jnp.int32)
    is_kept = ranking < capacity
    target = jnp.where(is_kept, expert_at * capacity + ranking, experts * capacity).astype(jnp.int32)
    slot_pair = jnp.full((experts * capacity,), pair_count, jnp.int32).at[target].set(order_idx, mode='drop')
    pair_slot = jnp.zeros((pair_count,), jnp.int32).at[order_idx].set(target)
    return (slot_pair.astype(jnp.int32), pair_slot.astype(jnp.int32))

def visible(segment_row, pad_row):
    position = jnp.arange(segment_row.shape[0], dtype=jnp.int32)
    same_doc = segment_row[:, None] == segment_row[None, :]
    causal = position[None, :] <= position[:, None]
    present = (pad_row[None, :] == 1) | (position[None, :] == position[:, None])
    return same_doc & causal & present

def segment_attend(parts):
    query_matrix, rows_of_key, rows_of_value, segment_row, pad_row = parts
    count_of_rows = query_matrix.shape[0]
    group_of_heads = QUERY_HEADS // KEY_VALUE_HEADS
    heads_of_query = query_matrix.reshape(count_of_rows, KEY_VALUE_HEADS, group_of_heads, HEAD_SIZE)
    heads_of_key = rows_of_key.reshape(count_of_rows, KEY_VALUE_HEADS, HEAD_SIZE)
    heads_of_value = rows_of_value.reshape(count_of_rows, KEY_VALUE_HEADS, HEAD_SIZE)
    scores = jnp.einsum('qkgd,skd->kgqs', heads_of_query, heads_of_key, precision=highest) * HEAD_SIZE ** (-0.5)
    scores = low_back(scores)
    scores = jnp.where(visible(segment_row, pad_row)[None, None], scores, neg_fill)
    weights = low(jax.nn.softmax(scores, axis=-1))
    attention_mixture = jnp.einsum('kgqs,skd->qkgd', weights, heads_of_value, precision=highest)
    return low(low_back(attention_mixture.reshape(count_of_rows, QUERY_HEADS * HEAD_SIZE)))

def expert_apply(parts):
    rows_in, gate_w, up_w, down_w = parts
    gate_pre = low_back(jnp.dot(rows_in, gate_w, precision=highest))
    up_pre = low_back(jnp.dot(rows_in, up_w, precision=highest))
    hidden = low(gate_pre * jax.nn.sigmoid(gate_pre) * up_pre)
    return low(low_back(jnp.dot(hidden, down_w, precision=highest)))

def forward(tokens, norm_attn, norm_moe, w_query, key_weight, value_weight, w_out, w_router, w_gate, w_up, w_down, document_index, padding_token_mask, routes, pair_order):
    inverse_one = lax.rsqrt(lax.optimization_barrier(jnp.mean(tokens * tokens, axis=1, keepdims=True)) + epsilon)
    normed_one = low(tokens * inverse_one * norm_attn)
    query_matrix = low(low_back(jnp.dot(normed_one, w_query, precision=highest)))
    rows_of_key = low(low_back(jnp.dot(normed_one, key_weight, precision=highest)))
    rows_of_value = low(low_back(jnp.dot(normed_one, value_weight, precision=highest)))
    attention_mixture = lax.map(jax.checkpoint(segment_attend), (query_matrix.reshape(SEQUENCE_TOTAL, DEVICE_TOKENS, QUERY_HEADS * HEAD_SIZE), rows_of_key.reshape(SEQUENCE_TOTAL, DEVICE_TOKENS, KEY_VALUE_HEADS * HEAD_SIZE), rows_of_value.reshape(SEQUENCE_TOTAL, DEVICE_TOKENS, KEY_VALUE_HEADS * HEAD_SIZE), document_index, padding_token_mask))
    attention_mixture = attention_mixture.reshape(TOKENS, QUERY_HEADS * HEAD_SIZE)
    hidden_one = tokens + low_back(jnp.dot(attention_mixture, w_out, precision=highest))
    inverse_two = lax.rsqrt(lax.optimization_barrier(jnp.mean(hidden_one * hidden_one, axis=1, keepdims=True)) + epsilon)
    normed_two = low(hidden_one * inverse_two * norm_moe)
    router = jax.nn.softmax(jnp.dot(normed_two, w_router, precision=highest), axis=-1)
    columns = jnp.arange(EXPERTS, dtype=jnp.int32)
    onehot = (routes[:, :, None] == columns[None, None, :]).astype(router.dtype)
    chosen = lax.optimization_barrier(jnp.sum(router[:, None, :] * onehot, axis=2))
    table = jax.vmap(partial(slot_table, experts=EXPERTS, capacity=CAP))
    slot_pair, pair_slot = table(routes.reshape(SEQUENCE_TOTAL, DEVICE_TOKENS, TOP), pair_order)
    normed_rows = normed_two.reshape(SEQUENCE_TOTAL, DEVICE_TOKENS, MODEL_WIDTH)
    normed_rows = jnp.concatenate([normed_rows, jnp.zeros((SEQUENCE_TOTAL, 1, MODEL_WIDTH), normed_rows.dtype)], axis=1)
    slot_token = (slot_pair // TOP).astype(jnp.int32)
    dispatched = low_back(jnp.take_along_axis(normed_rows, slot_token[:, :, None], axis=1))
    by_expert = dispatched.reshape(SEQUENCE_TOTAL, EXPERTS, CAP, MODEL_WIDTH).transpose(1, 0, 2, 3).reshape(EXPERTS, SEQUENCE_TOTAL * CAP, MODEL_WIDTH)
    produced = lax.map(jax.checkpoint(expert_apply), (by_expert, w_gate, w_up, w_down))
    produced = produced.reshape(EXPERTS, SEQUENCE_TOTAL, CAP, MODEL_WIDTH).transpose(1, 0, 2, 3).reshape(SEQUENCE_TOTAL, EXPERTS * CAP, MODEL_WIDTH)
    produced = jnp.concatenate([produced, jnp.zeros((SEQUENCE_TOTAL, 1, MODEL_WIDTH), produced.dtype)], axis=1)
    per_pair = jnp.take_along_axis(produced, pair_slot[:, :, None], axis=1).reshape(TOKENS, TOP, MODEL_WIDTH)
    routed = lax.optimization_barrier(jnp.sum(chosen[:, :, None] * per_pair, axis=1))
    return hidden_one + routed

def reference(tokens, cotangent, norm_attn, norm_moe, w_query, key_weight, value_weight, w_out, w_router, w_gate, w_up, w_down, document_index, padding_token_mask, routes, pair_order):
    floats = (tokens.astype(jnp.float32), norm_attn.astype(jnp.float32), norm_moe.astype(jnp.float32), w_query.astype(jnp.float32), key_weight.astype(jnp.float32), value_weight.astype(jnp.float32), w_out.astype(jnp.float32), w_router.astype(jnp.float32), w_gate.astype(jnp.float32), w_up.astype(jnp.float32), w_down.astype(jnp.float32))

    def closed(*arrays):
        return forward(*arrays, document_index, padding_token_mask, routes, pair_order)
    result, pullback = jax.vjp(closed, *floats)
    grads = pullback(cotangent.astype(jnp.float32))
    return (result.astype(jnp.bfloat16), grads[0], grads[1], grads[2], grads[3], grads[4], grads[5], grads[6], grads[7], grads[8], grads[9], grads[10])
```

```python
import functools
import jax
import jax.numpy as jnp
from jax import lax
from jax.experimental import pallas as pl
from jax.experimental.pallas import tpu as pltpu

bf16 = jnp.bfloat16
f32 = jnp.float32
NT_DIMS = (((1,), (1,)), ((), ()))
TN_DIMS = (((0,), (0,)), ((), ()))


def mm(a, b):
    return jnp.dot(a, b, preferred_element_type=f32)


def mm_nt(a, b):
    return lax.dot_general(a, b, NT_DIMS, preferred_element_type=f32)


def mm_tn(a, b):
    return lax.dot_general(a, b, TN_DIMS, preferred_element_type=f32)


def split_three(v):
    high = v.astype(bf16)
    rest = v - high.astype(f32)
    middle = rest.astype(bf16)
    low = (rest - middle.astype(f32)).astype(bf16)
    return high, middle, low


def expert_kernel(
    experts, chunks, tokens, features, ff, rows,
    hosted, slot_row, slot_col,
    n_same, n_other, c_same, c_other, gate0, up0, down0, gate1, up1, down1,
    po_same, po_other, pg_same, pg_other, x_out, gp_out, h_out, gg_out, gu_out,
    wg, wu, wd, nbuf, cbuf, po, pg, x, gp, gc, h, gg, gu, dmat, dtmat, gcol, vcol,
    w_sem, in_sem, act_sem, p_sem,
):
    wide = 256
    tiles = features // wide
    ff_tiles = ff // wide
    weight_copies = []
    for slot, (g_ref, u_ref, d_ref) in enumerate(((gate0, up0, down0), (gate1, up1, down1))):
        weight_copies.append((
            pltpu.make_async_copy(g_ref, wg.at[slot], w_sem.at[slot, 0]),
            pltpu.make_async_copy(u_ref, wu.at[slot], w_sem.at[slot, 1]),
            pltpu.make_async_copy(d_ref, wd.at[slot], w_sem.at[slot, 2]),
        ))

    def input_copies(chunk):
        return (
            pltpu.make_async_copy(n_same.at[chunk], nbuf.at[0], in_sem.at[0]),
            pltpu.make_async_copy(n_other.at[chunk], nbuf.at[1], in_sem.at[1]),
            pltpu.make_async_copy(c_same.at[chunk], cbuf.at[0], in_sem.at[2]),
            pltpu.make_async_copy(c_other.at[chunk], cbuf.at[1], in_sem.at[3]),
        )

    def act_copies(chunk, slot):
        at = pl.ds(pl.multiple_of(chunk * 2 * rows, 16), 2 * rows)
        return (
            pltpu.make_async_copy(x, x_out.at[slot, at], act_sem.at[0]),
            pltpu.make_async_copy(gp, gp_out.at[slot, at], act_sem.at[1]),
            pltpu.make_async_copy(h, h_out.at[slot, at], act_sem.at[2]),
            pltpu.make_async_copy(gg, gg_out.at[slot, at], act_sem.at[3]),
            pltpu.make_async_copy(gu, gu_out.at[slot, at], act_sem.at[4]),
        )

    def partial_copies(chunk):
        return (
            pltpu.make_async_copy(pg.at[0], pg_same.at[chunk], p_sem.at[0]),
            pltpu.make_async_copy(pg.at[1], pg_other.at[chunk], p_sem.at[1]),
            pltpu.make_async_copy(po.at[0], po_same.at[chunk], p_sem.at[2]),
            pltpu.make_async_copy(po.at[1], po_other.at[chunk], p_sem.at[3]),
        )

    def one_expert(chunk, slot):
        expert = hosted[slot]
        lane = lax.broadcasted_iota(jnp.int32, (rows, 128), 1)
        mine = lax.rem(lane, experts) == expert
        for q in range(2):
            at = slice(q * rows, (q + 1) * rows)
            row_slots = slot_row[chunk * 2 + slot, q:q + 1, :]
            onehot = lax.broadcasted_iota(jnp.int32, (rows, tokens), 0) == row_slots
            dmat[q] = jnp.where(onehot, 1.0, 0.0).astype(bf16)
            col_slots = slot_col[chunk * 2 + slot, :, q:q + 1]
            onehot_t = lax.broadcasted_iota(jnp.int32, (tokens, rows), 1) == col_slots
            dtmat[q] = jnp.where(onehot_t, 1.0, 0.0).astype(bf16)
            parts = mm(dmat[q], nbuf[q, :, features:features + 128])
            g = jnp.sum(jnp.where(mine & (lane < 3 * experts), parts, 0.0), axis=1, keepdims=True)
            gcol[at, :] = jnp.broadcast_to(g, (rows, 128))

            @pl.loop(0, tiles)
            def _(tile):
                cols = pl.ds(pl.multiple_of(tile * wide, wide), wide)
                x[at, cols] = mm(dmat[q], nbuf[q, :, cols]).astype(bf16)
                cot = mm(dmat[q], cbuf[q, :, cols])
                gc[at, cols] = cot.astype(bf16)
                gp[at, cols] = (cot * gcol[at, 0:1]).astype(bf16)

        @pl.loop(0, ff_tiles)
        def _(tile):
            cols = pl.ds(pl.multiple_of(tile * wide, wide), wide)
            gate = mm(x[...], wg[slot, :, cols])
            up = mm(x[...], wu[slot, :, cols])
            dh = mm_nt(gp[...], wd[slot, cols, :])
            sig = 1.0 / (1.0 + jnp.exp(-gate))
            act = gate * sig
            h[:, cols] = (act * up).astype(bf16)
            gg[:, cols] = (dh * up * (sig * (1.0 + gate * (1.0 - sig)))).astype(bf16)
            gu[:, cols] = (dh * act).astype(bf16)

        vcol[...] = jnp.zeros_like(vcol)

        @pl.loop(0, tiles)
        def _(tile):
            cols = pl.ds(pl.multiple_of(tile * wide, wide), wide)
            produced = mm(h[...], wd[slot, :, cols]).astype(bf16).astype(f32)
            along = produced * gc[:, cols].astype(f32)
            vcol[...] += along[:, :128] + along[:, 128:]
            scaled = (produced * gcol[:, 0:1]).astype(bf16)
            back = mm_nt(gg[...], wg[slot, cols, :]) + mm_nt(gu[...], wu[slot, cols, :])
            back = back.astype(bf16)
            for q in range(2):
                at = slice(q * rows, (q + 1) * rows)
                out_part = mm(dtmat[q], scaled[at])
                back_part = mm(dtmat[q], back[at])
                out_old = jnp.where(slot == 0, 0.0, po[q, :, cols].astype(f32))
                back_old = jnp.where(slot == 0, 0.0, pg[q, :, cols].astype(f32))
                po[q, :, cols] = (out_part + out_old).astype(bf16)
                pg[q, :, cols] = (back_part + back_old).astype(bf16)

        for q in range(2):
            at = slice(q * rows, (q + 1) * rows)
            high, middle, low = split_three(jnp.sum(vcol[at, :], axis=1, keepdims=True))
            payload = jnp.where(lane == expert, high.astype(f32), 0.0)
            payload = jnp.where(lane == expert + experts, middle.astype(f32), payload)
            payload = jnp.where(lane == expert + 2 * experts, low.astype(f32), payload)
            tail_part = mm(dtmat[q], payload.astype(bf16))
            tail = slice(features, features + 128)
            tail_old = jnp.where(slot == 0, 0.0, pg[q, :, tail].astype(f32))
            pg[q, :, tail] = (tail_part + tail_old).astype(bf16)

    for copies in weight_copies:
        for copy in copies:
            copy.start()
    for copy in input_copies(0):
        copy.start()

    @pl.loop(0, chunks)
    def _(chunk):
        for copy in input_copies(chunk):
            copy.wait()

        @pl.loop(0, 2)
        def _(slot):
            @pl.when((chunk == 0) & (slot == 0))
            def _():
                for copy in weight_copies[0]:
                    copy.wait()

            @pl.when((chunk == 0) & (slot == 1))
            def _():
                for copy in weight_copies[1]:
                    copy.wait()

            @pl.when(slot == 1)
            def _():
                for copy in act_copies(chunk, 0):
                    copy.wait()

            one_expert(chunk, slot)
            for copy in act_copies(chunk, slot):
                copy.start()

        for copy in partial_copies(chunk):
            copy.start()
        for copy in act_copies(chunk, 1):
            copy.wait()
        for copy in partial_copies(chunk):
            copy.wait()

        @pl.when(chunk + 1 < chunks)
        def _():
            for copy in input_copies(chunk + 1):
                copy.start()


def expert_call(hosted, slot_row, slot_col, n_same, n_other, c_same, c_other, own, partner, experts, rows):
    chunks, tokens, features = c_same.shape
    ff = own[0].shape[1]
    wide_n = n_same.shape[2]
    shape = jax.ShapeDtypeStruct
    anywhere = pl.BlockSpec(memory_space=pl.ANY)
    slots_total = chunks * 2 * rows
    act_f = shape((2, slots_total, features), bf16)
    act_h = shape((2, slots_total, ff), bf16)
    out_shape = (
        [shape((chunks, tokens, features), bf16)] * 2
        + [shape((chunks, tokens, wide_n), bf16)] * 2
        + [act_f, act_f, act_h, act_h, act_h]
    )
    many = 2 * rows
    flops = chunks * 2 * (14 * many * features * ff + 8 * many * tokens * features)
    return pl.pallas_call(
        functools.partial(expert_kernel, experts, chunks, tokens, features, ff, rows),
        out_shape=out_shape,
        in_specs=[
            pl.BlockSpec(memory_space=pltpu.SMEM),
            pl.BlockSpec(memory_space=pltpu.VMEM),
            pl.BlockSpec(memory_space=pltpu.VMEM),
        ] + [anywhere] * 10,
        out_specs=[anywhere] * 9,
        scratch_shapes=[
            pltpu.VMEM((2, features, ff), bf16),
            pltpu.VMEM((2, features, ff), bf16),
            pltpu.VMEM((2, ff, features), bf16),
            pltpu.VMEM((2, tokens, wide_n), bf16),
            pltpu.VMEM((2, tokens, features), bf16),
            pltpu.VMEM((2, tokens, features), bf16),
            pltpu.VMEM((2, tokens, wide_n), bf16),
            pltpu.VMEM((many, features), bf16),
            pltpu.VMEM((many, features), bf16),
            pltpu.VMEM((many, features), bf16),
            pltpu.VMEM((many, ff), bf16),
            pltpu.VMEM((many, ff), bf16),
            pltpu.VMEM((many, ff), bf16),
            pltpu.VMEM((2, rows, tokens), bf16),
            pltpu.VMEM((2, tokens, rows), bf16),
            pltpu.VMEM((many, 128), f32),
            pltpu.VMEM((many, 128), f32),
            pltpu.SemaphoreType.DMA((2, 3)),
            pltpu.SemaphoreType.DMA((4,)),
            pltpu.SemaphoreType.DMA((5,)),
            pltpu.SemaphoreType.DMA((4,)),
        ],
        compiler_params=pltpu.CompilerParams(vmem_limit_bytes=60 * 1024 * 1024),
        cost_estimate=pl.CostEstimate(flops=flops, bytes_accessed=40 << 20, transcendentals=chunks * 2 * many * ff),
        name="expert_rows",
    )(hosted, slot_row, slot_col, n_same, n_other, c_same, c_other, *own, *partner)


def weight_gradient_kernel(parts, *refs):
    ins, (gate_ref, up_ref, down_ref) = refs[:5 * parts], refs[5 * parts:]
    gate = up = down = None
    for p in range(parts):
        x, gg, gu, h, gp = ins[5 * p:5 * p + 5]
        g, u, d = mm_tn(x[0], gg[0]), mm_tn(x[0], gu[0]), mm_tn(h[0], gp[0])
        gate, up, down = (g, u, d) if gate is None else (gate + g, up + u, down + d)
    gate_ref[...] = gate.astype(bf16)
    up_ref[...] = up.astype(bf16)
    down_ref[...] = down.astype(bf16)


def weight_gradient_call(slot, saved):
    features, ff = saved[0][0].shape[2], saved[0][2].shape[2]
    steps = 6
    tall_f, tall_h = features // steps, ff // steps
    in_specs, args = [], []
    flops = 0
    for x, gp, h, gg, gu in saved:
        slots = x.shape[1]
        flops += 6 * slots * features * ff
        in_specs += [
            pl.BlockSpec((1, slots, tall_f), lambda i: (slot, 0, i)),
            pl.BlockSpec((1, slots, ff), lambda i: (slot, 0, 0)),
            pl.BlockSpec((1, slots, ff), lambda i: (slot, 0, 0)),
            pl.BlockSpec((1, slots, tall_h), lambda i: (slot, 0, i)),
            pl.BlockSpec((1, slots, features), lambda i: (slot, 0, 0)),
        ]
        args += [x, gg, gu, h, gp]
    return pl.pallas_call(
        functools.partial(weight_gradient_kernel, len(saved)),
        grid=(steps,),
        in_specs=in_specs,
        out_specs=[
            pl.BlockSpec((tall_f, ff), lambda i: (i, 0)),
            pl.BlockSpec((tall_f, ff), lambda i: (i, 0)),
            pl.BlockSpec((tall_h, features), lambda i: (i, 0)),
        ],
        out_shape=[
            jax.ShapeDtypeStruct((features, ff), bf16),
            jax.ShapeDtypeStruct((features, ff), bf16),
            jax.ShapeDtypeStruct((ff, features), bf16),
        ],
        compiler_params=pltpu.CompilerParams(vmem_limit_bytes=60 * 1024 * 1024),
        cost_estimate=pl.CostEstimate(flops=flops, bytes_accessed=24 << 20, transcendentals=0),
        name="expert_weight_gradients",
    )(*args)


from jax.sharding import PartitionSpec as P

QUERY_HEADS = 12
KEY_VALUE_HEADS = 2
HEAD_SIZE = 128


epsilon = 1e-06
neg_fill = -1e30
highest = lax.Precision.HIGHEST


def visible(segment_row, pad_row):
    position = jnp.arange(segment_row.shape[0], dtype=jnp.int32)
    same_doc = segment_row[:, None] == segment_row[None, :]
    causal = position[None, :] <= position[:, None]
    present = (pad_row[None, :] == 1) | (position[None, :] == position[:, None])
    return same_doc & causal & present


def score_block(heads_of_query, heads_of_key, segment_row, pad_row):
    scores = jnp.einsum(
        "qkgd,skd->kgqs", heads_of_query, heads_of_key, preferred_element_type=jnp.float32
    ) * HEAD_SIZE ** (-0.5)
    return jnp.where(visible(segment_row, pad_row)[None, None], scores, neg_fill)


def norm_back(grad_normed, source, inverse, gain):
    scaled = grad_normed * gain
    grad_source = inverse * scaled - source * inverse**3 * jnp.mean(
        scaled * source, axis=1, keepdims=True
    )
    grad_gain = jnp.sum(grad_normed * source * inverse, axis=0)
    return (grad_source, grad_gain)


def pair_slots(routes, order_row, experts, capacity):
    pair_count = order_row.shape[0]
    place = (
        jnp.zeros((pair_count,), jnp.int32)
        .at[order_row]
        .set(jnp.arange(pair_count, dtype=jnp.int32), unique_indices=True, mode="promise_in_bounds")
        .reshape(routes.shape)
    )
    columns = jnp.arange(experts, dtype=jnp.int32)
    hit = routes[None, :, :] == columns[:, None, None]
    key = jnp.min(jnp.where(hit, place[None], pair_count), axis=2)
    rank = jnp.sum((key[:, None, :] < key[:, :, None]).astype(jnp.int32), axis=2)
    return jnp.where((key < pair_count) & (rank < capacity), rank, -1)


def body(
    tokens,
    cotangent,
    norm_attn,
    norm_moe,
    w_query,
    key_weight,
    value_weight,
    w_out,
    w_router,
    w_gate,
    w_up,
    w_down,
    document_index,
    padding_token_mask,
    routes,
    pair_order,
):
    token_rows, features = tokens.shape
    top_count = routes.shape[1]
    experts = lax.axis_size("expert")
    data = lax.axis_size("dp")
    chips = experts // 2
    half = chips // 2
    ff = w_gate.shape[2]
    capacity = 9 * token_rows * top_count // (8 * experts)
    slot_rows = (capacity + 15) // 16 * 16
    group_of_heads = QUERY_HEADS // KEY_VALUE_HEADS
    score_scale = HEAD_SIZE ** (-0.5)
    me = lax.axis_index("expert")
    my_dp = lax.axis_index("dp")
    core = lax.rem(me, 2)
    core_swap = [(j, j ^ 1) for j in range(experts)]
    partner_swap = [(j, (j + experts // 2) % experts) for j in range(experts)]

    def shifted(j, k):
        chip = j // 2
        return ((chip // half) * half + (chip % half + k) % half) * 2 + j % 2

    def swap(v):
        return lax.ppermute(v, "expert", core_swap)

    def shift(v, k):
        return lax.ppermute(v, "expert", [(j, shifted(j, k)) for j in range(experts)])

    def across(v):
        return lax.ppermute(v, "expert", partner_swap)

    def gathered(shard):
        width = shard.shape[1] // 2
        mine = lax.dynamic_slice_in_dim(shard, core * width, width, axis=1)
        mine = lax.all_gather(mine, "dp", axis=0, tiled=True)
        other = swap(mine)
        first = jnp.where(core == 0, mine, other)
        second = jnp.where(core == 0, other, mine)
        return jnp.concatenate([first, second], axis=1)

    qkv_all = gathered(jnp.concatenate([w_query, key_weight, value_weight], axis=1))
    out_all = gathered(w_out)

    def dp_part(w):
        rows = w.shape[0] // data
        return lax.dynamic_slice_in_dim(w, my_dp * rows, rows, axis=0)

    own = (w_gate[0], w_up[0], w_down[0])
    partner = tuple(
        lax.all_gather(across(dp_part(w)), "dp", axis=0, tiled=True) for w in own
    )

    slots = pair_slots(routes, pair_order[0], experts, capacity)
    all_slots = lax.all_gather(slots, "expert", axis=0, tiled=False)
    hosted = jnp.stack([me, lax.rem(me + experts // 2, experts)]).astype(jnp.int32)

    def tables(sources):
        picked = jnp.stack([
            jnp.stack([
                jnp.stack([all_slots[source, hosted[0]], all_slots[source ^ 1, hosted[0]]]),
                jnp.stack([all_slots[source, hosted[1]], all_slots[source ^ 1, hosted[1]]]),
            ])
            for source in sources
        ])
        picked = picked.reshape(len(sources) * 2, 2, token_rows)
        return picked, jnp.swapaxes(picked, 1, 2)

    def source_of(k):
        chip = me // 2
        return ((chip // half) * half + lax.rem(chip % half + half - k, half)) * 2 + core

    cot_same = cotangent
    cot_other = swap(cotangent)
    cot_far_same = [shift(cotangent, k) for k in range(1, half)]
    cot_far_other = [swap(v) for v in cot_far_same]

    source = tokens.astype(jnp.float32)
    inverse_one = lax.rsqrt(jnp.mean(source * source, axis=1, keepdims=True) + epsilon)
    normed_one = (source * inverse_one * norm_attn).astype(jnp.bfloat16)
    qkv = jnp.dot(normed_one, qkv_all, preferred_element_type=jnp.float32).astype(jnp.bfloat16)
    query_width = QUERY_HEADS * HEAD_SIZE
    kv_width = KEY_VALUE_HEADS * HEAD_SIZE
    heads_of_query = qkv[:, :query_width].reshape(
        token_rows, KEY_VALUE_HEADS, group_of_heads, HEAD_SIZE
    )
    heads_of_key = qkv[:, query_width:query_width + kv_width].reshape(
        token_rows, KEY_VALUE_HEADS, HEAD_SIZE
    )
    heads_of_value = qkv[:, query_width + kv_width:].reshape(token_rows, KEY_VALUE_HEADS, HEAD_SIZE)
    segment_row = document_index[0]
    pad_row = padding_token_mask[0]
    scores = score_block(heads_of_query, heads_of_key, segment_row, pad_row)
    top_score = jnp.max(scores, axis=-1, keepdims=True)
    log_total = top_score + jnp.log(jnp.sum(jnp.exp(scores - top_score), axis=-1, keepdims=True))
    weights = jnp.exp(scores - log_total).astype(jnp.bfloat16)
    attention_mixture = jnp.einsum(
        "kgqs,skd->qkgd", weights, heads_of_value, preferred_element_type=jnp.float32
    )
    attention_mixture = attention_mixture.reshape(token_rows, query_width).astype(jnp.bfloat16)
    hidden_one = source + jnp.dot(attention_mixture, out_all, preferred_element_type=jnp.float32)
    inverse_two = lax.rsqrt(jnp.mean(hidden_one * hidden_one, axis=1, keepdims=True) + epsilon)
    normed_two = (hidden_one * inverse_two * norm_moe).astype(jnp.bfloat16)
    router = jax.nn.softmax(
        jnp.dot(normed_two, w_router, preferred_element_type=jnp.float32), axis=-1
    )
    payload = jnp.concatenate(
        [normed_two, *split_three(router), jnp.zeros((token_rows, 128 - 3 * experts), jnp.bfloat16)],
        axis=1,
    )

    payload_far_same = [shift(payload, k) for k in range(1, half)]
    payload_other = swap(payload)
    near_row, near_col = tables([me])
    near = expert_call(
        hosted, near_row, near_col, payload[None], payload_other[None], cot_same[None],
        cot_other[None], own, partner, experts, slot_rows,
    )
    payload_far_other = [swap(v) for v in payload_far_same]
    far_row, far_col = tables([source_of(k) for k in range(1, half)])
    far = expert_call(
        hosted, far_row, far_col, jnp.stack(payload_far_same), jnp.stack(payload_far_other),
        jnp.stack(cot_far_same), jnp.stack(cot_far_other), own, partner, experts, slot_rows,
    )

    def returned(near_same, near_other, far_same, far_other):
        total = near_same[0].astype(jnp.float32) + swap(near_other[0]).astype(jnp.float32)
        for k in range(1, half):
            both = far_same[k - 1].astype(jnp.float32) + swap(far_other[k - 1]).astype(jnp.float32)
            total = total + shift(both.astype(jnp.bfloat16), half - k).astype(jnp.float32)
        return total

    back = returned(near[2], near[3], far[2], far[3])
    routed = returned(near[0], near[1], far[0], far[1])
    block_out = (hidden_one + routed).astype(jnp.bfloat16)
    from_experts = back[:, :features]
    grad_select = (
        back[:, features:features + experts]
        + back[:, features + experts:features + 2 * experts]
        + back[:, features + 2 * experts:features + 3 * experts]
    )

    saved = [tuple(near[4:]), tuple(far[4:])]
    local_partner = weight_gradient_call(1, saved)
    local_own = weight_gradient_call(0, saved)

    def scattered(v):
        return lax.psum_scatter(v, "dp", scatter_dimension=0, tiled=True)

    expert_gradients = []
    for from_partner, from_own in zip(local_partner, local_own):
        arrived = across(scattered(from_partner))
        total = scattered(from_own).astype(jnp.float32) + arrived.astype(jnp.float32)
        whole = lax.all_gather(total.astype(jnp.bfloat16), "dp", axis=0, tiled=True)
        expert_gradients.append(whole.astype(jnp.float32)[None])
    grad_gate, grad_up, grad_down = expert_gradients

    cot_full = cotangent.astype(jnp.float32)
    grad_logits = router * (grad_select - jnp.sum(router * grad_select, axis=1, keepdims=True))
    grad_normed_two = (
        jnp.dot(grad_logits, w_router.astype(jnp.float32).T, precision=highest) + from_experts
    )
    local_router = jnp.dot(normed_two.astype(jnp.float32).T, grad_logits, precision=highest)
    through_two, local_norm_moe = norm_back(grad_normed_two, hidden_one, inverse_two, norm_moe)
    grad_hidden_one = cot_full + through_two
    grad_branch = grad_hidden_one.astype(jnp.bfloat16)

    def reduced(v):
        width = v.shape[1] // 2
        keep = lax.dynamic_slice_in_dim(v, core * width, width, axis=1)
        give = lax.dynamic_slice_in_dim(v, (1 - core) * width, width, axis=1)
        part = keep.astype(jnp.float32) + swap(give.astype(jnp.bfloat16)).astype(jnp.float32)
        part = scattered(part.astype(jnp.bfloat16))
        step = 1
        while step < chips:
            pairs = [(j, ((j // 2) ^ step) * 2 + j % 2) for j in range(experts)]
            arrived = lax.ppermute(part, "expert", pairs)
            part = (part.astype(jnp.float32) + arrived.astype(jnp.float32)).astype(jnp.bfloat16)
            step *= 2
        other = swap(part)
        first = jnp.where(core == 0, part, other)
        second = jnp.where(core == 0, other, part)
        return jnp.concatenate([first, second], axis=1).astype(jnp.float32)

    local_out = jnp.dot(attention_mixture.T, grad_branch, preferred_element_type=jnp.float32)
    grad_out = reduced(local_out)
    mixture_gradient = jnp.dot(grad_branch, out_all.T, preferred_element_type=jnp.float32).astype(
        jnp.bfloat16
    )
    heads_gradient = mixture_gradient.reshape(
        token_rows, KEY_VALUE_HEADS, group_of_heads, HEAD_SIZE
    )
    scores = score_block(heads_of_query, heads_of_key, segment_row, pad_row)
    probs = jnp.exp(scores - log_total)
    grad_weights = jnp.einsum(
        "qkgd,skd->kgqs", heads_gradient, heads_of_value, preferred_element_type=jnp.float32
    )
    grad_scores = (
        probs * (grad_weights - jnp.sum(probs * grad_weights, axis=-1, keepdims=True))
    ).astype(jnp.bfloat16)
    grad_queries = (
        jnp.einsum("kgqs,skd->qkgd", grad_scores, heads_of_key, preferred_element_type=jnp.float32)
        * score_scale
    )
    grad_queries = grad_queries.reshape(token_rows, query_width).astype(jnp.bfloat16)
    key_rows_gradient = (
        jnp.einsum(
            "kgqs,qkgd->skd", grad_scores, heads_of_query, preferred_element_type=jnp.float32
        )
        * score_scale
    )
    key_rows_gradient = key_rows_gradient.reshape(token_rows, kv_width).astype(jnp.bfloat16)
    value_rows_gradient = jnp.einsum(
        "kgqs,qkgd->skd", weights, heads_gradient, preferred_element_type=jnp.float32
    )
    value_rows_gradient = value_rows_gradient.reshape(token_rows, kv_width).astype(jnp.bfloat16)
    grad_qkv = jnp.concatenate([grad_queries, key_rows_gradient, value_rows_gradient], axis=1)
    local_qkv = jnp.dot(normed_one.T, grad_qkv, preferred_element_type=jnp.float32)
    summed_qkv = reduced(local_qkv)
    grad_query = summed_qkv[:, :query_width]
    grad_key = summed_qkv[:, query_width:query_width + kv_width]
    grad_value = summed_qkv[:, query_width + kv_width:]
    grad_normed_one = jnp.dot(grad_qkv, qkv_all.T, preferred_element_type=jnp.float32)
    through_one, local_norm_attn = norm_back(grad_normed_one, source, inverse_one, norm_attn)
    grad_tokens = grad_hidden_one + through_one
    grad_router, grad_norm_attn, grad_norm_moe = lax.psum(
        (local_router, local_norm_attn, local_norm_moe), ("dp", "expert")
    )
    return (
        block_out,
        grad_tokens,
        grad_norm_attn,
        grad_norm_moe,
        grad_query,
        grad_key,
        grad_value,
        grad_out,
        grad_router,
        grad_gate,
        grad_up,
        grad_down,
    )


def solution(mesh):
    placed = (
        P(("dp", "expert"), None),
        P(("dp", "expert"), None),
        P(),
        P(),
        P("dp", None),
        P("dp", None),
        P("dp", None),
        P("dp", None),
        P(),
        P("expert", None, None),
        P("expert", None, None),
        P("expert", None, None),
        P(("dp", "expert"), None),
        P(("dp", "expert"), None),
        P(("dp", "expert"), None),
        P(("dp", "expert"), None),
    )
    return jax.shard_map(
        body,
        mesh=mesh,
        in_specs=placed,
        out_specs=(
            P(("dp", "expert"), None),
            P(("dp", "expert"), None),
            P(),
            P(),
            P("dp", None),
            P("dp", None),
            P("dp", None),
            P("dp", None),
            P(),
            P("expert", None, None),
            P("expert", None, None),
            P("expert", None, None),
        ),
        check_vma=False,
    )
```

```python
import functools

import jax
import jax.numpy as jnp
from jax import lax
from jax.experimental import pallas as pl
from jax.experimental.pallas import tpu as pltpu
from jax.sharding import PartitionSpec as P

bf16 = jnp.bfloat16
f32 = jnp.float32
MIB = 1024 * 1024
LONG = pl.CostEstimate(flops=16 << 30, bytes_accessed=30 * MIB, transcendentals=0)
COST = pl.CostEstimate(flops=1000, bytes_accessed=1000, transcendentals=0)
NT_DIMS = (((1,), (1,)), ((), ()))
TN_DIMS = (((0,), (0,)), ((), ()))


def mm(a, b):
    return jnp.dot(a, b, preferred_element_type=f32)


def mm_nt(a, b):
    return lax.dot_general(a, b, NT_DIMS, preferred_element_type=f32)


def mm_tn(a, b):
    return lax.dot_general(a, b, TN_DIMS, preferred_element_type=f32)


def split_three(v):
    high = v.astype(bf16)
    rest = v - high.astype(f32)
    middle = rest.astype(bf16)
    low = (rest - middle.astype(f32)).astype(bf16)
    return high, middle, low


def lanes(start, size):
    return pl.ds(pl.multiple_of(start, 128), size)


def specs(kinds):
    table = {"s": pltpu.SMEM, "v": pltpu.VMEM, "a": pl.ANY}
    return [pl.BlockSpec(memory_space=table[kind]) for kind in kinds]


def params():
    return pltpu.CompilerParams(vmem_limit_bytes=60 * MIB)


def expert_kernel(experts, slots, base, data, pieces, chunks, n_weights, n_prev, n_saved, rows, *refs):
    count = len(slots)
    hosted, sources, refs = refs[0], refs[1:1 + 4 * chunks], refs[1 + 4 * chunks:]
    sources = [sources[4 * i:4 * i + 4] for i in range(chunks)]
    weight_refs, refs = refs[:n_weights], refs[n_weights:]
    prev, refs = refs[:n_prev], refs[n_prev + n_saved:]
    po_same, po_other, pg_same, pg_other, x_out, gp_out, h_out, gg_out, gu_out = refs[:9]
    (wg, wu, wd, nbuf, cbuf, x, gp, gc, sc, h, gg, gu, dmat, dtmat, gcol, vcol, tail_t,
     w_sem, in_sem, act_sem, p_sem) = refs[9:]
    tokens, features = sources[0][2].shape
    extra = sources[0][0].shape[1] - features
    ff = wg.shape[2]
    wide = features // 2
    tail = slice(features, features + extra)

    weight_copies = []
    taken = 0
    for place, slot in enumerate(slots):
        if slot == 0:
            pairs = list(zip(weight_refs[taken:taken + 3], (wg.at[place], wu.at[place], wd.at[place])))
            taken += 3
        else:
            tall_f, tall_h = features // data, ff // data
            pairs = []
            for index, begin, size, whose, first in pieces:
                ref = weight_refs[taken + index]
                source = jnp.bitwise_xor(hosted[2], whose[1]) if whose[0] else whose[1]
                wide_rows = max(0, min(size, tall_f - first))
                if wide_rows:
                    at = pl.ds(pl.multiple_of(source * tall_f + first, 16), wide_rows)
                    pairs += [
                        (ref.at[pl.ds(begin, wide_rows), pl.ds(0, ff)], wg.at[place, at]),
                        (ref.at[pl.ds(begin, wide_rows), pl.ds(ff, ff)], wu.at[place, at]),
                    ]
                if wide_rows < size:
                    at = pl.ds(pl.multiple_of(source * tall_h + first + wide_rows - tall_f, 16), size - wide_rows)
                    pairs.append((ref.at[pl.ds(begin + wide_rows, size - wide_rows)], wd.at[place, at]))
            taken += 1 + max(piece[0] for piece in pieces)
        weight_copies.append([
            pltpu.make_async_copy(source, target, w_sem.at[place, i])
            for i, (source, target) in enumerate(pairs)
        ])

    def input_copies(index):
        targets = (nbuf.at[0], nbuf.at[1], cbuf.at[0], cbuf.at[1])
        return [
            pltpu.make_async_copy(source, target, in_sem.at[i])
            for i, (source, target) in enumerate(zip(sources[index], targets))
        ]

    def act_copies(chunk, place):
        at = pl.ds(pl.multiple_of(base + chunk * 2 * rows, 16), 2 * rows)
        return [
            pltpu.make_async_copy(source.at[place], target.at[place, at], act_sem.at[place, i])
            for i, (source, target) in enumerate(
                ((x, x_out), (gp, gp_out), (h, h_out), (gg, gg_out), (gu, gu_out)))
        ]

    def partial_copies(chunk):
        return (
            pltpu.make_async_copy(nbuf.at[0], pg_same.at[chunk], p_sem.at[0]),
            pltpu.make_async_copy(nbuf.at[1], pg_other.at[chunk], p_sem.at[1]),
            pltpu.make_async_copy(cbuf.at[0], po_same.at[chunk], p_sem.at[2]),
            pltpu.make_async_copy(cbuf.at[1], po_other.at[chunk], p_sem.at[3]),
        )

    def dispatch(q):
        columns = nbuf[q, :, tail].astype(f32)
        tail_t[...] = columns.T
        token_lane = lax.broadcasted_iota(jnp.int32, (tokens, extra), 1)
        wanted = lax.broadcasted_iota(jnp.int32, (tokens, count * rows), 1)
        slot_cols = []
        for place in range(count):
            expert = hosted[slots[place]]
            row = (tail_t[pl.ds(3 * experts + expert, 1), :] * 128.0
                   + tail_t[pl.ds(4 * experts + expert, 1), :] - 1.0).astype(jnp.int32)
            hit = lax.broadcasted_iota(jnp.int32, (rows, tokens), 0) == row
            dmat[q, place * rows:(place + 1) * rows, :] = jnp.where(hit, 1.0, 0.0).astype(bf16)
            factor = jnp.where(token_lane == 3 * experts + expert, 128.0, 0.0)
            factor = jnp.where(token_lane == 4 * experts + expert, 1.0, factor)
            slot_cols.append(jnp.sum(columns * factor, axis=1, keepdims=True).astype(jnp.int32) - 1)
        target = slot_cols[0]
        if count == 2:
            second = wanted >= rows
            target = jnp.where(second, slot_cols[1], slot_cols[0])
            wanted = jnp.where(second, wanted - rows, wanted)
        dtmat[q] = jnp.where(wanted == target, 1.0, 0.0).astype(bf16)
        parts = mm(dmat[q], nbuf[q, :, tail])
        lane = lax.broadcasted_iota(jnp.int32, (rows, extra), 1)
        for place in range(count):
            expert = hosted[slots[place]]
            mine = (lane == expert) | (lane == expert + experts) | (lane == expert + 2 * experts)
            g = jnp.sum(jnp.where(mine, parts[place * rows:(place + 1) * rows], 0.0), axis=1, keepdims=True)
            gcol[place, q * rows:(q + 1) * rows, :] = jnp.broadcast_to(g, (rows, 128))

        @pl.loop(0, 2)
        def _(tile):
            cols = lanes(tile * wide, wide)
            found = mm(dmat[q], nbuf[q, :, cols]).astype(bf16)
            cot = mm(dmat[q], cbuf[q, :, cols])
            gc[q, :, cols] = cot.astype(bf16)
            for place in range(count):
                at = slice(q * rows, (q + 1) * rows)
                own = slice(place * rows, (place + 1) * rows)
                x[place, at, cols] = found[own]
                gp[place, at, cols] = (cot[own] * gcol[place, at, 0:1]).astype(bf16)

    def forward_backward(place):
        for q in range(2):
            at = slice(q * rows, (q + 1) * rows)
            gate = mm(x[place, at, :], wg[place])
            up = mm(x[place, at, :], wu[place])
            dh = mm_nt(gp[place, at, :], wd[place])
            sig = 1.0 / (1.0 + jnp.exp(-gate))
            act = gate * sig
            h[place, at, :] = (act * up).astype(bf16)
            gg[place, at, :] = (dh * up * (sig * (1.0 + gate * (1.0 - sig)))).astype(bf16)
            gu[place, at, :] = (dh * act).astype(bf16)

    def produce(place):
        vcol[place] = jnp.zeros(vcol.shape[1:], f32)

        @pl.loop(0, 2)
        def _(tile):
            cols = lanes(tile * wide, wide)
            for q in range(2):
                at = slice(q * rows, (q + 1) * rows)
                own = pl.ds(pl.multiple_of(place * rows, 16), rows)
                produced = mm(h[place, at, :], wd[place, :, cols]).astype(bf16).astype(f32)
                along = produced * gc[q, own, cols].astype(f32)
                folded = along[:, :128]
                for part in range(1, wide // 128):
                    folded = folded + along[:, part * 128:(part + 1) * 128]
                vcol[place, at, :] += folded
                sc[q, own, cols] = (produced * gcol[place, at, 0:1]).astype(bf16)
                back = mm_nt(gg[place, at, :], wg[place, cols, :]) + mm_nt(gu[place, at, :], wu[place, cols, :])
                gc[q, own, cols] = back.astype(bf16)

    def combine(q):
        at = slice(q * rows, (q + 1) * rows)
        lane = lax.broadcasted_iota(jnp.int32, (rows, extra), 1)
        payload = []
        for place in range(count):
            expert = hosted[slots[place]]
            high, middle, low = split_three(jnp.sum(vcol[place, at, :], axis=1, keepdims=True))
            part = jnp.where(lane == expert, high.astype(f32), 0.0)
            part = jnp.where(lane == expert + experts, middle.astype(f32), part)
            part = jnp.where(lane == expert + 2 * experts, low.astype(f32), part)
            payload.append(part.astype(bf16))
        payload = jnp.concatenate(payload, axis=0) if count > 1 else payload[0]
        tail_sum = mm(dtmat[q], payload)
        if n_prev:
            tail_sum = tail_sum + nbuf[q, :, tail].astype(f32)
        nbuf[q, :, tail] = tail_sum.astype(bf16)

        @pl.loop(0, 2)
        def _(tile):
            cols = lanes(tile * wide, wide)
            back = mm(dtmat[q], gc[q, :, cols])
            out = mm(dtmat[q], sc[q, :, cols])
            if n_prev:
                back = back + nbuf[q, :, cols].astype(f32)
                out = out + cbuf[q, :, cols].astype(f32)
            nbuf[q, :, cols] = back.astype(bf16)
            cbuf[q, :, cols] = out.astype(bf16)

    def prev_copies(chunk):
        po0, po1, pg0, pg1 = prev
        return (
            pltpu.make_async_copy(pg0.at[chunk], nbuf.at[0], in_sem.at[0]),
            pltpu.make_async_copy(pg1.at[chunk], nbuf.at[1], in_sem.at[1]),
            pltpu.make_async_copy(po0.at[chunk], cbuf.at[0], in_sem.at[2]),
            pltpu.make_async_copy(po1.at[chunk], cbuf.at[1], in_sem.at[3]),
        )

    for copy in input_copies(0):
        copy.start()
    for copies in weight_copies:
        for copy in copies:
            copy.start()

    @pl.loop(0, chunks)
    def _(chunk):
        for copy in input_copies(0):
            copy.wait()
        for q in range(2):
            dispatch(q)
        if n_prev:
            for copy in prev_copies(chunk):
                copy.start()
        for place in range(count):
            @pl.when(chunk == 0)
            def _():
                for copy in weight_copies[place]:
                    copy.wait()

            forward_backward(place)
            for copy in act_copies(chunk, place):
                copy.start()
            produce(place)
        if n_prev:
            for copy in prev_copies(chunk):
                copy.wait()
        for q in range(2):
            combine(q)
        for copy in partial_copies(chunk):
            copy.start()
        for place in range(count):
            for copy in act_copies(chunk, place):
                copy.wait()
        for copy in partial_copies(chunk):
            copy.wait()

        for index in range(1, chunks):
            @pl.when(chunk + 1 == index)
            def _():
                for copy in input_copies(index):
                    copy.start()


def expert_call(hosted, slots, sources, weights, prev, saved, base, total, experts, rows, data, pieces, cost):
    chunks = len(sources)
    tokens, features = sources[0][2].shape
    ff = weights[0].shape[1] if slots[0] == 0 else weights[0].shape[1] // 2
    wide_n = sources[0][0].shape[1]
    extra = wide_n - features
    count = len(slots)
    shape = jax.ShapeDtypeStruct
    act_f = shape((count, total, features), bf16)
    act_h = shape((count, total, ff), bf16)
    out_shape = (
        [shape((chunks, tokens, features), bf16)] * 2
        + [shape((chunks, tokens, wide_n), bf16)] * 2
        + [act_f, act_f, act_h, act_h, act_h]
    )
    many = 2 * rows
    first_prev = 1 + 4 * chunks + len(weights)
    first_saved = first_prev + len(prev)
    return pl.pallas_call(
        functools.partial(
            expert_kernel, experts, slots, base, data, pieces, chunks, len(weights), len(prev), len(saved), rows),
        out_shape=out_shape,
        in_specs=specs("s" + "a" * (4 * chunks + len(weights) + len(prev) + len(saved))),
        out_specs=specs("a" * 9),
        input_output_aliases={
            **{first_prev + i: i for i in range(len(prev))},
            **{first_saved + i: 4 + i for i in range(len(saved))},
        },
        scratch_shapes=[
            pltpu.VMEM((count, features, ff), bf16),
            pltpu.VMEM((count, features, ff), bf16),
            pltpu.VMEM((count, ff, features), bf16),
            pltpu.VMEM((2, tokens, wide_n), bf16),
            pltpu.VMEM((2, tokens, features), bf16),
            pltpu.VMEM((count, many, features), bf16),
            pltpu.VMEM((count, many, features), bf16),
            pltpu.VMEM((2, count * rows, features), bf16),
            pltpu.VMEM((2, count * rows, features), bf16),
            pltpu.VMEM((count, many, ff), bf16),
            pltpu.VMEM((count, many, ff), bf16),
            pltpu.VMEM((count, many, ff), bf16),
            pltpu.VMEM((2, count * rows, tokens), bf16),
            pltpu.VMEM((2, tokens, count * rows), bf16),
            pltpu.VMEM((count, many, 128), f32),
            pltpu.VMEM((count, many, 128), f32),
            pltpu.VMEM((extra, tokens), f32),
            pltpu.SemaphoreType.DMA((count, 3 * max(1, len(pieces)))),
            pltpu.SemaphoreType.DMA((4,)),
            pltpu.SemaphoreType.DMA((count, 5)),
            pltpu.SemaphoreType.DMA((4,)),
        ],
        compiler_params=params(),
        cost_estimate=cost,
        name="expert_rows",
    )(hosted, *[v for group in sources for v in group], *weights, *prev, *saved)


def weight_gradient_kernel(data, x_in, gg_in, gu_in, h_in, gp_in, out, x, gg, gu, h, gp, wide, down, sem, out_sem):
    features, ff = x.shape[1], h.shape[1]
    loads = [
        pltpu.make_async_copy(source.at[0], target, sem.at[i])
        for i, (source, target) in enumerate(((gg_in, gg), (x_in, x), (gu_in, gu), (h_in, h), (gp_in, gp)))
    ]
    for copy in loads:
        copy.start()
    tall_f, tall_h = features // data, ff // data
    step = tall_f + tall_h
    stores = [
        pltpu.make_async_copy(wide.at[pl.ds(d * tall_f, tall_f)], out.at[pl.ds(d * step, tall_f)], out_sem.at[2 * d])
        for d in range(data)
    ] + [
        pltpu.make_async_copy(down.at[pl.ds(d * tall_h, tall_h)], out.at[pl.ds(d * step + tall_f, tall_h)],
                              out_sem.at[2 * d + 1])
        for d in range(data)
    ]
    for copy in loads[:3]:
        copy.wait()
    tall = 256

    @pl.loop(0, features // tall)
    def _(tile):
        cols = lanes(tile * tall, tall)
        at = pl.ds(pl.multiple_of(tile * tall, tall), tall)
        wide[at, :ff] = mm_tn(x[:, cols], gg[...]).astype(bf16)
        wide[at, ff:] = mm_tn(x[:, cols], gu[...]).astype(bf16)

    for copy in stores[:data]:
        copy.start()
    for copy in loads[3:]:
        copy.wait()

    @pl.loop(0, ff // tall)
    def _(tile):
        cols = lanes(tile * tall, tall)
        at = pl.ds(pl.multiple_of(tile * tall, tall), tall)
        down[at, :] = mm_tn(h[:, cols], gp[...]).astype(bf16)

    for copy in stores[data:]:
        copy.start()
    for copy in stores:
        copy.wait()


def weight_gradient_call(saved, data):
    x, gp, h, gg, gu = saved
    slots, features, ff = x.shape[1], x.shape[2], h.shape[2]
    return pl.pallas_call(
        functools.partial(weight_gradient_kernel, data),
        out_shape=jax.ShapeDtypeStruct((features + ff, 2 * ff), bf16),
        in_specs=specs("aaaaa"),
        out_specs=pl.BlockSpec(memory_space=pl.ANY),
        scratch_shapes=[
            pltpu.VMEM((slots, features), bf16),
            pltpu.VMEM((slots, ff), bf16),
            pltpu.VMEM((slots, ff), bf16),
            pltpu.VMEM((slots, ff), bf16),
            pltpu.VMEM((slots, features), bf16),
            pltpu.VMEM((features, 2 * ff), bf16),
            pltpu.VMEM((ff, features), bf16),
            pltpu.SemaphoreType.DMA((5,)),
            pltpu.SemaphoreType.DMA((2 * data,)),
        ],
        compiler_params=params(),
        cost_estimate=COST,
        name="expert_weight_gradients",
    )(x, gg, gu, h, gp)


epsilon = 1e-06
neg_fill = -1e30
QUERY_HEADS = 12
KEY_VALUE_HEADS = 2
HEAD_SIZE = 128
GROUP = QUERY_HEADS // KEY_VALUE_HEADS
SCORE_SCALE = HEAD_SIZE ** (-0.5)


def piece_copies(place, own, pieces, begin, weight, sem):
    rows, half = own[0].shape[0], weight.shape[1] // 2
    mine, core = place[0], place[1]
    copies = []
    column = 0
    for part in own:
        at = weight.at[pl.ds(pl.multiple_of(mine * rows, 16), rows), pl.ds(column, part.shape[1])]
        copies.append(pltpu.make_async_copy(part, at, sem.at[len(copies)]))
        column += part.shape[1]
    for (k, skip), pair in zip(((1, 0), (2, 0), (3, 0), (3, rows // 2)), pieces):
        first = pl.multiple_of(jnp.bitwise_xor(mine, k) * rows + skip, 16)
        for part, which in zip(pair, (core, 1 - core)):
            at = weight.at[pl.ds(first, part.shape[0]), lanes(which * half, half)]
            copies.append(pltpu.make_async_copy(part.at[:, pl.ds(begin, half)], at, sem.at[len(copies)]))
    return copies


def attention_mask(segment_row, segment_col, pad_row, first, size, span):
    row = first + lax.broadcasted_iota(jnp.int32, (size, span), 0)
    col = lax.broadcasted_iota(jnp.int32, (size, span), 1)
    same = segment_col[first:first + size, :] == segment_row[:, :span]
    return same & (((pad_row[:, :span] == 1) & (col < row)) | (col == row))


def stacked(ref, rows, c):
    return jnp.concatenate(
        [ref[rows, lanes((c * GROUP + g) * HEAD_SIZE, HEAD_SIZE)] for g in range(GROUP)], axis=0
    )


def attend_kernel(
    n_own, n_pairs, tokens_total, block,
    place, tokens, gain, segment_row, segment_col, pad_row, *refs,
):
    own = refs[:n_own]
    flat = refs[n_own:n_own + 2 * n_pairs]
    pieces = [(flat[2 * k], flat[2 * k + 1]) for k in range(n_pairs)]
    normed, qkv, mixture, totals, weight, sem = refs[n_own + 2 * n_pairs:]
    copies = piece_copies(place, own, pieces, 0, weight, sem)
    for copy in copies:
        copy.start()
    width = QUERY_HEADS * HEAD_SIZE
    kv_width = KEY_VALUE_HEADS * HEAD_SIZE
    source = tokens[...].astype(f32)
    inverse = lax.rsqrt(jnp.mean(source * source, axis=1, keepdims=True) + epsilon)
    normed[...] = (source * inverse * gain[...]).astype(bf16)
    for copy in copies:
        copy.wait()
    wide = 512

    @pl.loop(0, qkv.shape[1] // wide)
    def _(tile):
        cols = lanes(tile * wide, wide)
        qkv[:, cols] = mm(normed[...], weight[:, cols]).astype(bf16)

    totals[...] = jnp.zeros_like(totals)
    segment_of_row, segment_of_col, pad = segment_row[...], segment_col[...], pad_row[...]

    @pl.loop(0, KEY_VALUE_HEADS)
    def _(c):
        for first in range(0, tokens_total, block):
            span = first + block
            rows = slice(first, span)
            mask = attention_mask(segment_of_row, segment_of_col, pad, first, block, span)
            keys = qkv[:span, lanes(width + c * HEAD_SIZE, HEAD_SIZE)]
            values = qkv[:span, lanes(width + kv_width + c * HEAD_SIZE, HEAD_SIZE)]
            scores = mm_nt(stacked(qkv, rows, c), keys) * SCORE_SCALE
            lane = lax.broadcasted_iota(jnp.int32, (block, 128), 1)
            stats = totals[rows, :]
            weights = []
            for g in range(GROUP):
                part = jnp.where(mask, scores[g * block:(g + 1) * block], neg_fill)
                top = jnp.max(part, axis=1, keepdims=True)
                raised = jnp.exp(part - top)
                total = jnp.sum(raised, axis=1, keepdims=True)
                stats = jnp.where(lane == c * GROUP + g, top + jnp.log(total), stats)
                weights.append((raised * (1.0 / total)).astype(bf16))
            totals[rows, :] = stats
            mixed = mm(jnp.concatenate(weights, axis=0), values).astype(bf16)
            for g in range(GROUP):
                mixture[rows, lanes((c * GROUP + g) * HEAD_SIZE, HEAD_SIZE)] = mixed[g * block:(g + 1) * block]


def attend_call(place, tokens, gain, segments, pads, own, pieces):
    rows, features = tokens.shape
    width = (QUERY_HEADS + 2 * KEY_VALUE_HEADS) * HEAD_SIZE
    mixed = QUERY_HEADS * HEAD_SIZE
    flat = [part for pair in pieces for part in pair]
    shape = jax.ShapeDtypeStruct
    return pl.pallas_call(
        functools.partial(attend_kernel, len(own), len(pieces), rows, 128),
        out_shape=[
            shape((rows, features), bf16), shape((rows, width), bf16), shape((rows, mixed), bf16),
            shape((rows, 128), f32),
        ],
        in_specs=specs("s" + "v" * 5 + "a" * (len(own) + len(flat))),
        out_specs=specs("vvvv"),
        scratch_shapes=[
            pltpu.VMEM((features, width), bf16),
            pltpu.SemaphoreType.DMA((len(own) + len(flat),)),
        ],
        compiler_params=params(),
        cost_estimate=COST,
        name="attend",
    )(place, tokens, gain, segments, segments.reshape(rows, 1), pads, *own, *flat)


def attend_back_kernel(tokens_total, block, segment_row, segment_col, pad_row, qkv, totals, given, normed,
                       grad, local, grad_keys, grad_values):
    width = QUERY_HEADS * HEAD_SIZE
    kv_width = KEY_VALUE_HEADS * HEAD_SIZE
    segment_of_row, segment_of_col, pad = segment_row[...], segment_col[...], pad_row[...]

    @pl.loop(0, KEY_VALUE_HEADS)
    def _(c):
        grad_keys[...] = jnp.zeros_like(grad_keys)
        grad_values[...] = jnp.zeros_like(grad_values)
        for first in range(0, tokens_total, block):
            span = first + block
            rows = slice(first, span)
            mask = attention_mask(segment_of_row, segment_of_col, pad, first, block, span)
            keys = qkv[:span, lanes(width + c * HEAD_SIZE, HEAD_SIZE)]
            values = qkv[:span, lanes(width + kv_width + c * HEAD_SIZE, HEAD_SIZE)]
            queries = stacked(qkv, rows, c)
            arrived = stacked(given, rows, c)
            scores = mm_nt(queries, keys) * SCORE_SCALE
            grad_weights = mm_nt(arrived, values)
            lane = lax.broadcasted_iota(jnp.int32, (block, 128), 1)
            stats = totals[rows, :]
            weights, grad_scores = [], []
            for g in range(GROUP):
                at = slice(g * block, (g + 1) * block)
                total = jnp.sum(jnp.where(lane == c * GROUP + g, stats, 0.0), axis=1, keepdims=True)
                probs = jnp.exp(jnp.where(mask, scores[at], neg_fill) - total)
                weights.append(probs.astype(bf16))
                dw = grad_weights[at]
                mean = jnp.sum(probs * dw, axis=1, keepdims=True)
                grad_scores.append((probs * (dw - mean)).astype(bf16))
            weights = jnp.concatenate(weights, axis=0)
            grad_scores = jnp.concatenate(grad_scores, axis=0)
            grad_queries = (mm(grad_scores, keys) * SCORE_SCALE).astype(bf16)
            for g in range(GROUP):
                grad[rows, lanes((c * GROUP + g) * HEAD_SIZE, HEAD_SIZE)] = grad_queries[g * block:(g + 1) * block]
            grad_keys[:span, :] += mm_tn(grad_scores, queries)
            grad_values[:span, :] += mm_tn(weights, arrived)
        grad[:, lanes(width + c * HEAD_SIZE, HEAD_SIZE)] = (grad_keys[...] * SCORE_SCALE).astype(bf16)
        grad[:, lanes(width + kv_width + c * HEAD_SIZE, HEAD_SIZE)] = grad_values[...].astype(bf16)

    tall = 256

    @pl.loop(0, normed.shape[1] // tall)
    def _(tile):
        cols = lanes(tile * tall, tall)
        local[pl.ds(pl.multiple_of(tile * tall, tall), tall), :] = mm_tn(normed[:, cols], grad[...]).astype(bf16)


def attend_back_call(segments, pads, qkv, totals, given, normed):
    rows, width = qkv.shape
    features = normed.shape[1]
    shape = jax.ShapeDtypeStruct
    return pl.pallas_call(
        functools.partial(attend_back_kernel, rows, 128),
        out_shape=[shape((rows, width), bf16), shape((features, width), bf16)],
        in_specs=specs("v" * 7),
        out_specs=specs("vv"),
        scratch_shapes=[pltpu.VMEM((rows, HEAD_SIZE), f32), pltpu.VMEM((rows, HEAD_SIZE), f32)],
        compiler_params=params(),
        cost_estimate=COST,
        name="attend_back",
    )(segments, segments.reshape(rows, 1), pads, qkv, totals, given, normed)


def route_kernel(experts, n_own, n_pairs, place, mixture, tokens, gain, router_weight, slots, *refs):
    own = refs[:n_own]
    flat = refs[n_own:n_own + 2 * n_pairs]
    pieces = [(flat[2 * k], flat[2 * k + 1]) for k in range(n_pairs)]
    hidden, payload, weight, sem = refs[n_own + 2 * n_pairs:]
    copies = piece_copies(place, own, pieces, (QUERY_HEADS + 2 * KEY_VALUE_HEADS) * HEAD_SIZE // 2, weight, sem)
    for copy in copies:
        copy.start()
    for copy in copies:
        copy.wait()
    features = tokens.shape[1]
    wide = features // 2

    @pl.loop(0, 2)
    def _(tile):
        cols = lanes(tile * wide, wide)
        hidden[:, cols] = tokens[:, cols].astype(f32) + mm(mixture[...], weight[:, cols])

    value = hidden[...]
    inverse = lax.rsqrt(jnp.mean(value * value, axis=1, keepdims=True) + epsilon)
    payload[:, :features] = (value * inverse * gain[...]).astype(bf16)
    extra = payload.shape[1] - features
    logits = mm(payload[:, :features], router_weight[...])
    lane = lax.broadcasted_iota(jnp.int32, logits.shape, 1)
    logits = jnp.where(lane < experts, logits, neg_fill)
    raised = jnp.exp(logits - jnp.max(logits, axis=1, keepdims=True))
    router = raised / jnp.sum(raised, axis=1, keepdims=True)
    high, middle, low = split_three(router)
    tail = high.astype(f32)
    tail = tail + pltpu.roll(middle.astype(f32), experts, 1)
    tail = tail + pltpu.roll(low.astype(f32), 2 * experts, 1)
    payload[:, features:] = (tail + slots[...]).astype(bf16)


def tail_width(experts):
    return (5 * experts + 127) // 128 * 128


def route_call(place, mixture, tokens, gain, router_weight, slots, own, pieces, experts):
    rows, features = tokens.shape
    extra = tail_width(experts)
    flat = [part for pair in pieces for part in pair]
    shape = jax.ShapeDtypeStruct
    return pl.pallas_call(
        functools.partial(route_kernel, experts, len(own), len(pieces)),
        out_shape=[shape((rows, features), f32), shape((rows, features + extra), bf16)],
        in_specs=specs("s" + "v" * 5 + "a" * (len(own) + len(flat))),
        out_specs=specs("vv"),
        scratch_shapes=[
            pltpu.VMEM((mixture.shape[1], features), bf16),
            pltpu.SemaphoreType.DMA((len(own) + len(flat),)),
        ],
        compiler_params=params(),
        cost_estimate=COST,
        name="route",
    )(place, mixture, tokens, gain, router_weight, slots, *own, *flat)


def branch_kernel(experts, n_back, n_own, n_pairs, place, cotangent, hidden, payload, gain, router_weight,
                  mixture, *refs):
    backs, refs = refs[:n_back], refs[n_back:]
    own = refs[:n_own]
    flat = refs[n_own:n_own + 2 * n_pairs]
    pieces = [(flat[2 * k], flat[2 * k + 1]) for k in range(n_pairs)]
    grad_hidden, given, local_out, local_gain, local_router, weight, branch, sem = refs[n_own + 2 * n_pairs:]
    copies = piece_copies(place, own, pieces, (QUERY_HEADS + 2 * KEY_VALUE_HEADS) * HEAD_SIZE // 2, weight, sem)
    for copy in copies:
        copy.start()
    rows, features = cotangent.shape
    extra = payload.shape[1] - features

    def arrived(cols):
        total = backs[0][:, cols].astype(f32)
        for ref in backs[1:]:
            total = total + ref[:, cols].astype(f32)
        return total

    def three(value):
        width = value.shape[1]
        return (value + pltpu.roll(value, width - experts, 1)
                + pltpu.roll(value, width - 2 * experts, 1))

    lane = lax.broadcasted_iota(jnp.int32, (rows, extra), 1)
    router = jnp.where(lane < experts, three(payload[:, features:].astype(f32)), 0.0)
    select = jnp.where(lane < experts, three(arrived(slice(features, features + extra))), 0.0)
    logits = router * (select - jnp.sum(router * select, axis=1, keepdims=True))
    high, middle, low = split_three(logits)
    packed = high.astype(f32) + pltpu.roll(middle.astype(f32), experts, 1)
    packed = (packed + pltpu.roll(low.astype(f32), 2 * experts, 1)).astype(bf16)
    grad_normed = arrived(slice(0, features)) + mm_nt(packed, router_weight[...])
    local_router[...] = mm_tn(packed, payload[:, :features])
    value = hidden[...]
    inverse = lax.rsqrt(jnp.mean(value * value, axis=1, keepdims=True) + epsilon)
    along = grad_normed * value
    local_gain[...] = jnp.sum(along * inverse, axis=0, keepdims=True)
    mean = jnp.mean(along * gain[...], axis=1, keepdims=True)
    total = cotangent[...].astype(f32) + inverse * (grad_normed * gain[...]) - value * (inverse * inverse * inverse * mean)
    grad_hidden[...] = total
    branch[...] = total.astype(bf16)
    tall = 256

    @pl.loop(0, mixture.shape[1] // tall)
    def _(tile):
        cols = lanes(tile * tall, tall)
        local_out[pl.ds(pl.multiple_of(tile * tall, tall), tall), :] = mm_tn(mixture[:, cols], branch[...]).astype(bf16)

    for copy in copies:
        copy.wait()
    wide = mixture.shape[1] // 2

    @pl.loop(0, 2)
    def _(tile):
        at = pl.ds(pl.multiple_of(tile * wide, 128), wide)
        given[:, lanes(tile * wide, wide)] = mm_nt(branch[...], weight[at, :]).astype(bf16)


def branch_call(place, cotangent, hidden, payload, gain, router_weight, mixture, backs, own, pieces, experts):
    rows, features = cotangent.shape
    extra = payload.shape[1] - features
    mixed = mixture.shape[1]
    flat = [part for pair in pieces for part in pair]
    shape = jax.ShapeDtypeStruct
    return pl.pallas_call(
        functools.partial(branch_kernel, experts, len(backs), len(own), len(pieces)),
        out_shape=[
            shape((rows, features), f32), shape((rows, mixed), bf16), shape((mixed, features), bf16),
            shape((1, features), f32), shape((extra, features), f32),
        ],
        in_specs=specs("s" + "v" * (6 + len(backs)) + "a" * (len(own) + len(flat))),
        out_specs=specs("vvvvv"),
        scratch_shapes=[
            pltpu.VMEM((mixed, features), bf16),
            pltpu.VMEM((rows, features), bf16),
            pltpu.SemaphoreType.DMA((len(own) + len(flat),)),
        ],
        compiler_params=params(),
        cost_estimate=COST,
        name="branch",
    )(place, cotangent, hidden, payload, gain, router_weight, mixture, *backs, *own, *flat)


def input_grad_kernel(n_own, n_pairs, place, tokens, gain, grad, grad_hidden, *refs):
    own = refs[:n_own]
    flat = refs[n_own:n_own + 2 * n_pairs]
    pieces = [(flat[2 * k], flat[2 * k + 1]) for k in range(n_pairs)]
    out, local_gain, weight, normed_grad, sem = refs[n_own + 2 * n_pairs:]
    copies = piece_copies(place, own, pieces, 0, weight, sem)
    for copy in copies:
        copy.start()
    for copy in copies:
        copy.wait()
    features = tokens.shape[1]
    wide = features // 2

    @pl.loop(0, 2)
    def _(tile):
        at = pl.ds(pl.multiple_of(tile * wide, 128), wide)
        normed_grad[:, lanes(tile * wide, wide)] = mm_nt(grad[...], weight[at, :])

    value = tokens[...].astype(f32)
    inverse = lax.rsqrt(jnp.mean(value * value, axis=1, keepdims=True) + epsilon)
    grad_normed = normed_grad[...]
    along = grad_normed * value
    local_gain[...] = jnp.sum(along * inverse, axis=0, keepdims=True)
    mean = jnp.mean(along * gain[...], axis=1, keepdims=True)
    out[...] = grad_hidden[...] + inverse * (grad_normed * gain[...]) - value * (inverse * inverse * inverse * mean)


def input_grad_call(place, tokens, gain, grad, grad_hidden, own, pieces):
    rows, features = tokens.shape
    flat = [part for pair in pieces for part in pair]
    shape = jax.ShapeDtypeStruct
    return pl.pallas_call(
        functools.partial(input_grad_kernel, len(own), len(pieces)),
        out_shape=[shape((rows, features), f32), shape((1, features), f32)],
        in_specs=specs("s" + "v" * 4 + "a" * (len(own) + len(flat))),
        out_specs=specs("vv"),
        scratch_shapes=[
            pltpu.VMEM((features, grad.shape[1]), bf16),
            pltpu.VMEM((rows, features), f32),
            pltpu.SemaphoreType.DMA((len(own) + len(flat),)),
        ],
        compiler_params=params(),
        cost_estimate=COST,
        name="input_grad",
    )(place, tokens, gain, grad, grad_hidden, *own, *flat)


def pair_slots(routes, order_row, experts, capacity):
    pair_count = order_row.shape[0]
    place = (
        jnp.zeros((pair_count,), jnp.int32)
        .at[order_row]
        .set(jnp.arange(pair_count, dtype=jnp.int32), unique_indices=True, mode="promise_in_bounds")
        .reshape(routes.shape)
    )
    columns = jnp.arange(experts, dtype=jnp.int32)
    hit = routes[None, :, :] == columns[:, None, None]
    key = jnp.min(jnp.where(hit, place[None], pair_count), axis=2)
    rank = jnp.sum((key[:, None, :] < key[:, :, None]).astype(jnp.int32), axis=2)
    return jnp.where((key < pair_count) & (rank < capacity), rank + 1, 0).T


def body(
    tokens,
    cotangent,
    norm_attn,
    norm_moe,
    w_query,
    key_weight,
    value_weight,
    w_out,
    w_router,
    w_gate,
    w_up,
    w_down,
    document_index,
    padding_token_mask,
    routes,
    pair_order,
):
    token_rows, features = tokens.shape
    top_count = routes.shape[1]
    experts = lax.axis_size("expert")
    data = lax.axis_size("dp")
    chips = experts // 2
    half = chips // 2
    ff = w_gate.shape[2]
    capacity = 9 * token_rows * top_count // (8 * experts)
    slot_rows = (capacity + 15) // 16 * 16
    extra = tail_width(experts)
    query_width = QUERY_HEADS * HEAD_SIZE
    kv_width = KEY_VALUE_HEADS * HEAD_SIZE
    me = lax.axis_index("expert")
    my_dp = lax.axis_index("dp")
    core = lax.rem(me, 2)
    place = jnp.stack([my_dp, core]).astype(jnp.int32)
    hosted = jnp.stack([me, lax.rem(me + experts // 2, experts), my_dp]).astype(jnp.int32)

    def swap(v):
        return lax.ppermute(v, "expert", [(j, j ^ 1) for j in range(experts)])

    def shift(v, k):
        def to(j):
            chip = j // 2
            return ((chip // half) * half + (chip % half + k) % half) * 2 + j % 2

        return lax.ppermute(v, "expert", [(j, to(j)) for j in range(experts)])

    def across(v):
        return lax.ppermute(v, "expert", [(j, (j + experts // 2) % experts) for j in range(experts)])

    def chip_xor(v, step):
        return lax.ppermute(v, "expert", [(j, ((j // 2) ^ step) * 2 + j % 2) for j in range(experts)])

    def dp_xor(v, k):
        return lax.ppermute(v, "dp", [(j, j ^ k) for j in range(data)])

    def core_half(v):
        width = v.shape[1] // 2
        return jnp.where(core == 0, v[:, :width], v[:, width:])

    def after(v, *others):
        return lax.optimization_barrier((v, others))[0]

    def from_dp(v):
        return [dp_xor(v, k) for k in range(1, data)]

    def dp_part(w):
        rows = w.shape[0] // data
        return lax.dynamic_slice_in_dim(w, my_dp * rows, rows, axis=0)

    own = [w_gate[0], w_up[0], w_down[0]]
    quarter = jnp.concatenate(
        [jnp.concatenate([dp_part(own[0]), dp_part(own[1])], axis=1), dp_part(own[2])], axis=0
    )
    part_rows = quarter.shape[0] // 2
    crossed_one = across(quarter[:part_rows])

    cot_far_same = [shift(cotangent, k) for k in range(1, half)]

    qkv_own = [w_query, key_weight, value_weight]
    qkv_half = (query_width + 2 * kv_width) // 2
    mine = jnp.concatenate([core_half(jnp.concatenate(qkv_own, axis=1)), core_half(w_out)], axis=1)
    near_one, near_two = dp_xor(mine, 1), dp_xor(mine, 2)
    tall = mine.shape[0] // 2
    got = [near_one, near_two, dp_xor(near_two[:tall], 1), dp_xor(near_one[tall:], 2)]
    slots = pair_slots(routes, pair_order[0], experts, capacity)
    slot_columns = jnp.pad(
        jnp.concatenate([slots // 128, slots % 128], axis=1).astype(f32),
        ((0, 0), (3 * experts, extra - 5 * experts)),
    )
    router_weight = jnp.pad(w_router, ((0, 0), (0, extra - experts)))
    router_weight_three = jnp.pad(jnp.concatenate([w_router] * 3, axis=1), ((0, 0), (0, extra - 3 * experts)))
    ready = after(got, crossed_one, cot_far_same, slot_columns, router_weight, router_weight_three)
    pieces = [(v, swap(v)) for v in ready]
    crossed_two = across(after(quarter[part_rows:], crossed_one))
    cot_other = swap(after(cotangent, pieces))
    cot_far_other = [swap(after(v, pieces)) for v in cot_far_same]
    partner_one = lax.all_gather(after(crossed_one, pieces), "dp", axis=0, tiled=True)

    gain_one = norm_attn.reshape(1, features)
    gain_two = norm_moe.reshape(1, features)

    normed_one, qkv, mixture, totals = attend_call(
        place, tokens, gain_one, document_index, padding_token_mask, qkv_own, pieces
    )
    hidden_one, payload = route_call(
        place, after(mixture, crossed_two, cot_other, cot_far_other), tokens, gain_two, router_weight,
        slot_columns, [w_out], pieces, experts,
    )

    payload_far_same = [shift(payload, k) for k in range(1, half)]
    payload_other = swap(payload)
    total_rows = chips // 2 * 2 * slot_rows

    two = after(crossed_two, payload_other)
    partner = [partner_one, two] + from_dp(two)
    spread = tuple((0, d * part_rows, part_rows, (False, d), 0) for d in range(data))
    spread += tuple((1 + k, 0, part_rows, (True, k), part_rows) for k in range(data))

    def rows_of(slot, sources, weights, prev, saved, base, cost=COST):
        return expert_call(
            hosted, (slot,), sources, weights, prev, saved, base, total_rows, experts, slot_rows, data, spread, cost
        )

    one = [(payload, payload_other, cotangent, cot_other)]
    near = rows_of(0, one, own, [], [], 0)
    near_saved = near[4:]
    near = rows_of(1, one, partner, near[:4], [], 0, LONG)
    payload_far_other = [swap(after(v, near[0])) for v in payload_far_same]
    many = list(zip(payload_far_same, payload_far_other, cot_far_same, cot_far_other))
    far = rows_of(1, many, partner, [], near[4:], 2 * slot_rows)
    partner_local = weight_gradient_call(far[4:], data)
    far = rows_of(0, many, own, far[:4], near_saved, 2 * slot_rows)
    saved = far[4:]

    def returned(near_same, near_other, far_same, far_other):
        sums = [
            (far_same[k].astype(f32) + swap(far_other[k]).astype(f32)).astype(bf16)
            for k in range(half - 1)
        ]
        return [near_same[0], swap(near_other[0])], sums

    def scattered(v):
        return lax.psum_scatter(v, "dp", scatter_dimension=0, tiled=True)

    partner_sum = scattered(partner_local)
    backs, back_sums = returned(near[2], near[3], far[2], far[3])
    backs += [shift(v, half - 1 - k) for k, v in enumerate(back_sums)]
    own_local = weight_gradient_call([after(saved[0], back_sums), *saved[1:]], data)
    own_sum = scattered(after(own_local, partner_sum, backs))
    grad_hidden, given, local_out, local_norm_moe, local_router = branch_call(
        place, cotangent, hidden_one, payload, gain_two, router_weight_three, mixture, backs,
        [w_out], pieces, experts,
    )

    def halved(v):
        width = v.shape[1] // 2
        keep = core_half(v)
        give = jnp.where(core == 0, v[:, width:], v[:, :width])
        return (keep.astype(f32) + swap(give).astype(f32)).astype(bf16)

    def fold(sides, stage, *others):
        done = []
        for side, order in zip(sides, ((0, 1), (1, 0))):
            axis = order[stage]
            bit, step = ((my_dp // 2, 2), (lax.rem(my_dp, 2), 1))[axis]
            keep = lax.dynamic_index_in_dim(side, bit, axis, keepdims=True)
            give = lax.dynamic_index_in_dim(side, 1 - bit, axis, keepdims=True)
            done.append((keep.astype(f32) + after(dp_xor(give, step), *others).astype(f32)).astype(bf16))
        return done

    def sides_of(part):
        rows, quart = part.shape[0] // data, part.shape[1] // 2
        return [v.reshape(2, 2, rows, quart) for v in (part[:, :quart], part[:, quart:])]

    def chip_sum(part):
        sizes = []
        step = 1
        chip = me // 2
        while step < chips:
            size = part.shape[0] // 2
            bit = lax.rem(chip // step, 2)
            keep = lax.dynamic_slice_in_dim(part, bit * size, size, axis=0)
            give = lax.dynamic_slice_in_dim(part, (1 - bit) * size, size, axis=0)
            part = (keep.astype(f32) + chip_xor(give, step).astype(f32)).astype(bf16)
            sizes.append((step, bit))
            step *= 2
        for step, bit in reversed(sizes):
            other = chip_xor(part, step)
            part = jnp.concatenate(
                [jnp.where(bit == 0, part, other), jnp.where(bit == 0, other, part)], axis=0
            )
        return part

    def joined(part):
        other = swap(part)
        first = jnp.where(core == 0, part, other)
        second = jnp.where(core == 0, other, part)
        return first, second

    thirds = jnp.split(partner_sum, 3, axis=0)
    arrived_one = across(after(thirds[0], backs))
    arrived_two = across(after(thirds[1], arrived_one))
    given, local_out = after((given, local_out), arrived_one)
    out_half = halved(local_out)
    outs, out_sums = returned(near[0], near[1], far[0], far[1])
    half_rows = token_rows // 2
    outs_one = [shift(after(v[:half_rows], arrived_one), half - 1 - k) for k, v in enumerate(out_sums)]
    grad_qkv, local_qkv = attend_back_call(
        document_index, padding_token_mask, qkv, totals, given, normed_one
    )
    local_qkv = after(local_qkv, arrived_two, outs_one)
    arrived_three = across(after(thirds[2], arrived_two))
    outs_two = [shift(after(v[half_rows:], outs_one), half - 1 - k) for k, v in enumerate(out_sums)]
    sides = sides_of(jnp.concatenate([out_half, halved(local_qkv)], axis=1))
    grad_tokens, local_norm_attn = input_grad_call(
        place, tokens, gain_one, grad_qkv, grad_hidden, qkv_own, pieces
    )
    sides = fold(sides, 0, grad_tokens)
    arrived_three = after(arrived_three, sides)
    arrived = jnp.concatenate([arrived_one, arrived_two, arrived_three], axis=0)
    expert_sum = (own_sum.astype(f32) + arrived.astype(f32)).astype(bf16)
    whole = lax.all_gather(expert_sum, "dp", axis=0, tiled=True).reshape(data, -1, 2 * ff)
    tall = features // data
    grad_gate = whole[:, :tall, :ff].reshape(1, features, ff).astype(f32)
    grad_up = whole[:, :tall, ff:].reshape(1, features, ff).astype(f32)
    grad_down = whole[:, tall:, :].reshape(1, ff, features).astype(f32)
    outs_two = after(outs_two, grad_tokens)
    sides = fold(sides, 1, outs_two)
    outs += [jnp.concatenate([one, two], axis=0) for one, two in zip(outs_one, outs_two)]
    rows = features // data
    part = jnp.concatenate([v.reshape(rows, -1) for v in sides], axis=1)
    local_norm_attn = after(local_norm_attn, part)
    first, second = joined(chip_sum(part))
    out_half = features // 2
    grad_out = jnp.concatenate([first[:, :out_half], second[:, :out_half]], axis=1).astype(f32)
    first, second = first[:, out_half:].astype(f32), second[:, out_half:].astype(f32)
    kept = query_width - qkv_half
    grad_query = jnp.concatenate([first, second[:, :kept]], axis=1)
    grad_key = second[:, kept:kept + kv_width]
    grad_value = second[:, kept + kv_width:]

    routed = outs[0].astype(f32)
    for part in outs[1:]:
        routed = routed + part.astype(f32)
    block_out = (hidden_one + routed).astype(bf16)

    local_router = local_router[:3 * experts].reshape(3, experts, features).sum(0)
    small = jnp.concatenate([local_router, local_norm_attn, local_norm_moe], axis=0)
    small = small + swap(small)
    for step in range(data.bit_length() - 1):
        small = small + dp_xor(small, 1 << step)
    step = 1
    while step < chips:
        small = small + chip_xor(small, step)
        step *= 2
    grad_router = small[:experts].T
    grad_norm_attn = small[experts]
    grad_norm_moe = small[experts + 1]
    return (
        block_out,
        grad_tokens,
        grad_norm_attn,
        grad_norm_moe,
        grad_query,
        grad_key,
        grad_value,
        grad_out,
        grad_router,
        grad_gate,
        grad_up,
        grad_down,
    )


def solution(mesh):
    rows = P(("dp", "expert"), None)
    over_dp = P("dp", None)
    over_expert = P("expert", None, None)
    return jax.shard_map(
        body,
        mesh=mesh,
        in_specs=(
            rows, rows, P(), P(), over_dp, over_dp, over_dp, over_dp, P(),
            over_expert, over_expert, over_expert, rows, rows, rows, rows,
        ),
        out_specs=(
            rows, rows, P(), P(), over_dp, over_dp, over_dp, over_dp, P(),
            over_expert, over_expert, over_expert,
        ),
        check_vma=False,
    )
```

```python
import functools

import jax
import jax.numpy as jnp
from jax import lax
from jax.experimental import pallas as pl
from jax.experimental.pallas import tpu as pltpu
from jax.sharding import PartitionSpec as P

bf16 = jnp.bfloat16
f32 = jnp.float32
MIB = 1024 * 1024
LONG = pl.CostEstimate(flops=16 << 30, bytes_accessed=30 * MIB, transcendentals=0)
COST = pl.CostEstimate(flops=1000, bytes_accessed=1000, transcendentals=0)
NT_DIMS = (((1,), (1,)), ((), ()))
TN_DIMS = (((0,), (0,)), ((), ()))


def mm(a, b):
    return jnp.dot(a, b, preferred_element_type=f32)


def mm_nt(a, b):
    return lax.dot_general(a, b, NT_DIMS, preferred_element_type=f32)


def mm_tn(a, b):
    return lax.dot_general(a, b, TN_DIMS, preferred_element_type=f32)


def split_three(v):
    high = v.astype(bf16)
    rest = v - high.astype(f32)
    middle = rest.astype(bf16)
    low = (rest - middle.astype(f32)).astype(bf16)
    return high, middle, low


def lanes(start, size):
    return pl.ds(pl.multiple_of(start, 128), size)


def specs(kinds):
    table = {"s": pltpu.SMEM, "v": pltpu.VMEM, "a": pl.ANY}
    return [pl.BlockSpec(memory_space=table[kind]) for kind in kinds]


def params():
    return pltpu.CompilerParams(vmem_limit_bytes=60 * MIB)


def expert_kernel(experts, slots, base, data, pieces, chunks, cuts, n_weights, n_prev, n_saved, rows, *refs):
    count = len(slots)
    each = 2 + 2 * len(cuts)
    hosted, sources, refs = refs[0], refs[1:1 + each * chunks], refs[1 + each * chunks:]
    sources = [sources[each * i:each * (i + 1)] for i in range(chunks)]
    weight_refs, refs = refs[:n_weights], refs[n_weights:]
    prev, refs = refs[:n_prev], refs[n_prev + n_saved:]
    po_same, po_other, pg_same, pg_other, x_out, gp_out, h_out, gg_out, gu_out = refs[:9]
    (wg, wu, wd, nbuf, cbuf, x, gp, gc, sc, h, gg, gu, dmat, dtmat, gcol, vcol, tail_t,
     w_sem, in_sem, act_sem, p_sem) = refs[9:]
    tokens, features = sources[0][0].shape[0], sources[0][2].shape[1]
    extra = sources[0][0].shape[1] - features
    ff = wg.shape[2]
    wide = features // 2
    tail = slice(features, features + extra)

    weight_copies = []
    taken = 0
    for place, slot in enumerate(slots):
        if slot == 0:
            pairs = list(zip(weight_refs[taken:taken + 3], (wg.at[place], wu.at[place], wd.at[place])))
            taken += 3
        else:
            tall_f, tall_h = features // data, ff // data
            pairs = []
            for index, begin, size, whose, first in pieces:
                ref = weight_refs[taken + index]
                source = jnp.bitwise_xor(hosted[2], whose[1]) if whose[0] else whose[1]
                wide_rows = max(0, min(size, tall_f - first))
                if wide_rows:
                    at = pl.ds(pl.multiple_of(source * tall_f + first, 16), wide_rows)
                    pairs += [
                        (ref.at[pl.ds(begin, wide_rows), pl.ds(0, ff)], wg.at[place, at]),
                        (ref.at[pl.ds(begin, wide_rows), pl.ds(ff, ff)], wu.at[place, at]),
                    ]
                if wide_rows < size:
                    at = pl.ds(pl.multiple_of(source * tall_h + first + wide_rows - tall_f, 16), size - wide_rows)
                    pairs.append((ref.at[pl.ds(begin + wide_rows, size - wide_rows)], wd.at[place, at]))
            taken += 1 + max(piece[0] for piece in pieces)
        weight_copies.append([
            pltpu.make_async_copy(source, target, w_sem.at[place, i])
            for i, (source, target) in enumerate(pairs)
        ])

    def input_copies(index):
        parts = [cbuf.at[q, pl.ds(first, size)] for q in range(2) for first, size in cuts]
        targets = [nbuf.at[0], nbuf.at[1]] + parts
        return [
            pltpu.make_async_copy(source, target, in_sem.at[i])
            for i, (source, target) in enumerate(zip(sources[index], targets))
        ]

    def act_copies(chunk, place):
        at = pl.ds(pl.multiple_of(base + chunk * 2 * rows, 16), 2 * rows)
        return [
            pltpu.make_async_copy(source.at[place], target.at[place, at], act_sem.at[place, i])
            for i, (source, target) in enumerate(
                ((x, x_out), (gp, gp_out), (h, h_out), (gg, gg_out), (gu, gu_out)))
        ]

    def partial_copies(chunk):
        return (
            pltpu.make_async_copy(nbuf.at[0], pg_same.at[chunk], p_sem.at[0]),
            pltpu.make_async_copy(nbuf.at[1], pg_other.at[chunk], p_sem.at[1]),
            pltpu.make_async_copy(cbuf.at[0], po_same.at[chunk], p_sem.at[2]),
            pltpu.make_async_copy(cbuf.at[1], po_other.at[chunk], p_sem.at[3]),
        )

    def dispatch(q):
        columns = nbuf[q, :, tail].astype(f32)
        tail_t[...] = columns.T
        token_lane = lax.broadcasted_iota(jnp.int32, (tokens, extra), 1)
        wanted = lax.broadcasted_iota(jnp.int32, (tokens, count * rows), 1)
        slot_cols = []
        for place in range(count):
            expert = hosted[slots[place]]
            row = (tail_t[pl.ds(3 * experts + expert, 1), :] * 128.0
                   + tail_t[pl.ds(4 * experts + expert, 1), :] - 1.0).astype(jnp.int32)
            hit = lax.broadcasted_iota(jnp.int32, (rows, tokens), 0) == row
            dmat[q, place * rows:(place + 1) * rows, :] = jnp.where(hit, 1.0, 0.0).astype(bf16)
            factor = jnp.where(token_lane == 3 * experts + expert, 128.0, 0.0)
            factor = jnp.where(token_lane == 4 * experts + expert, 1.0, factor)
            slot_cols.append(jnp.sum(columns * factor, axis=1, keepdims=True).astype(jnp.int32) - 1)
        target = slot_cols[0]
        if count == 2:
            second = wanted >= rows
            target = jnp.where(second, slot_cols[1], slot_cols[0])
            wanted = jnp.where(second, wanted - rows, wanted)
        dtmat[q] = jnp.where(wanted == target, 1.0, 0.0).astype(bf16)
        parts = mm(dmat[q], nbuf[q, :, tail])
        lane = lax.broadcasted_iota(jnp.int32, (rows, extra), 1)
        for place in range(count):
            expert = hosted[slots[place]]
            mine = (lane == expert) | (lane == expert + experts) | (lane == expert + 2 * experts)
            g = jnp.sum(jnp.where(mine, parts[place * rows:(place + 1) * rows], 0.0), axis=1, keepdims=True)
            gcol[place, q * rows:(q + 1) * rows, :] = jnp.broadcast_to(g, (rows, 128))

        @pl.loop(0, 2)
        def _(tile):
            cols = lanes(tile * wide, wide)
            found = mm(dmat[q], nbuf[q, :, cols]).astype(bf16)
            cot = mm(dmat[q], cbuf[q, :, cols])
            gc[q, :, cols] = cot.astype(bf16)
            for place in range(count):
                at = slice(q * rows, (q + 1) * rows)
                own = slice(place * rows, (place + 1) * rows)
                x[place, at, cols] = found[own]
                gp[place, at, cols] = (cot[own] * gcol[place, at, 0:1]).astype(bf16)

    def forward_backward(place):
        for q in range(2):
            at = slice(q * rows, (q + 1) * rows)
            gate = mm(x[place, at, :], wg[place])
            up = mm(x[place, at, :], wu[place])
            dh = mm_nt(gp[place, at, :], wd[place])
            sig = 1.0 / (1.0 + jnp.exp(-gate))
            act = gate * sig
            h[place, at, :] = (act * up).astype(bf16)
            gg[place, at, :] = (dh * up * (sig * (1.0 + gate * (1.0 - sig)))).astype(bf16)
            gu[place, at, :] = (dh * act).astype(bf16)

    def produce(place):
        vcol[place] = jnp.zeros(vcol.shape[1:], f32)

        @pl.loop(0, 2)
        def _(tile):
            cols = lanes(tile * wide, wide)
            for q in range(2):
                at = slice(q * rows, (q + 1) * rows)
                own = pl.ds(pl.multiple_of(place * rows, 16), rows)
                produced = mm(h[place, at, :], wd[place, :, cols]).astype(bf16).astype(f32)
                along = produced * gc[q, own, cols].astype(f32)
                folded = along[:, :128]
                for part in range(1, wide // 128):
                    folded = folded + along[:, part * 128:(part + 1) * 128]
                vcol[place, at, :] += folded
                sc[q, own, cols] = (produced * gcol[place, at, 0:1]).astype(bf16)
                back = mm_nt(gg[place, at, :], wg[place, cols, :]) + mm_nt(gu[place, at, :], wu[place, cols, :])
                gc[q, own, cols] = back.astype(bf16)

    def combine(q):
        at = slice(q * rows, (q + 1) * rows)
        lane = lax.broadcasted_iota(jnp.int32, (rows, extra), 1)
        payload = []
        for place in range(count):
            expert = hosted[slots[place]]
            high, middle, low = split_three(jnp.sum(vcol[place, at, :], axis=1, keepdims=True))
            part = jnp.where(lane == expert, high.astype(f32), 0.0)
            part = jnp.where(lane == expert + experts, middle.astype(f32), part)
            part = jnp.where(lane == expert + 2 * experts, low.astype(f32), part)
            payload.append(part.astype(bf16))
        payload = jnp.concatenate(payload, axis=0) if count > 1 else payload[0]
        tail_sum = mm(dtmat[q], payload)
        if n_prev:
            tail_sum = tail_sum + nbuf[q, :, tail].astype(f32)
        nbuf[q, :, tail] = tail_sum.astype(bf16)

        @pl.loop(0, 2)
        def _(tile):
            cols = lanes(tile * wide, wide)
            back = mm(dtmat[q], gc[q, :, cols])
            out = mm(dtmat[q], sc[q, :, cols])
            if n_prev:
                back = back + nbuf[q, :, cols].astype(f32)
                out = out + cbuf[q, :, cols].astype(f32)
            nbuf[q, :, cols] = back.astype(bf16)
            cbuf[q, :, cols] = out.astype(bf16)

    def prev_copies(chunk):
        po0, po1, pg0, pg1 = prev
        return (
            pltpu.make_async_copy(pg0.at[chunk], nbuf.at[0], in_sem.at[0]),
            pltpu.make_async_copy(pg1.at[chunk], nbuf.at[1], in_sem.at[1]),
            pltpu.make_async_copy(po0.at[chunk], cbuf.at[0], in_sem.at[2]),
            pltpu.make_async_copy(po1.at[chunk], cbuf.at[1], in_sem.at[3]),
        )

    for copy in input_copies(0):
        copy.start()
    for copies in weight_copies:
        for copy in copies:
            copy.start()

    @pl.loop(0, chunks)
    def _(chunk):
        for copy in input_copies(0):
            copy.wait()
        for q in range(2):
            dispatch(q)
        if n_prev:
            for copy in prev_copies(chunk):
                copy.start()
        for place in range(count):
            @pl.when(chunk == 0)
            def _():
                for copy in weight_copies[place]:
                    copy.wait()

            forward_backward(place)
            for copy in act_copies(chunk, place):
                copy.start()
            produce(place)
        if n_prev:
            for copy in prev_copies(chunk):
                copy.wait()
        for q in range(2):
            combine(q)
        for copy in partial_copies(chunk):
            copy.start()
        for place in range(count):
            for copy in act_copies(chunk, place):
                copy.wait()
        for copy in partial_copies(chunk):
            copy.wait()

        for index in range(1, chunks):
            @pl.when(chunk + 1 == index)
            def _():
                for copy in input_copies(index):
                    copy.start()


def expert_call(hosted, slots, sources, weights, prev, saved, base, total, experts, rows, data, pieces, cost):
    chunks = len(sources)
    tokens, features = sources[0][0].shape[0], sources[0][2][0].shape[1]
    cuts, first = [], 0
    for part in sources[0][2]:
        cuts.append((first, part.shape[0]))
        first += part.shape[0]
    flat = [v for same, other, *parts in sources for v in (same, other, *parts[0], *parts[1])]
    ff = weights[0].shape[1] if slots[0] == 0 else weights[0].shape[1] // 2
    wide_n = sources[0][0].shape[1]
    extra = wide_n - features
    count = len(slots)
    shape = jax.ShapeDtypeStruct
    act_f = shape((count, total, features), bf16)
    act_h = shape((count, total, ff), bf16)
    out_shape = (
        [shape((chunks, tokens, features), bf16)] * 2
        + [shape((chunks, tokens, wide_n), bf16)] * 2
        + [act_f, act_f, act_h, act_h, act_h]
    )
    many = 2 * rows
    first_prev = 1 + len(flat) + len(weights)
    first_saved = first_prev + len(prev)
    return pl.pallas_call(
        functools.partial(
            expert_kernel, experts, slots, base, data, pieces, chunks, tuple(cuts), len(weights), len(prev), len(saved), rows),
        out_shape=out_shape,
        in_specs=specs("s" + "a" * (len(flat) + len(weights) + len(prev) + len(saved))),
        out_specs=specs("a" * 9),
        input_output_aliases={
            **{first_prev + i: i for i in range(len(prev))},
            **{first_saved + i: 4 + i for i in range(len(saved))},
        },
        scratch_shapes=[
            pltpu.VMEM((count, features, ff), bf16),
            pltpu.VMEM((count, features, ff), bf16),
            pltpu.VMEM((count, ff, features), bf16),
            pltpu.VMEM((2, tokens, wide_n), bf16),
            pltpu.VMEM((2, tokens, features), bf16),
            pltpu.VMEM((count, many, features), bf16),
            pltpu.VMEM((count, many, features), bf16),
            pltpu.VMEM((2, count * rows, features), bf16),
            pltpu.VMEM((2, count * rows, features), bf16),
            pltpu.VMEM((count, many, ff), bf16),
            pltpu.VMEM((count, many, ff), bf16),
            pltpu.VMEM((count, many, ff), bf16),
            pltpu.VMEM((2, count * rows, tokens), bf16),
            pltpu.VMEM((2, tokens, count * rows), bf16),
            pltpu.VMEM((count, many, 128), f32),
            pltpu.VMEM((count, many, 128), f32),
            pltpu.VMEM((extra, tokens), f32),
            pltpu.SemaphoreType.DMA((count, 3 * max(1, len(pieces)))),
            pltpu.SemaphoreType.DMA((max(4, 2 + 2 * len(cuts)),)),
            pltpu.SemaphoreType.DMA((count, 5)),
            pltpu.SemaphoreType.DMA((4,)),
        ],
        compiler_params=params(),
        cost_estimate=cost,
        name="expert_rows",
    )(hosted, *flat, *weights, *prev, *saved)


def weight_gradient_kernel(data, x_in, gg_in, gu_in, h_in, gp_in, out, x, gg, gu, h, gp, wide, down, sem, out_sem):
    features, ff = x.shape[1], h.shape[1]
    loads = [
        pltpu.make_async_copy(source.at[0], target, sem.at[i])
        for i, (source, target) in enumerate(((gg_in, gg), (x_in, x), (gu_in, gu), (h_in, h), (gp_in, gp)))
    ]
    for copy in loads:
        copy.start()
    tall_f, tall_h = features // data, ff // data
    step = tall_f + tall_h
    stores = [
        pltpu.make_async_copy(wide.at[pl.ds(d * tall_f, tall_f)], out.at[pl.ds(d * step, tall_f)], out_sem.at[2 * d])
        for d in range(data)
    ] + [
        pltpu.make_async_copy(down.at[pl.ds(d * tall_h, tall_h)], out.at[pl.ds(d * step + tall_f, tall_h)],
                              out_sem.at[2 * d + 1])
        for d in range(data)
    ]
    for copy in loads[:3]:
        copy.wait()
    tall = 256

    @pl.loop(0, features // tall)
    def _(tile):
        cols = lanes(tile * tall, tall)
        at = pl.ds(pl.multiple_of(tile * tall, tall), tall)
        wide[at, :ff] = mm_tn(x[:, cols], gg[...]).astype(bf16)
        wide[at, ff:] = mm_tn(x[:, cols], gu[...]).astype(bf16)

    for copy in stores[:data]:
        copy.start()
    for copy in loads[3:]:
        copy.wait()

    @pl.loop(0, ff // tall)
    def _(tile):
        cols = lanes(tile * tall, tall)
        at = pl.ds(pl.multiple_of(tile * tall, tall), tall)
        down[at, :] = mm_tn(h[:, cols], gp[...]).astype(bf16)

    for copy in stores[data:]:
        copy.start()
    for copy in stores:
        copy.wait()


def weight_gradient_call(saved, data):
    x, gp, h, gg, gu = saved
    slots, features, ff = x.shape[1], x.shape[2], h.shape[2]
    return pl.pallas_call(
        functools.partial(weight_gradient_kernel, data),
        out_shape=jax.ShapeDtypeStruct((features + ff, 2 * ff), bf16),
        in_specs=specs("aaaaa"),
        out_specs=pl.BlockSpec(memory_space=pl.ANY),
        scratch_shapes=[
            pltpu.VMEM((slots, features), bf16),
            pltpu.VMEM((slots, ff), bf16),
            pltpu.VMEM((slots, ff), bf16),
            pltpu.VMEM((slots, ff), bf16),
            pltpu.VMEM((slots, features), bf16),
            pltpu.VMEM((features, 2 * ff), bf16),
            pltpu.VMEM((ff, features), bf16),
            pltpu.SemaphoreType.DMA((5,)),
            pltpu.SemaphoreType.DMA((2 * data,)),
        ],
        compiler_params=params(),
        cost_estimate=COST,
        name="expert_weight_gradients",
    )(x, gg, gu, h, gp)


def widened_kernel(whole, gate, up, down):
    tall, ff = gate.shape
    gate[...] = whole[:tall, :ff].astype(f32)
    up[...] = whole[:tall, ff:].astype(f32)
    down[...] = whole[tall:, :].astype(f32)


def widened(whole, data):
    rows, features = whole.shape[0] // data, whole.shape[1]
    ff = features // 2
    tall = rows * 2 // 3
    blocks = [(tall, ff), (tall, ff), (rows - tall, features)]
    return pl.pallas_call(
        widened_kernel,
        grid=(data,),
        in_specs=[pl.BlockSpec((rows, features), lambda d: (d, 0))],
        out_specs=[pl.BlockSpec(block, lambda d: (d, 0)) for block in blocks],
        out_shape=[jax.ShapeDtypeStruct((data * block[0], block[1]), f32) for block in blocks],
        compiler_params=params(),
        cost_estimate=COST,
        name="widened",
    )(whole)


epsilon = 1e-06
neg_fill = -1e30
QUERY_HEADS = 12
KEY_VALUE_HEADS = 2
HEAD_SIZE = 128
GROUP = QUERY_HEADS // KEY_VALUE_HEADS
SCORE_SCALE = HEAD_SIZE ** (-0.5)


def piece_copies(place, own, pieces, begin, weight, sem):
    rows, half = own[0].shape[0], weight.shape[1] // 2
    mine, core = place[0], place[1]
    copies = []
    column = 0
    for part in own:
        at = weight.at[pl.ds(pl.multiple_of(mine * rows, 16), rows), pl.ds(column, part.shape[1])]
        copies.append(pltpu.make_async_copy(part, at, sem.at[len(copies)]))
        column += part.shape[1]
    for (k, skip), pair in zip(((1, 0), (2, 0), (3, 0), (3, rows // 2)), pieces):
        first = pl.multiple_of(jnp.bitwise_xor(mine, k) * rows + skip, 16)
        for part, which in zip(pair, (core, 1 - core)):
            at = weight.at[pl.ds(first, part.shape[0]), lanes(which * half, half)]
            copies.append(pltpu.make_async_copy(part.at[:, pl.ds(begin, half)], at, sem.at[len(copies)]))
    return copies


def attention_mask(segment_row, segment_col, pad_row, first, size, span):
    row = first + lax.broadcasted_iota(jnp.int32, (size, span), 0)
    col = lax.broadcasted_iota(jnp.int32, (size, span), 1)
    same = segment_col[first:first + size, :] == segment_row[:, :span]
    return same & (((pad_row[:, :span] == 1) & (col < row)) | (col == row))


def stacked(ref, rows, c):
    return jnp.concatenate(
        [ref[rows, lanes((c * GROUP + g) * HEAD_SIZE, HEAD_SIZE)] for g in range(GROUP)], axis=0
    )


def attend_kernel(
    n_own, n_pairs, tokens_total, block,
    place, tokens, gain, segment_row, segment_col, pad_row, *refs,
):
    own = refs[:n_own]
    flat = refs[n_own:n_own + 2 * n_pairs]
    pieces = [(flat[2 * k], flat[2 * k + 1]) for k in range(n_pairs)]
    normed, qkv, mixture, totals, weight, sem = refs[n_own + 2 * n_pairs:]
    copies = piece_copies(place, own, pieces, 0, weight, sem)
    for copy in copies:
        copy.start()
    width = QUERY_HEADS * HEAD_SIZE
    kv_width = KEY_VALUE_HEADS * HEAD_SIZE
    source = tokens[...].astype(f32)
    inverse = lax.rsqrt(jnp.mean(source * source, axis=1, keepdims=True) + epsilon)
    normed[...] = (source * inverse * gain[...]).astype(bf16)
    for copy in copies:
        copy.wait()
    wide = 512

    @pl.loop(0, qkv.shape[1] // wide)
    def _(tile):
        cols = lanes(tile * wide, wide)
        qkv[:, cols] = mm(normed[...], weight[:, cols]).astype(bf16)

    totals[...] = jnp.zeros_like(totals)
    segment_of_row, segment_of_col, pad = segment_row[...], segment_col[...], pad_row[...]

    @pl.loop(0, KEY_VALUE_HEADS)
    def _(c):
        for first in range(0, tokens_total, block):
            span = first + block
            rows = slice(first, span)
            mask = attention_mask(segment_of_row, segment_of_col, pad, first, block, span)
            keys = qkv[:span, lanes(width + c * HEAD_SIZE, HEAD_SIZE)]
            values = qkv[:span, lanes(width + kv_width + c * HEAD_SIZE, HEAD_SIZE)]
            scores = mm_nt(stacked(qkv, rows, c), keys) * SCORE_SCALE
            lane = lax.broadcasted_iota(jnp.int32, (block, 128), 1)
            stats = totals[rows, :]
            weights = []
            for g in range(GROUP):
                part = jnp.where(mask, scores[g * block:(g + 1) * block], neg_fill)
                top = jnp.max(part, axis=1, keepdims=True)
                raised = jnp.exp(part - top)
                total = jnp.sum(raised, axis=1, keepdims=True)
                stats = jnp.where(lane == c * GROUP + g, top + jnp.log(total), stats)
                weights.append((raised * (1.0 / total)).astype(bf16))
            totals[rows, :] = stats
            mixed = mm(jnp.concatenate(weights, axis=0), values).astype(bf16)
            for g in range(GROUP):
                mixture[rows, lanes((c * GROUP + g) * HEAD_SIZE, HEAD_SIZE)] = mixed[g * block:(g + 1) * block]


def attend_call(place, tokens, gain, segments, segment_columns, pads, own, pieces):
    rows, features = tokens.shape
    width = (QUERY_HEADS + 2 * KEY_VALUE_HEADS) * HEAD_SIZE
    mixed = QUERY_HEADS * HEAD_SIZE
    flat = [part for pair in pieces for part in pair]
    shape = jax.ShapeDtypeStruct
    return pl.pallas_call(
        functools.partial(attend_kernel, len(own), len(pieces), rows, 128),
        out_shape=[
            shape((rows, features), bf16), shape((rows, width), bf16), shape((rows, mixed), bf16),
            shape((rows, 128), f32),
        ],
        in_specs=specs("s" + "v" * 5 + "a" * (len(own) + len(flat))),
        out_specs=specs("vvvv"),
        scratch_shapes=[
            pltpu.VMEM((features, width), bf16),
            pltpu.SemaphoreType.DMA((len(own) + len(flat),)),
        ],
        compiler_params=params(),
        cost_estimate=COST,
        name="attend",
    )(place, tokens, gain, segments, segment_columns, pads, *own, *flat)


def attend_back_kernel(tokens_total, block, place, segment_row, segment_col, pad_row, qkv, totals, given, normed,
                       grad, keep, give, grad_keys, grad_values):
    width = QUERY_HEADS * HEAD_SIZE
    kv_width = KEY_VALUE_HEADS * HEAD_SIZE
    segment_of_row, segment_of_col, pad = segment_row[...], segment_col[...], pad_row[...]

    @pl.loop(0, KEY_VALUE_HEADS)
    def _(c):
        grad_keys[...] = jnp.zeros_like(grad_keys)
        grad_values[...] = jnp.zeros_like(grad_values)
        for first in range(0, tokens_total, block):
            span = first + block
            rows = slice(first, span)
            mask = attention_mask(segment_of_row, segment_of_col, pad, first, block, span)
            keys = qkv[:span, lanes(width + c * HEAD_SIZE, HEAD_SIZE)]
            values = qkv[:span, lanes(width + kv_width + c * HEAD_SIZE, HEAD_SIZE)]
            queries = stacked(qkv, rows, c)
            arrived = stacked(given, rows, c)
            scores = mm_nt(queries, keys) * SCORE_SCALE
            grad_weights = mm_nt(arrived, values)
            lane = lax.broadcasted_iota(jnp.int32, (block, 128), 1)
            stats = totals[rows, :]
            weights, grad_scores = [], []
            for g in range(GROUP):
                at = slice(g * block, (g + 1) * block)
                total = jnp.sum(jnp.where(lane == c * GROUP + g, stats, 0.0), axis=1, keepdims=True)
                probs = jnp.exp(jnp.where(mask, scores[at], neg_fill) - total)
                weights.append(probs.astype(bf16))
                dw = grad_weights[at]
                mean = jnp.sum(probs * dw, axis=1, keepdims=True)
                grad_scores.append((probs * (dw - mean)).astype(bf16))
            weights = jnp.concatenate(weights, axis=0)
            grad_scores = jnp.concatenate(grad_scores, axis=0)
            grad_queries = (mm(grad_scores, keys) * SCORE_SCALE).astype(bf16)
            for g in range(GROUP):
                grad[rows, lanes((c * GROUP + g) * HEAD_SIZE, HEAD_SIZE)] = grad_queries[g * block:(g + 1) * block]
            grad_keys[:span, :] += mm_tn(grad_scores, queries)
            grad_values[:span, :] += mm_tn(weights, arrived)
        grad[:, lanes(width + c * HEAD_SIZE, HEAD_SIZE)] = (grad_keys[...] * SCORE_SCALE).astype(bf16)
        grad[:, lanes(width + kv_width + c * HEAD_SIZE, HEAD_SIZE)] = grad_values[...].astype(bf16)

    tall = 256

    @pl.loop(0, normed.shape[1] // tall)
    def _(tile):
        cols = lanes(tile * tall, tall)
        at = pl.ds(pl.multiple_of(tile * tall, tall), tall)
        for core, out in ((place[1], keep), (1 - place[1], give)):
            out[at, :] = mm_tn(normed[:, cols], grad[:, lanes(core * keep.shape[1], keep.shape[1])]).astype(bf16)


def attend_back_call(place, segments, segment_columns, pads, qkv, totals, given, normed):
    rows, width = qkv.shape
    features = normed.shape[1]
    shape = jax.ShapeDtypeStruct
    return pl.pallas_call(
        functools.partial(attend_back_kernel, rows, 128),
        out_shape=[shape((rows, width), bf16)] + [shape((features, width // 2), bf16)] * 2,
        in_specs=specs("s" + "v" * 7),
        out_specs=specs("vvv"),
        scratch_shapes=[pltpu.VMEM((rows, HEAD_SIZE), f32), pltpu.VMEM((rows, HEAD_SIZE), f32)],
        compiler_params=params(),
        cost_estimate=COST,
        name="attend_back",
    )(place, segments, segment_columns, pads, qkv, totals, given, normed)


def route_kernel(experts, n_own, n_pairs, place, mixture, tokens, gain, router_weight, slots, *refs):
    own = refs[:n_own]
    flat = refs[n_own:n_own + 2 * n_pairs]
    pieces = [(flat[2 * k], flat[2 * k + 1]) for k in range(n_pairs)]
    hidden, payload, weight, sem = refs[n_own + 2 * n_pairs:]
    copies = piece_copies(place, own, pieces, (QUERY_HEADS + 2 * KEY_VALUE_HEADS) * HEAD_SIZE // 2, weight, sem)
    for copy in copies:
        copy.start()
    for copy in copies:
        copy.wait()
    features = tokens.shape[1]
    wide = features // 2

    @pl.loop(0, 2)
    def _(tile):
        cols = lanes(tile * wide, wide)
        hidden[:, cols] = tokens[:, cols].astype(f32) + mm(mixture[...], weight[:, cols])

    value = hidden[...]
    inverse = lax.rsqrt(jnp.mean(value * value, axis=1, keepdims=True) + epsilon)
    payload[:, :features] = (value * inverse * gain[...]).astype(bf16)
    extra = payload.shape[1] - features
    logits = mm(payload[:, :features], router_weight[...])
    lane = lax.broadcasted_iota(jnp.int32, logits.shape, 1)
    logits = jnp.where(lane < experts, logits, neg_fill)
    raised = jnp.exp(logits - jnp.max(logits, axis=1, keepdims=True))
    router = raised / jnp.sum(raised, axis=1, keepdims=True)
    high, middle, low = split_three(router)
    tail = high.astype(f32)
    tail = tail + pltpu.roll(middle.astype(f32), experts, 1)
    tail = tail + pltpu.roll(low.astype(f32), 2 * experts, 1)
    payload[:, features:] = (tail + slots[...]).astype(bf16)


def tail_width(experts):
    return (5 * experts + 127) // 128 * 128


def route_call(place, mixture, tokens, gain, router_weight, slots, own, pieces, experts):
    rows, features = tokens.shape
    extra = tail_width(experts)
    flat = [part for pair in pieces for part in pair]
    shape = jax.ShapeDtypeStruct
    return pl.pallas_call(
        functools.partial(route_kernel, experts, len(own), len(pieces)),
        out_shape=[shape((rows, features), f32), shape((rows, features + extra), bf16)],
        in_specs=specs("s" + "v" * 5 + "a" * (len(own) + len(flat))),
        out_specs=specs("vv"),
        scratch_shapes=[
            pltpu.VMEM((mixture.shape[1], features), bf16),
            pltpu.SemaphoreType.DMA((len(own) + len(flat),)),
        ],
        compiler_params=params(),
        cost_estimate=COST,
        name="route",
    )(place, mixture, tokens, gain, router_weight, slots, *own, *flat)


def branch_kernel(experts, n_back, n_own, n_pairs, place, cotangent, hidden, payload, gain, router_weight,
                  mixture, *refs):
    backs, refs = refs[:n_back], refs[n_back:]
    own = refs[:n_own]
    flat = refs[n_own:n_own + 2 * n_pairs]
    pieces = [(flat[2 * k], flat[2 * k + 1]) for k in range(n_pairs)]
    grad_hidden, given, keep, give, local_gain, local_router, weight, branch, sem = refs[n_own + 2 * n_pairs:]
    copies = piece_copies(place, own, pieces, (QUERY_HEADS + 2 * KEY_VALUE_HEADS) * HEAD_SIZE // 2, weight, sem)
    for copy in copies:
        copy.start()
    rows, features = cotangent.shape
    extra = payload.shape[1] - features

    def arrived(cols):
        total = backs[0][:, cols].astype(f32)
        for ref in backs[1:]:
            total = total + ref[:, cols].astype(f32)
        return total

    def three(value):
        width = value.shape[1]
        return (value + pltpu.roll(value, width - experts, 1)
                + pltpu.roll(value, width - 2 * experts, 1))

    lane = lax.broadcasted_iota(jnp.int32, (rows, extra), 1)
    router = jnp.where(lane < experts, three(payload[:, features:].astype(f32)), 0.0)
    select = jnp.where(lane < experts, three(arrived(slice(features, features + extra))), 0.0)
    logits = router * (select - jnp.sum(router * select, axis=1, keepdims=True))
    high, middle, low = split_three(logits)
    packed = high.astype(f32) + pltpu.roll(middle.astype(f32), experts, 1)
    packed = (packed + pltpu.roll(low.astype(f32), 2 * experts, 1)).astype(bf16)
    grad_normed = arrived(slice(0, features)) + mm_nt(packed, router_weight[...])
    local_router[...] = mm_tn(packed, payload[:, :features])
    value = hidden[...]
    inverse = lax.rsqrt(jnp.mean(value * value, axis=1, keepdims=True) + epsilon)
    along = grad_normed * value
    local_gain[...] = jnp.sum(along * inverse, axis=0, keepdims=True)
    mean = jnp.mean(along * gain[...], axis=1, keepdims=True)
    total = cotangent[...].astype(f32) + inverse * (grad_normed * gain[...]) - value * (inverse * inverse * inverse * mean)
    grad_hidden[...] = total
    branch[...] = total.astype(bf16)
    tall = 256

    @pl.loop(0, mixture.shape[1] // tall)
    def _(tile):
        cols = lanes(tile * tall, tall)
        at = pl.ds(pl.multiple_of(tile * tall, tall), tall)
        for core, out in ((place[1], keep), (1 - place[1], give)):
            out[at, :] = mm_tn(mixture[:, cols], branch[:, lanes(core * keep.shape[1], keep.shape[1])]).astype(bf16)

    for copy in copies:
        copy.wait()
    wide = mixture.shape[1] // 2

    @pl.loop(0, 2)
    def _(tile):
        at = pl.ds(pl.multiple_of(tile * wide, 128), wide)
        given[:, lanes(tile * wide, wide)] = mm_nt(branch[...], weight[at, :]).astype(bf16)


def branch_call(place, cotangent, hidden, payload, gain, router_weight, mixture, backs, own, pieces, experts):
    rows, features = cotangent.shape
    extra = payload.shape[1] - features
    mixed = mixture.shape[1]
    flat = [part for pair in pieces for part in pair]
    shape = jax.ShapeDtypeStruct
    return pl.pallas_call(
        functools.partial(branch_kernel, experts, len(backs), len(own), len(pieces)),
        out_shape=[
            shape((rows, features), f32), shape((rows, mixed), bf16), shape((mixed, features // 2), bf16),
            shape((mixed, features // 2), bf16), shape((1, features), f32), shape((extra, features), f32),
        ],
        in_specs=specs("s" + "v" * (6 + len(backs)) + "a" * (len(own) + len(flat))),
        out_specs=specs("vvvvvv"),
        scratch_shapes=[
            pltpu.VMEM((mixed, features), bf16),
            pltpu.VMEM((rows, features), bf16),
            pltpu.SemaphoreType.DMA((len(own) + len(flat),)),
        ],
        compiler_params=params(),
        cost_estimate=COST,
        name="branch",
    )(place, cotangent, hidden, payload, gain, router_weight, mixture, *backs, *own, *flat)


def input_grad_kernel(n_own, n_pairs, place, tokens, gain, grad, grad_hidden, *refs):
    own = refs[:n_own]
    flat = refs[n_own:n_own + 2 * n_pairs]
    pieces = [(flat[2 * k], flat[2 * k + 1]) for k in range(n_pairs)]
    out, local_gain, weight, normed_grad, sem = refs[n_own + 2 * n_pairs:]
    copies = piece_copies(place, own, pieces, 0, weight, sem)
    for copy in copies:
        copy.start()
    for copy in copies:
        copy.wait()
    features = tokens.shape[1]
    wide = features // 2

    @pl.loop(0, 2)
    def _(tile):
        at = pl.ds(pl.multiple_of(tile * wide, 128), wide)
        normed_grad[:, lanes(tile * wide, wide)] = mm_nt(grad[...], weight[at, :])

    value = tokens[...].astype(f32)
    inverse = lax.rsqrt(jnp.mean(value * value, axis=1, keepdims=True) + epsilon)
    grad_normed = normed_grad[...]
    along = grad_normed * value
    local_gain[...] = jnp.sum(along * inverse, axis=0, keepdims=True)
    mean = jnp.mean(along * gain[...], axis=1, keepdims=True)
    out[...] = grad_hidden[...] + inverse * (grad_normed * gain[...]) - value * (inverse * inverse * inverse * mean)


def input_grad_call(place, tokens, gain, grad, grad_hidden, own, pieces):
    rows, features = tokens.shape
    flat = [part for pair in pieces for part in pair]
    shape = jax.ShapeDtypeStruct
    return pl.pallas_call(
        functools.partial(input_grad_kernel, len(own), len(pieces)),
        out_shape=[shape((rows, features), f32), shape((1, features), f32)],
        in_specs=specs("s" + "v" * 4 + "a" * (len(own) + len(flat))),
        out_specs=specs("vv"),
        scratch_shapes=[
            pltpu.VMEM((features, grad.shape[1]), bf16),
            pltpu.VMEM((rows, features), f32),
            pltpu.SemaphoreType.DMA((len(own) + len(flat),)),
        ],
        compiler_params=params(),
        cost_estimate=COST,
        name="input_grad",
    )(place, tokens, gain, grad, grad_hidden, *own, *flat)


def fold_first_kernel(place, keep, got, keep_a, give_a, keep_b, give_b):
    rows, quart = keep_a.shape[1], keep_a.shape[2]
    high, low = lax.div(place[0], 2), lax.rem(place[0], 2)

    def total(high_bit, low_bit, first):
        at = pl.ds(pl.multiple_of((high_bit * 2 + low_bit) * rows, 16), rows)
        cols = slice(first, first + quart)
        return (keep[at, cols].astype(f32) + got[at, cols].astype(f32)).astype(bf16)

    for bit in range(2):
        keep_a[bit] = total(high, bit, 0)
        give_a[bit] = total(1 - high, bit, 0)
        keep_b[bit] = total(bit, low, quart)
        give_b[bit] = total(bit, 1 - low, quart)


def fold_first(place, keep, got, data):
    rows, quart = keep.shape[0] // data, keep.shape[1] // 2
    return pl.pallas_call(
        fold_first_kernel,
        out_shape=[jax.ShapeDtypeStruct((2, rows, quart), bf16)] * 4,
        in_specs=specs("svv"),
        out_specs=specs("vvvv"),
        compiler_params=params(),
        cost_estimate=COST,
        name="fold_first",
    )(place, keep, got)


def fold_second_kernel(place, keep_a, got_a, keep_b, got_b, next_a, give_a, next_b, give_b):
    high, low = lax.div(place[0], 2), lax.rem(place[0], 2)
    for bit, keep, got, kept, give in ((low, keep_a, got_a, next_a, give_a), (high, keep_b, got_b, next_b, give_b)):
        kept[...] = (keep[bit].astype(f32) + got[bit].astype(f32)).astype(bf16)
        give[...] = (keep[1 - bit].astype(f32) + got[1 - bit].astype(f32)).astype(bf16)


def fold_second(place, keep_a, got_a, keep_b, got_b):
    return pl.pallas_call(
        fold_second_kernel,
        out_shape=[jax.ShapeDtypeStruct(keep_a.shape[1:], bf16)] * 4,
        in_specs=specs("svvvv"),
        out_specs=specs("vvvv"),
        compiler_params=params(),
        cost_estimate=COST,
        name="fold_second",
    )(place, keep_a, got_a, keep_b, got_b)


def joined_kernel(place, mine, other, *outs):
    half = mine.shape[1]
    first = 0
    for out in outs:
        done = 0
        while done < out.shape[1]:
            at = first + done
            size = min(out.shape[1] - done, half - at % half)
            cols = slice(at % half, at % half + size)
            own = place[1] == at // half
            out[:, done:done + size] = jnp.where(own, mine[:, cols], other[:, cols]).astype(f32)
            done += size
        first += out.shape[1]


def joined(place, mine, other, widths):
    return pl.pallas_call(
        joined_kernel,
        out_shape=[jax.ShapeDtypeStruct((mine.shape[0], width), f32) for width in widths],
        in_specs=specs("svv"),
        out_specs=specs("v" * len(widths)),
        compiler_params=params(),
        cost_estimate=COST,
        name="joined",
    )(place, mine, other)


def pair_slots(routes, order_row, experts, capacity):
    pair_count = order_row.shape[0]
    place = (
        jnp.zeros((pair_count,), jnp.int32)
        .at[order_row]
        .set(jnp.arange(pair_count, dtype=jnp.int32), unique_indices=True, mode="promise_in_bounds")
        .reshape(routes.shape)
    )
    columns = jnp.arange(experts, dtype=jnp.int32)
    hit = routes[None, :, :] == columns[:, None, None]
    key = jnp.min(jnp.where(hit, place[None], pair_count), axis=2)
    rank = jnp.sum((key[:, None, :] < key[:, :, None]).astype(jnp.int32), axis=2)
    return jnp.where((key < pair_count) & (rank < capacity), rank + 1, 0).T


def body(
    tokens,
    cotangent,
    norm_attn,
    norm_moe,
    w_query,
    key_weight,
    value_weight,
    w_out,
    w_router,
    w_gate,
    w_up,
    w_down,
    document_index,
    padding_token_mask,
    routes,
    pair_order,
):
    token_rows, features = tokens.shape
    top_count = routes.shape[1]
    experts = lax.axis_size("expert")
    data = lax.axis_size("dp")
    chips = experts // 2
    half = chips // 2
    ff = w_gate.shape[2]
    capacity = 9 * token_rows * top_count // (8 * experts)
    slot_rows = (capacity + 15) // 16 * 16
    extra = tail_width(experts)
    query_width = QUERY_HEADS * HEAD_SIZE
    kv_width = KEY_VALUE_HEADS * HEAD_SIZE
    me = lax.axis_index("expert")
    my_dp = lax.axis_index("dp")
    core = lax.rem(me, 2)
    place = jnp.stack([my_dp, core]).astype(jnp.int32)
    hosted = jnp.stack([me, lax.rem(me + experts // 2, experts), my_dp]).astype(jnp.int32)

    def swap(v):
        return lax.ppermute(v, "expert", [(j, j ^ 1) for j in range(experts)])

    def shift(v, k):
        def to(j):
            chip = j // 2
            return ((chip // half) * half + (chip % half + k) % half) * 2 + j % 2

        return lax.ppermute(v, "expert", [(j, to(j)) for j in range(experts)])

    def across(v):
        return lax.ppermute(v, "expert", [(j, (j + experts // 2) % experts) for j in range(experts)])

    def chip_xor(v, step):
        return lax.ppermute(v, "expert", [(j, ((j // 2) ^ step) * 2 + j % 2) for j in range(experts)])

    def dp_xor(v, k):
        return lax.ppermute(v, "dp", [(j, j ^ k) for j in range(data)])

    def core_half(v):
        width = v.shape[1] // 2
        return jnp.where(core == 0, v[:, :width], v[:, width:])

    def after(v, *others):
        return lax.optimization_barrier((v, others))[0]

    def from_dp(v):
        return [dp_xor(v, k) for k in range(1, data)]

    def dp_part(w):
        rows = w.shape[0] // data
        return lax.dynamic_slice_in_dim(w, my_dp * rows, rows, axis=0)

    own = [w_gate[0], w_up[0], w_down[0]]
    quarter = jnp.concatenate(
        [jnp.concatenate([dp_part(own[0]), dp_part(own[1])], axis=1), dp_part(own[2])], axis=0
    )
    part_rows = quarter.shape[0] * 11 // 18
    crossed_one = across(quarter[:part_rows])

    token_half = token_rows // 2
    cot_first = [shift(cotangent[:token_half], k) for k in range(1, half)]

    qkv_own = [w_query, key_weight, value_weight]
    qkv_half = (query_width + 2 * kv_width) // 2
    mine = jnp.concatenate([core_half(jnp.concatenate(qkv_own, axis=1)), core_half(w_out)], axis=1)
    near_one, near_two = dp_xor(mine, 1), dp_xor(mine, 2)
    tall = mine.shape[0] // 2
    got = [near_one, near_two, dp_xor(near_two[:tall], 1), dp_xor(near_one[tall:], 2)]
    slots = pair_slots(routes, pair_order[0], experts, capacity)
    slot_columns = jnp.pad(
        jnp.concatenate([slots // 128, slots % 128], axis=1).astype(f32),
        ((0, 0), (3 * experts, extra - 5 * experts)),
    )
    router_weight = jnp.pad(w_router, ((0, 0), (0, extra - experts)))
    router_weight_three = jnp.pad(jnp.concatenate([w_router] * 3, axis=1), ((0, 0), (0, extra - 3 * experts)))
    gain_one = norm_attn.reshape(1, features)
    gain_two = norm_moe.reshape(1, features)
    segment_columns = document_index.reshape(token_rows, 1)
    ready, gain_one, gain_two, segment_columns = after(
        (got, gain_one, gain_two, segment_columns),
        crossed_one, cot_first, slot_columns, router_weight, router_weight_three,
    )
    pieces = [(v, swap(v)) for v in ready]
    crossed_two = across(after(quarter[part_rows:], crossed_one))
    cot_second = [shift(after(cotangent[token_half:], pieces), k) for k in range(1, half)]
    cot_other = swap(after(cotangent, pieces))
    cot_first_other = [swap(after(v, pieces)) for v in cot_first]
    partner_one = lax.all_gather(after(crossed_one, pieces), "dp", axis=0, tiled=True)

    normed_one, qkv, mixture, totals = attend_call(
        place, tokens, gain_one, document_index, segment_columns, padding_token_mask, qkv_own, pieces
    )
    hidden_one, payload = route_call(
        place, after(mixture, crossed_two, cot_second, cot_other, cot_first_other), tokens, gain_two, router_weight,
        slot_columns, [w_out], pieces, experts,
    )

    payload_other = swap(payload)
    payload_far_same = [shift(payload, k) for k in range(1, half)]
    total_rows = chips // 2 * 2 * slot_rows

    two = after(crossed_two, payload_other)
    partner = [partner_one, two] + from_dp(two)
    spread = tuple((0, d * part_rows, part_rows, (False, d), 0) for d in range(data))
    spread += tuple((1 + k, 0, quarter.shape[0] - part_rows, (True, k), part_rows) for k in range(data))

    def rows_of(slot, sources, weights, prev, saved, base, cost=COST):
        return expert_call(
            hosted, (slot,), sources, weights, prev, saved, base, total_rows, experts, slot_rows, data, spread, cost
        )

    one = [(payload, payload_other, (cotangent,), (cot_other,))]
    near = rows_of(0, one, own, [], [], 0)
    near_saved = near[4:]
    near = rows_of(1, one, partner, near[:4], [], 0, LONG)
    payload_far_other = [swap(after(v, near[0])) for v in payload_far_same]
    cot_second_other = [swap(after(v, near[0])) for v in cot_second]
    many = list(zip(
        payload_far_same, payload_far_other, zip(cot_first, cot_second), zip(cot_first_other, cot_second_other)
    ))
    many = [(same, other, tuple(c_same), tuple(c_other)) for same, other, c_same, c_other in many]
    far = rows_of(1, many, partner, [], near[4:], 2 * slot_rows)
    partner_local = weight_gradient_call(far[4:], data)
    far = rows_of(0, many, own, far[:4], near_saved, 2 * slot_rows)
    saved = far[4:]

    def returned(near_same, near_other, far_same, far_other):
        sums = [
            (far_same[k].astype(f32) + swap(far_other[k]).astype(f32)).astype(bf16)
            for k in range(half - 1)
        ]
        return [near_same[0], swap(near_other[0])], sums

    def scattered(v):
        return lax.psum_scatter(v, "dp", scatter_dimension=0, tiled=True)

    partner_sum = scattered(partner_local)
    backs, back_sums = returned(near[2], near[3], far[2], far[3])
    backs += [shift(v, half - 1 - k) for k, v in enumerate(back_sums)]
    outs, out_sums = returned(near[0], after(near[1], back_sums), far[0], after(far[1], back_sums))
    own_local = weight_gradient_call([after(saved[0], back_sums, out_sums), *saved[1:]], data)
    own_sum = scattered(after(own_local, partner_sum, backs))
    grad_hidden, given, out_keep, out_give, local_norm_moe, local_router = branch_call(
        place, cotangent, hidden_one, payload, gain_two, router_weight_three, mixture, backs,
        [w_out], pieces, experts,
    )

    def chip_sum(part, beside, middle, last):
        sizes = []
        step = 1
        chip = me // 2
        while step < chips:
            size = part.shape[0] // 2
            bit = lax.rem(chip // step, 2)
            keep = lax.dynamic_slice_in_dim(part, bit * size, size, axis=0)
            give = lax.dynamic_slice_in_dim(part, (1 - bit) * size, size, axis=0)
            part = (keep.astype(f32) + chip_xor(beside(give), step).astype(f32)).astype(bf16)
            sizes.append((step, bit))
            step *= 2
        for step, bit in reversed(sizes):
            part = after(beside(part), *middle)
            other = chip_xor(part, step)
            if step == 1:
                other = after(other, *last)
            part = jnp.concatenate(
                [jnp.where(bit == 0, part, other), jnp.where(bit == 0, other, part)], axis=0
            )
        return part

    first_cut, second_cut = partner_sum.shape[0] * 11 // 36, partner_sum.shape[0] * 24 // 36
    thirds = jnp.split(partner_sum, (first_cut, second_cut), axis=0)
    arrived_one = across(after(thirds[0], backs))
    arrived_two = across(after(thirds[1], arrived_one, grad_hidden))
    given, out_give = after((given, out_give), arrived_one)
    cuts = [0, 9 * token_rows // 40, token_rows // 2, token_rows]

    def out_parts(index, *others):
        rows = slice(cuts[index], cuts[index + 1])
        return [shift(after(v[rows], *others), half - 1 - k) for k, v in enumerate(out_sums)]

    outs_one = out_parts(0, backs)
    outs_two = out_parts(1, arrived_one, grad_hidden, outs_one)
    given, out_give = after((given, out_give), outs_one)
    out_got = swap(out_give)
    grad_qkv, qkv_keep, qkv_give = attend_back_call(
        place, document_index, segment_columns, padding_token_mask, qkv, totals, given, normed_one
    )
    qkv_give, out_got = after((qkv_give, out_got), arrived_two, outs_two)
    arrived_three = across(after(thirds[2], arrived_two))
    out_folds = fold_first(place, out_keep, out_got, data)
    out_arrived = [dp_xor(out_folds[1], 2), dp_xor(out_folds[3], 1)]
    qkv_folds = fold_first(place, qkv_keep, swap(qkv_give), data)
    qkv_arrived = [dp_xor(qkv_folds[1], 2), dp_xor(qkv_folds[3], 1)]
    grad_tokens, local_norm_attn = input_grad_call(
        place, tokens, gain_one, after(grad_qkv, qkv_folds, out_folds), grad_hidden, qkv_own, pieces
    )
    qkv_arrived, out_arrived, arrived_three = after((qkv_arrived, out_arrived, arrived_three), grad_tokens)
    outs_three = out_parts(2, arrived_three)
    local_router = local_router[:3 * experts].reshape(3, experts, features).sum(0)
    small = jnp.concatenate([local_router, local_norm_attn, local_norm_moe], axis=0)
    small_steps = [swap] + [functools.partial(dp_xor, k=1 << i) for i in range(data.bit_length() - 1)]
    small_steps += [functools.partial(chip_xor, step=1 << i) for i in range(chips.bit_length() - 1)]

    def beside(large):
        nonlocal small
        large, small = after((large, small))
        if small_steps:
            small = small + small_steps.pop(0)(small)
        return large

    def folded(folds, arrived):
        keep_a, give_a, keep_b, give_b = fold_second(place, folds[0], arrived[0], folds[2], arrived[1])
        got_a, got_b = dp_xor(give_a, 1), dp_xor(give_b, 2)
        return jnp.concatenate([
            (keep.astype(f32) + got.astype(f32)).astype(bf16) for keep, got in ((keep_a, got_a), (keep_b, got_b))
        ], axis=1)

    out_part = folded(out_folds, out_arrived)
    qkv_part = beside(folded(qkv_folds, qkv_arrived))
    arrived_three = after(arrived_three, out_part, qkv_part)
    arrived = jnp.concatenate([arrived_one, arrived_two, arrived_three], axis=0)
    expert_sum = (own_sum.astype(f32) + arrived.astype(f32)).astype(bf16)
    whole = lax.all_gather(expert_sum, "dp", axis=0, tiled=True)
    outs += [jnp.concatenate(v, axis=0) for v in zip(outs_one, outs_two, outs_three)]
    routed = outs[0].astype(f32)
    for part in outs[1:]:
        routed = routed + part.astype(f32)
    block_out = (hidden_one + routed).astype(bf16)
    grad_gate, grad_up, grad_down = widened(whole, data)
    out_part = chip_sum(out_part, lambda v: v, (), ())
    qkv_part = chip_sum(qkv_part, beside, (block_out,), (grad_gate,))
    (grad_out,) = joined(place, out_part, swap(out_part), (features,))
    qkv_part = after(qkv_part, grad_out)
    qkv_other = swap(qkv_part)
    grad_query, grad_key, grad_value = joined(
        place, qkv_part, qkv_other, (query_width, kv_width, kv_width)
    )
    while small_steps:
        small = small + small_steps.pop(0)(small)
    grad_router = small[:experts].T
    grad_norm_attn = small[experts]
    grad_norm_moe = small[experts + 1]
    return (
        block_out,
        grad_tokens,
        grad_norm_attn,
        grad_norm_moe,
        grad_query,
        grad_key,
        grad_value,
        grad_out,
        grad_router,
        grad_gate[None],
        grad_up[None],
        grad_down[None],
    )


def solution(mesh):
    rows = P(("dp", "expert"), None)
    over_dp = P("dp", None)
    over_expert = P("expert", None, None)
    return jax.shard_map(
        body,
        mesh=mesh,
        in_specs=(
            rows, rows, P(), P(), over_dp, over_dp, over_dp, over_dp, P(),
            over_expert, over_expert, over_expert, rows, rows, rows, rows,
        ),
        out_specs=(
            rows, rows, P(), P(), over_dp, over_dp, over_dp, over_dp, P(),
            over_expert, over_expert, over_expert,
        ),
        check_vma=False,
    )
```

```python
import functools

import jax
import jax.numpy as jnp
from jax import lax
from jax.experimental import pallas as pl
from jax.experimental.pallas import tpu as pltpu
from jax.sharding import PartitionSpec as P

bf16 = jnp.bfloat16
f32 = jnp.float32
MIB = 1024 * 1024
LONG = pl.CostEstimate(flops=16 << 30, bytes_accessed=30 * MIB, transcendentals=0)
COST = pl.CostEstimate(flops=1000, bytes_accessed=1000, transcendentals=0)
NT_DIMS = (((1,), (1,)), ((), ()))
TN_DIMS = (((0,), (0,)), ((), ()))


def mm(a, b):
    return jnp.dot(a, b, preferred_element_type=f32)


def mm_nt(a, b):
    return lax.dot_general(a, b, NT_DIMS, preferred_element_type=f32)


def mm_tn(a, b):
    return lax.dot_general(a, b, TN_DIMS, preferred_element_type=f32)


def split_three(v):
    high = v.astype(bf16)
    rest = v - high.astype(f32)
    middle = rest.astype(bf16)
    low = (rest - middle.astype(f32)).astype(bf16)
    return high, middle, low


def lanes(start, size):
    return pl.ds(pl.multiple_of(start, 128), size)


def specs(kinds):
    table = {"s": pltpu.SMEM, "v": pltpu.VMEM, "a": pl.ANY}
    return [pl.BlockSpec(memory_space=table[kind]) for kind in kinds]


def params():
    return pltpu.CompilerParams(vmem_limit_bytes=60 * MIB)


def expert_kernel(experts, slots, base, data, pieces, chunks, cuts, n_weights, n_prev, n_saved, rows, *refs):
    count = len(slots)
    each = 2 + 2 * len(cuts)
    hosted, sources, refs = refs[0], refs[1:1 + each * chunks], refs[1 + each * chunks:]
    sources = [sources[each * i:each * (i + 1)] for i in range(chunks)]
    weight_refs, refs = refs[:n_weights], refs[n_weights:]
    prev, refs = refs[:n_prev], refs[n_prev + n_saved:]
    po_same, po_other, pg_same, pg_other, x_out, gp_out, h_out, gg_out, gu_out = refs[:9]
    (wg, wu, wd, nbuf, cbuf, x, gp, gc, sc, h, gg, gu, dmat, dtmat, gcol, vcol, tail_t,
     w_sem, in_sem, act_sem, p_sem) = refs[9:]
    tokens, features = sources[0][0].shape[0], sources[0][2].shape[1]
    extra = sources[0][0].shape[1] - features
    ff = wg.shape[2]
    wide = features // 2
    tail = slice(features, features + extra)

    weight_copies = []
    taken = 0
    for place, slot in enumerate(slots):
        if slot == 0:
            pairs = list(zip(weight_refs[taken:taken + 3], (wg.at[place], wu.at[place], wd.at[place])))
            taken += 3
        else:
            tall_f, tall_h = features // data, ff // data
            pairs = []
            for index, begin, size, whose, first in pieces:
                ref = weight_refs[taken + index]
                source = jnp.bitwise_xor(hosted[2], whose[1]) if whose[0] else whose[1]
                wide_rows = max(0, min(size, tall_f - first))
                if wide_rows:
                    at = pl.ds(pl.multiple_of(source * tall_f + first, 16), wide_rows)
                    pairs += [
                        (ref.at[pl.ds(begin, wide_rows), pl.ds(0, ff)], wg.at[place, at]),
                        (ref.at[pl.ds(begin, wide_rows), pl.ds(ff, ff)], wu.at[place, at]),
                    ]
                if wide_rows < size:
                    at = pl.ds(pl.multiple_of(source * tall_h + first + wide_rows - tall_f, 16), size - wide_rows)
                    pairs.append((ref.at[pl.ds(begin + wide_rows, size - wide_rows)], wd.at[place, at]))
            taken += 1 + max(piece[0] for piece in pieces)
        weight_copies.append([
            pltpu.make_async_copy(source, target, w_sem.at[place, i])
            for i, (source, target) in enumerate(pairs)
        ])

    def input_copies(index, q):
        pairs = [(sources[index][q], nbuf.at[q])]
        for part, (first, size) in zip(sources[index][2 + q * len(cuts):], cuts):
            pairs.append((part, cbuf.at[q, pl.ds(first, size)]))
        return [pltpu.make_async_copy(source, target, in_sem.at[q, i]) for i, (source, target) in enumerate(pairs)]

    def act_copies(chunk, place):
        at = pl.ds(pl.multiple_of(base + chunk * 2 * rows, 16), 2 * rows)
        return [
            pltpu.make_async_copy(source.at[place], target.at[place, at], act_sem.at[place, i])
            for i, (source, target) in enumerate(
                ((x, x_out), (gp, gp_out), (h, h_out), (gg, gg_out), (gu, gu_out)))
        ]

    def partial_copies(chunk, q):
        return (
            pltpu.make_async_copy(nbuf.at[q], (pg_same, pg_other)[q].at[chunk], p_sem.at[q, 0]),
            pltpu.make_async_copy(cbuf.at[q], (po_same, po_other)[q].at[chunk], p_sem.at[q, 1]),
        )

    def dispatch(q):
        columns = nbuf[q, :, tail].astype(f32)
        tail_t[...] = columns.T
        token_lane = lax.broadcasted_iota(jnp.int32, (tokens, extra), 1)
        wanted = lax.broadcasted_iota(jnp.int32, (tokens, count * rows), 1)
        slot_cols = []
        for place in range(count):
            expert = hosted[slots[place]]
            row = (tail_t[pl.ds(3 * experts + expert, 1), :] * 128.0
                   + tail_t[pl.ds(4 * experts + expert, 1), :] - 1.0).astype(jnp.int32)
            hit = lax.broadcasted_iota(jnp.int32, (rows, tokens), 0) == row
            dmat[q, place * rows:(place + 1) * rows, :] = jnp.where(hit, 1.0, 0.0).astype(bf16)
            factor = jnp.where(token_lane == 3 * experts + expert, 128.0, 0.0)
            factor = jnp.where(token_lane == 4 * experts + expert, 1.0, factor)
            slot_cols.append(jnp.sum(columns * factor, axis=1, keepdims=True).astype(jnp.int32) - 1)
        target = slot_cols[0]
        if count == 2:
            second = wanted >= rows
            target = jnp.where(second, slot_cols[1], slot_cols[0])
            wanted = jnp.where(second, wanted - rows, wanted)
        dtmat[q] = jnp.where(wanted == target, 1.0, 0.0).astype(bf16)
        parts = mm(dmat[q], nbuf[q, :, tail])
        lane = lax.broadcasted_iota(jnp.int32, (rows, extra), 1)
        for place in range(count):
            expert = hosted[slots[place]]
            mine = (lane == expert) | (lane == expert + experts) | (lane == expert + 2 * experts)
            g = jnp.sum(jnp.where(mine, parts[place * rows:(place + 1) * rows], 0.0), axis=1, keepdims=True)
            gcol[place, q * rows:(q + 1) * rows, :] = jnp.broadcast_to(g, (rows, 128))

        for tile in range(2):
            cols = slice(tile * wide, (tile + 1) * wide)
            found = mm(dmat[q], nbuf[q, :, cols]).astype(bf16)
            cot = mm(dmat[q], cbuf[q, :, cols])
            gc[q, :, cols] = cot.astype(bf16)
            for place in range(count):
                at = slice(q * rows, (q + 1) * rows)
                own = slice(place * rows, (place + 1) * rows)
                x[place, at, cols] = found[own]
                gp[place, at, cols] = (cot[own] * gcol[place, at, 0:1]).astype(bf16)

    def forward_backward(place):
        for q in range(2):
            at = slice(q * rows, (q + 1) * rows)
            gate = mm(x[place, at, :], wg[place])
            up = mm(x[place, at, :], wu[place])
            dh = mm_nt(gp[place, at, :], wd[place])
            sig = 1.0 / (1.0 + jnp.exp(-gate))
            act = gate * sig
            h[place, at, :] = (act * up).astype(bf16)
            gg[place, at, :] = (dh * up * (sig * (1.0 + gate * (1.0 - sig)))).astype(bf16)
            gu[place, at, :] = (dh * act).astype(bf16)

    def produce(place):
        vcol[place] = jnp.zeros(vcol.shape[1:], f32)

        @pl.loop(0, 2)
        def _(tile):
            cols = lanes(tile * wide, wide)
            for q in range(2):
                at = slice(q * rows, (q + 1) * rows)
                own = pl.ds(pl.multiple_of(place * rows, 16), rows)
                produced = mm(h[place, at, :], wd[place, :, cols]).astype(bf16).astype(f32)
                along = produced * gc[q, own, cols].astype(f32)
                folded = along[:, :128]
                for part in range(1, wide // 128):
                    folded = folded + along[:, part * 128:(part + 1) * 128]
                vcol[place, at, :] += folded
                sc[q, own, cols] = (produced * gcol[place, at, 0:1]).astype(bf16)
                back = mm_nt(gg[place, at, :], wg[place, cols, :]) + mm_nt(gu[place, at, :], wu[place, cols, :])
                gc[q, own, cols] = back.astype(bf16)

    def combine(q):
        at = slice(q * rows, (q + 1) * rows)
        lane = lax.broadcasted_iota(jnp.int32, (rows, extra), 1)
        payload = []
        for place in range(count):
            expert = hosted[slots[place]]
            high, middle, low = split_three(jnp.sum(vcol[place, at, :], axis=1, keepdims=True))
            part = jnp.where(lane == expert, high.astype(f32), 0.0)
            part = jnp.where(lane == expert + experts, middle.astype(f32), part)
            part = jnp.where(lane == expert + 2 * experts, low.astype(f32), part)
            payload.append(part.astype(bf16))
        payload = jnp.concatenate(payload, axis=0) if count > 1 else payload[0]
        tail_sum = mm(dtmat[q], payload)
        if n_prev:
            tail_sum = tail_sum + nbuf[q, :, tail].astype(f32)
        nbuf[q, :, tail] = tail_sum.astype(bf16)

        for tile in range(2):
            cols = slice(tile * wide, (tile + 1) * wide)
            back = mm(dtmat[q], gc[q, :, cols])
            out = mm(dtmat[q], sc[q, :, cols])
            if n_prev:
                back = back + nbuf[q, :, cols].astype(f32)
                out = out + cbuf[q, :, cols].astype(f32)
            nbuf[q, :, cols] = back.astype(bf16)
            cbuf[q, :, cols] = out.astype(bf16)

    def prev_copies(chunk):
        po0, po1, pg0, pg1 = prev
        return (
            pltpu.make_async_copy(pg0.at[chunk], nbuf.at[0], in_sem.at[0, 0]),
            pltpu.make_async_copy(pg1.at[chunk], nbuf.at[1], in_sem.at[1, 0]),
            pltpu.make_async_copy(po0.at[chunk], cbuf.at[0], in_sem.at[0, 1]),
            pltpu.make_async_copy(po1.at[chunk], cbuf.at[1], in_sem.at[1, 1]),
        )

    for q in range(2):
        for copy in input_copies(0, q):
            copy.start()
    for copies in weight_copies:
        for copy in copies:
            copy.start()

    @pl.loop(0, chunks)
    def _(chunk):
        for q in range(2):
            for copy in input_copies(0, q):
                copy.wait()
            dispatch(q)
        if n_prev:
            for copy in prev_copies(chunk):
                copy.start()
        for place in range(count):
            @pl.when(chunk == 0)
            def _():
                for copy in weight_copies[place]:
                    copy.wait()

            forward_backward(place)
            for copy in act_copies(chunk, place):
                copy.start()
            produce(place)
        if n_prev:
            for copy in prev_copies(chunk):
                copy.wait()
        for q in range(2):
            combine(q)
            for copy in partial_copies(chunk, q):
                copy.start()
        for place in range(count):
            for copy in act_copies(chunk, place):
                copy.wait()
        for q in range(2):
            for copy in partial_copies(chunk, q):
                copy.wait()

        for index in range(1, chunks):
            @pl.when(chunk + 1 == index)
            def _():
                for q in range(2):
                    for copy in input_copies(index, q):
                        copy.start()


def expert_call(hosted, slots, sources, weights, prev, saved, base, total, experts, rows, data, pieces, cost):
    chunks = len(sources)
    tokens, features = sources[0][0].shape[0], sources[0][2][0].shape[1]
    cuts, first = [], 0
    for part in sources[0][2]:
        cuts.append((first, part.shape[0]))
        first += part.shape[0]
    flat = [v for same, other, *parts in sources for v in (same, other, *parts[0], *parts[1])]
    ff = weights[0].shape[1] if slots[0] == 0 else weights[0].shape[1] // 2
    wide_n = sources[0][0].shape[1]
    extra = wide_n - features
    count = len(slots)
    shape = jax.ShapeDtypeStruct
    act_f = shape((count, total, features), bf16)
    act_h = shape((count, total, ff), bf16)
    out_shape = (
        [shape((chunks, tokens, features), bf16)] * 2
        + [shape((chunks, tokens, wide_n), bf16)] * 2
        + [act_f, act_f, act_h, act_h, act_h]
    )
    many = 2 * rows
    first_prev = 1 + len(flat) + len(weights)
    first_saved = first_prev + len(prev)
    return pl.pallas_call(
        functools.partial(
            expert_kernel, experts, slots, base, data, pieces, chunks, tuple(cuts), len(weights), len(prev), len(saved), rows),
        out_shape=out_shape,
        in_specs=specs("s" + "a" * (len(flat) + len(weights) + len(prev) + len(saved))),
        out_specs=specs("a" * 9),
        input_output_aliases={
            **{first_prev + i: i for i in range(len(prev))},
            **{first_saved + i: 4 + i for i in range(len(saved))},
        },
        scratch_shapes=[
            pltpu.VMEM((count, features, ff), bf16),
            pltpu.VMEM((count, features, ff), bf16),
            pltpu.VMEM((count, ff, features), bf16),
            pltpu.VMEM((2, tokens, wide_n), bf16),
            pltpu.VMEM((2, tokens, features), bf16),
            pltpu.VMEM((count, many, features), bf16),
            pltpu.VMEM((count, many, features), bf16),
            pltpu.VMEM((2, count * rows, features), bf16),
            pltpu.VMEM((2, count * rows, features), bf16),
            pltpu.VMEM((count, many, ff), bf16),
            pltpu.VMEM((count, many, ff), bf16),
            pltpu.VMEM((count, many, ff), bf16),
            pltpu.VMEM((2, count * rows, tokens), bf16),
            pltpu.VMEM((2, tokens, count * rows), bf16),
            pltpu.VMEM((count, many, 128), f32),
            pltpu.VMEM((count, many, 128), f32),
            pltpu.VMEM((extra, tokens), f32),
            pltpu.SemaphoreType.DMA((count, 3 * max(1, len(pieces)))),
            pltpu.SemaphoreType.DMA((2, 1 + len(cuts))),
            pltpu.SemaphoreType.DMA((count, 5)),
            pltpu.SemaphoreType.DMA((2, 2)),
        ],
        compiler_params=params(),
        cost_estimate=cost,
        name="expert_rows",
    )(hosted, *flat, *weights, *prev, *saved)


def weight_gradient_kernel(data, x_in, gg_in, gu_in, h_in, gp_in, out, x, ggu, h, gp, wide, down, sem, out_sem):
    features, ff = x.shape[1], h.shape[1]
    tall = 512
    tall_f, tall_h = features // data, ff // data
    step = tall_f + tall_h
    loads = [
        pltpu.make_async_copy(source.at[0], target, sem.at[i])
        for i, (source, target) in enumerate((
            (gg_in, ggu.at[:, pl.ds(0, ff)]), (gu_in, ggu.at[:, pl.ds(ff, ff)]), (x_in, x), (h_in, h), (gp_in, gp)))
    ]
    for copy in loads:
        copy.start()
    stores = [
        pltpu.make_async_copy(wide.at[pl.ds(d * tall_f, tall_f)], out.at[pl.ds(d * step, tall_f)], out_sem.at[2 * d])
        for d in range(data)
    ] + [
        pltpu.make_async_copy(down.at[pl.ds(d * tall_h, tall_h)], out.at[pl.ds(d * step + tall_f, tall_h)],
                              out_sem.at[2 * d + 1])
        for d in range(data)
    ]
    for copy in loads[:3]:
        copy.wait()

    @pl.loop(0, features // tall)
    def _(tile):
        at = pl.ds(pl.multiple_of(tile * tall, tall), tall)
        wide[at, :] = mm_tn(x[:, lanes(tile * tall, tall)], ggu[...]).astype(bf16)

    for copy in stores[:data]:
        copy.start()
    for copy in loads[3:]:
        copy.wait()

    @pl.loop(0, ff // (tall // 2))
    def _(tile):
        at = pl.ds(pl.multiple_of(tile * 256, 256), 256)
        down[at, :] = mm_tn(h[:, lanes(tile * 256, 256)], gp[...]).astype(bf16)

    for copy in stores[data:]:
        copy.start()
    for copy in stores:
        copy.wait()


def weight_gradient_call(saved, data):
    x, gp, h, gg, gu = saved
    slots, features, ff = x.shape[1], x.shape[2], h.shape[2]
    return pl.pallas_call(
        functools.partial(weight_gradient_kernel, data),
        out_shape=jax.ShapeDtypeStruct((features + ff, 2 * ff), bf16),
        in_specs=specs("aaaaa"),
        out_specs=pl.BlockSpec(memory_space=pl.ANY),
        scratch_shapes=[
            pltpu.VMEM((slots, features), bf16),
            pltpu.VMEM((slots, 2 * ff), bf16),
            pltpu.VMEM((slots, ff), bf16),
            pltpu.VMEM((slots, features), bf16),
            pltpu.VMEM((features, 2 * ff), bf16),
            pltpu.VMEM((ff, features), bf16),
            pltpu.SemaphoreType.DMA((5,)),
            pltpu.SemaphoreType.DMA((2 * data,)),
        ],
        compiler_params=params(),
        cost_estimate=COST,
        name="expert_weight_gradients",
    )(x, gg, gu, h, gp)


def widened_kernel(whole, gate, up, down):
    tall, ff = gate.shape
    gate[...] = whole[:tall, :ff].astype(f32)
    up[...] = whole[:tall, ff:].astype(f32)
    down[...] = whole[tall:, :].astype(f32)


def widened(whole, data):
    rows, features = whole.shape[0] // data, whole.shape[1]
    ff = features // 2
    tall = rows * 2 // 3
    blocks = [(tall, ff), (tall, ff), (rows - tall, features)]
    return pl.pallas_call(
        widened_kernel,
        grid=(data,),
        in_specs=[pl.BlockSpec((rows, features), lambda d: (d, 0))],
        out_specs=[pl.BlockSpec(block, lambda d: (d, 0)) for block in blocks],
        out_shape=[jax.ShapeDtypeStruct((data * block[0], block[1]), f32) for block in blocks],
        compiler_params=params(),
        cost_estimate=COST,
        name="widened",
    )(whole)


epsilon = 1e-06
neg_fill = -1e30
QUERY_HEADS = 12
KEY_VALUE_HEADS = 2
HEAD_SIZE = 128
GROUP = QUERY_HEADS // KEY_VALUE_HEADS
SCORE_SCALE = HEAD_SIZE ** (-0.5)


def piece_copies(place, own, pieces, begin, weight, sem):
    rows, half = own[0].shape[0], weight.shape[1] // 2
    mine, core = place[0], place[1]
    copies = []
    column = 0
    for part in own:
        at = weight.at[pl.ds(pl.multiple_of(mine * rows, 16), rows), pl.ds(column, part.shape[1])]
        copies.append(pltpu.make_async_copy(part, at, sem.at[len(copies)]))
        column += part.shape[1]
    for (k, skip), pair in zip(((1, 0), (2, 0), (3, 0), (3, rows // 2)), pieces):
        first = pl.multiple_of(jnp.bitwise_xor(mine, k) * rows + skip, 16)
        for part, which in zip(pair, (core, 1 - core)):
            at = weight.at[pl.ds(first, part.shape[0]), lanes(which * half, half)]
            copies.append(pltpu.make_async_copy(part.at[:, pl.ds(begin, half)], at, sem.at[len(copies)]))
    return copies


def attention_mask(segment_row, segment_col, pad_row, first, size, span):
    row = first + lax.broadcasted_iota(jnp.int32, (size, span), 0)
    col = lax.broadcasted_iota(jnp.int32, (size, span), 1)
    same = segment_col[first:first + size, :] == segment_row[:, :span]
    return same & (((pad_row[:, :span] == 1) & (col < row)) | (col == row))


def stacked(ref, rows, c):
    return jnp.concatenate(
        [ref[rows, lanes((c * GROUP + g) * HEAD_SIZE, HEAD_SIZE)] for g in range(GROUP)], axis=0
    )


def attend_kernel(
    n_own, n_pairs, tokens_total, block,
    place, tokens, gain, segment_row, segment_col, pad_row, *refs,
):
    own = refs[:n_own]
    flat = refs[n_own:n_own + 2 * n_pairs]
    pieces = [(flat[2 * k], flat[2 * k + 1]) for k in range(n_pairs)]
    normed, qkv, mixture, totals, weight, sem = refs[n_own + 2 * n_pairs:]
    copies = piece_copies(place, own, pieces, 0, weight, sem)
    for copy in copies:
        copy.start()
    width = QUERY_HEADS * HEAD_SIZE
    kv_width = KEY_VALUE_HEADS * HEAD_SIZE
    source = tokens[...].astype(f32)
    inverse = lax.rsqrt(jnp.mean(source * source, axis=1, keepdims=True) + epsilon)
    normed[...] = (source * inverse * gain[...]).astype(bf16)
    for copy in copies:
        copy.wait()
    wide = 512

    @pl.loop(0, qkv.shape[1] // wide)
    def _(tile):
        cols = lanes(tile * wide, wide)
        qkv[:, cols] = mm(normed[...], weight[:, cols]).astype(bf16)

    totals[...] = jnp.zeros_like(totals)
    segment_of_row, segment_of_col, pad = segment_row[...], segment_col[...], pad_row[...]

    @pl.loop(0, KEY_VALUE_HEADS)
    def _(c):
        for first in range(0, tokens_total, block):
            span = first + block
            rows = slice(first, span)
            mask = attention_mask(segment_of_row, segment_of_col, pad, first, block, span)
            keys = qkv[:span, lanes(width + c * HEAD_SIZE, HEAD_SIZE)]
            values = qkv[:span, lanes(width + kv_width + c * HEAD_SIZE, HEAD_SIZE)]
            scores = mm_nt(stacked(qkv, rows, c), keys) * SCORE_SCALE
            lane = lax.broadcasted_iota(jnp.int32, (block, 128), 1)
            stats = totals[rows, :]
            weights = []
            for g in range(GROUP):
                part = jnp.where(mask, scores[g * block:(g + 1) * block], neg_fill)
                top = jnp.max(part, axis=1, keepdims=True)
                raised = jnp.exp(part - top)
                total = jnp.sum(raised, axis=1, keepdims=True)
                stats = jnp.where(lane == c * GROUP + g, top + jnp.log(total), stats)
                weights.append((raised * (1.0 / total)).astype(bf16))
            totals[rows, :] = stats
            mixed = mm(jnp.concatenate(weights, axis=0), values).astype(bf16)
            for g in range(GROUP):
                mixture[rows, lanes((c * GROUP + g) * HEAD_SIZE, HEAD_SIZE)] = mixed[g * block:(g + 1) * block]


def attend_call(place, tokens, gain, segments, segment_columns, pads, own, pieces):
    rows, features = tokens.shape
    width = (QUERY_HEADS + 2 * KEY_VALUE_HEADS) * HEAD_SIZE
    mixed = QUERY_HEADS * HEAD_SIZE
    flat = [part for pair in pieces for part in pair]
    shape = jax.ShapeDtypeStruct
    return pl.pallas_call(
        functools.partial(attend_kernel, len(own), len(pieces), rows, 128),
        out_shape=[
            shape((rows, features), bf16), shape((rows, width), bf16), shape((rows, mixed), bf16),
            shape((rows, 128), f32),
        ],
        in_specs=specs("s" + "v" * 5 + "a" * (len(own) + len(flat))),
        out_specs=specs("vvvv"),
        scratch_shapes=[
            pltpu.VMEM((features, width), bf16),
            pltpu.SemaphoreType.DMA((len(own) + len(flat),)),
        ],
        compiler_params=params(),
        cost_estimate=COST,
        name="attend",
    )(place, tokens, gain, segments, segment_columns, pads, *own, *flat)


def attend_back_kernel(tokens_total, block, place, segment_row, segment_col, pad_row, qkv, totals, given, normed_in,
                       grad_out, keep_out, give_out, grad_keys, grad_values, normed, grad, keep, give, sem, out_sem):
    width = QUERY_HEADS * HEAD_SIZE
    kv_width = KEY_VALUE_HEADS * HEAD_SIZE
    segment_of_row, segment_of_col, pad = segment_row[...], segment_col[...], pad_row[...]
    normed_load = pltpu.make_async_copy(normed_in, normed, sem)
    normed_load.start()

    @pl.loop(0, KEY_VALUE_HEADS)
    def _(c):
        grad_keys[...] = jnp.zeros_like(grad_keys)
        grad_values[...] = jnp.zeros_like(grad_values)
        for first in range(0, tokens_total, block):
            span = first + block
            rows = slice(first, span)
            mask = attention_mask(segment_of_row, segment_of_col, pad, first, block, span)
            keys = qkv[:span, lanes(width + c * HEAD_SIZE, HEAD_SIZE)]
            values = qkv[:span, lanes(width + kv_width + c * HEAD_SIZE, HEAD_SIZE)]
            queries = stacked(qkv, rows, c)
            arrived = stacked(given, rows, c)
            scores = mm_nt(queries, keys) * SCORE_SCALE
            grad_weights = mm_nt(arrived, values)
            lane = lax.broadcasted_iota(jnp.int32, (block, 128), 1)
            stats = totals[rows, :]
            weights, grad_scores = [], []
            for g in range(GROUP):
                at = slice(g * block, (g + 1) * block)
                total = jnp.sum(jnp.where(lane == c * GROUP + g, stats, 0.0), axis=1, keepdims=True)
                probs = jnp.exp(jnp.where(mask, scores[at], neg_fill) - total)
                weights.append(probs.astype(bf16))
                dw = grad_weights[at]
                mean = jnp.sum(probs * dw, axis=1, keepdims=True)
                grad_scores.append((probs * (dw - mean)).astype(bf16))
            weights = jnp.concatenate(weights, axis=0)
            grad_scores = jnp.concatenate(grad_scores, axis=0)
            grad_queries = (mm(grad_scores, keys) * SCORE_SCALE).astype(bf16)
            for g in range(GROUP):
                grad[rows, lanes((c * GROUP + g) * HEAD_SIZE, HEAD_SIZE)] = grad_queries[g * block:(g + 1) * block]
            grad_keys[:span, :] += mm_tn(grad_scores, queries)
            grad_values[:span, :] += mm_tn(weights, arrived)
        grad[:, lanes(width + c * HEAD_SIZE, HEAD_SIZE)] = (grad_keys[...] * SCORE_SCALE).astype(bf16)
        grad[:, lanes(width + kv_width + c * HEAD_SIZE, HEAD_SIZE)] = grad_values[...].astype(bf16)

    grad_store = pltpu.make_async_copy(grad, grad_out, out_sem.at[0])
    grad_store.start()
    normed_load.wait()
    tall = 256

    def stores(tile):
        at = pl.ds(pl.multiple_of(tile * tall, tall), tall)
        return (
            pltpu.make_async_copy(keep.at[at], keep_out.at[at], out_sem.at[1 + 2 * tile]),
            pltpu.make_async_copy(give.at[at], give_out.at[at], out_sem.at[2 + 2 * tile]),
        )

    @pl.loop(0, normed.shape[1] // tall)
    def _(tile):
        cols = lanes(tile * tall, tall)
        at = pl.ds(pl.multiple_of(tile * tall, tall), tall)
        for core, out in ((place[1], keep), (1 - place[1], give)):
            out[at, :] = mm_tn(normed[:, cols], grad[:, lanes(core * keep.shape[1], keep.shape[1])]).astype(bf16)
        for copy in stores(tile):
            copy.start()

    grad_store.wait()

    @pl.loop(0, normed.shape[1] // tall)
    def _(tile):
        for copy in stores(tile):
            copy.wait()


def attend_back_call(place, segments, segment_columns, pads, qkv, totals, given, normed):
    rows, width = qkv.shape
    features = normed.shape[1]
    shape = jax.ShapeDtypeStruct
    return pl.pallas_call(
        functools.partial(attend_back_kernel, rows, 128),
        out_shape=[shape((rows, width), bf16)] + [shape((features, width // 2), bf16)] * 2,
        in_specs=specs("s" + "v" * 6 + "a"),
        out_specs=specs("aaa"),
        scratch_shapes=[
            pltpu.VMEM((rows, HEAD_SIZE), f32),
            pltpu.VMEM((rows, HEAD_SIZE), f32),
            pltpu.VMEM((rows, features), bf16),
            pltpu.VMEM((rows, width), bf16),
            pltpu.VMEM((features, width // 2), bf16),
            pltpu.VMEM((features, width // 2), bf16),
            pltpu.SemaphoreType.DMA,
            pltpu.SemaphoreType.DMA((1 + 2 * (features // 256),)),
        ],
        compiler_params=params(),
        cost_estimate=COST,
        name="attend_back",
    )(place, segments, segment_columns, pads, qkv, totals, given, normed)


def route_kernel(experts, n_own, n_pairs, place, mixture, tokens, gain, router_weight, slots, *refs):
    own = refs[:n_own]
    flat = refs[n_own:n_own + 2 * n_pairs]
    pieces = [(flat[2 * k], flat[2 * k + 1]) for k in range(n_pairs)]
    hidden, payload, weight, sem = refs[n_own + 2 * n_pairs:]
    copies = piece_copies(place, own, pieces, (QUERY_HEADS + 2 * KEY_VALUE_HEADS) * HEAD_SIZE // 2, weight, sem)
    for copy in copies:
        copy.start()
    for copy in copies:
        copy.wait()
    features = tokens.shape[1]
    wide = features // 2

    @pl.loop(0, 2)
    def _(tile):
        cols = lanes(tile * wide, wide)
        hidden[:, cols] = tokens[:, cols].astype(f32) + mm(mixture[...], weight[:, cols])

    value = hidden[...]
    inverse = lax.rsqrt(jnp.mean(value * value, axis=1, keepdims=True) + epsilon)
    payload[:, :features] = (value * inverse * gain[...]).astype(bf16)
    extra = payload.shape[1] - features
    logits = mm(payload[:, :features], router_weight[...])
    lane = lax.broadcasted_iota(jnp.int32, logits.shape, 1)
    logits = jnp.where(lane < experts, logits, neg_fill)
    raised = jnp.exp(logits - jnp.max(logits, axis=1, keepdims=True))
    router = raised / jnp.sum(raised, axis=1, keepdims=True)
    high, middle, low = split_three(router)
    tail = high.astype(f32)
    tail = tail + pltpu.roll(middle.astype(f32), experts, 1)
    tail = tail + pltpu.roll(low.astype(f32), 2 * experts, 1)
    payload[:, features:] = (tail + slots[...]).astype(bf16)


def tail_width(experts):
    return (5 * experts + 127) // 128 * 128


def route_call(place, mixture, tokens, gain, router_weight, slots, own, pieces, experts):
    rows, features = tokens.shape
    extra = tail_width(experts)
    flat = [part for pair in pieces for part in pair]
    shape = jax.ShapeDtypeStruct
    return pl.pallas_call(
        functools.partial(route_kernel, experts, len(own), len(pieces)),
        out_shape=[shape((rows, features), f32), shape((rows, features + extra), bf16)],
        in_specs=specs("s" + "v" * 5 + "a" * (len(own) + len(flat))),
        out_specs=specs("vv"),
        scratch_shapes=[
            pltpu.VMEM((mixture.shape[1], features), bf16),
            pltpu.SemaphoreType.DMA((len(own) + len(flat),)),
        ],
        compiler_params=params(),
        cost_estimate=COST,
        name="route",
    )(place, mixture, tokens, gain, router_weight, slots, *own, *flat)


def branch_kernel(experts, n_back, n_own, n_pairs, place, gain, router_weight, cotangent, hidden, payload, mixture_in, *refs):
    backs, refs = refs[:n_back], refs[n_back:]
    own = refs[:n_own]
    flat = refs[n_own:n_own + 2 * n_pairs]
    pieces = [(flat[2 * k], flat[2 * k + 1]) for k in range(n_pairs)]
    grad_hidden, given, keep_out, give_out, local_gain, local_router = refs[n_own + 2 * n_pairs:][:6]
    (weight, branch, mixture, cot_buf, hidden_buf, payload_buf, back_buf, keep, give, given_buf,
     sem, mix_sem, in_sem, out_sem, sum_sem) = refs[n_own + 2 * n_pairs + 6:]
    parts, short = cot_buf.shape[0], cot_buf.shape[1]
    features = cot_buf.shape[2]
    extra = payload_buf.shape[2] - features
    wide_rows = mixture.shape[1]

    def loads(part):
        at = pl.ds(pl.multiple_of(part * short, 16), short)
        pairs = [(ref, back_buf.at[part, i]) for i, ref in enumerate(backs)]
        pairs += [(hidden, hidden_buf.at[part]), (payload, payload_buf.at[part]), (cotangent, cot_buf.at[part])]
        return [
            pltpu.make_async_copy(source.at[at], target, in_sem.at[part, i]) for i, (source, target) in enumerate(pairs)
        ]

    def hidden_store(part):
        at = pl.ds(pl.multiple_of(part * short, 16), short)
        return pltpu.make_async_copy(hidden_buf.at[part], grad_hidden.at[at], out_sem.at[part])

    for part in range(parts):
        for copy in loads(part):
            copy.start()
    mixture_load = pltpu.make_async_copy(mixture_in, mixture, mix_sem)
    mixture_load.start()
    copies = piece_copies(place, own, pieces, (QUERY_HEADS + 2 * KEY_VALUE_HEADS) * HEAD_SIZE // 2, weight, sem)
    for copy in copies:
        copy.start()
    local_gain[...] = jnp.zeros_like(local_gain)
    local_router[...] = jnp.zeros_like(local_router)

    def three(value):
        width = value.shape[1]
        return (value + pltpu.roll(value, width - experts, 1)
                + pltpu.roll(value, width - 2 * experts, 1))

    @pl.loop(0, parts)
    def _(part):
        for copy in loads(part):
            copy.wait()

        def arrived(cols):
            total = back_buf[part, 0, :, cols].astype(f32)
            for i in range(1, n_back):
                total = total + back_buf[part, i, :, cols].astype(f32)
            return total

        lane = lax.broadcasted_iota(jnp.int32, (short, extra), 1)
        router = jnp.where(lane < experts, three(payload_buf[part, :, features:].astype(f32)), 0.0)
        select = jnp.where(lane < experts, three(arrived(slice(features, features + extra))), 0.0)
        logits = router * (select - jnp.sum(router * select, axis=1, keepdims=True))
        high, middle, low = split_three(logits)
        packed = high.astype(f32) + pltpu.roll(middle.astype(f32), experts, 1)
        packed = (packed + pltpu.roll(low.astype(f32), 2 * experts, 1)).astype(bf16)
        grad_normed = arrived(slice(0, features)) + mm_nt(packed, router_weight[...])
        local_router[...] += mm_tn(packed, payload_buf[part, :, :features])
        value = hidden_buf[part]
        inverse = lax.rsqrt(jnp.mean(value * value, axis=1, keepdims=True) + epsilon)
        along = grad_normed * value
        local_gain[...] += jnp.sum(along * inverse, axis=0, keepdims=True)
        mean = jnp.mean(along * gain[...], axis=1, keepdims=True)
        total = (cot_buf[part].astype(f32) + inverse * (grad_normed * gain[...])
                 - value * (inverse * inverse * inverse * mean))
        hidden_buf[part] = total
        branch[pl.ds(pl.multiple_of(part * short, 16), short), :] = total.astype(bf16)
        hidden_store(part).start()

    mixture_load.wait()
    tall = 256

    def sum_stores(tile):
        at = pl.ds(pl.multiple_of(tile * tall, tall), tall)
        return (
            pltpu.make_async_copy(keep.at[at], keep_out.at[at], sum_sem.at[tile, 0]),
            pltpu.make_async_copy(give.at[at], give_out.at[at], sum_sem.at[tile, 1]),
        )

    @pl.loop(0, wide_rows // tall)
    def _(tile):
        cols = lanes(tile * tall, tall)
        at = pl.ds(pl.multiple_of(tile * tall, tall), tall)
        for core, out in ((place[1], keep), (1 - place[1], give)):
            out[at, :] = mm_tn(mixture[:, cols], branch[:, lanes(core * keep.shape[1], keep.shape[1])]).astype(bf16)
        for copy in sum_stores(tile):
            copy.start()

    for copy in copies:
        copy.wait()
    wide = wide_rows // 2

    def given_store(tile):
        cols = lanes(tile * wide, wide)
        return pltpu.make_async_copy(given_buf.at[:, cols], given.at[:, cols], out_sem.at[parts + tile])

    @pl.loop(0, 2)
    def _(tile):
        at = pl.ds(pl.multiple_of(tile * wide, 128), wide)
        given_buf[:, lanes(tile * wide, wide)] = mm_nt(branch[...], weight[at, :]).astype(bf16)
        given_store(tile).start()

    for part in range(parts):
        hidden_store(part).wait()

    @pl.loop(0, wide_rows // tall)
    def _(tile):
        for copy in sum_stores(tile):
            copy.wait()

    for tile in range(2):
        given_store(tile).wait()


def branch_call(place, cotangent, hidden, payload, gain, router_weight, mixture, backs, own, pieces, experts):
    rows, features = cotangent.shape
    wide_n = payload.shape[1]
    mixed = mixture.shape[1]
    parts = 4
    short = rows // parts
    flat = [part for pair in pieces for part in pair]
    shape = jax.ShapeDtypeStruct
    return pl.pallas_call(
        functools.partial(branch_kernel, experts, len(backs), len(own), len(pieces)),
        out_shape=[
            shape((rows, features), f32), shape((rows, mixed), bf16), shape((mixed, features // 2), bf16),
            shape((mixed, features // 2), bf16), shape((1, features), f32), shape((wide_n - features, features), f32),
        ],
        in_specs=specs("svv" + "a" * (4 + len(backs) + len(own) + len(flat))),
        out_specs=specs("aaaavv"),
        scratch_shapes=[
            pltpu.VMEM((mixed, features), bf16),
            pltpu.VMEM((rows, features), bf16),
            pltpu.VMEM((rows, mixed), bf16),
            pltpu.VMEM((parts, short, features), bf16),
            pltpu.VMEM((parts, short, features), f32),
            pltpu.VMEM((parts, short, wide_n), bf16),
            pltpu.VMEM((parts, len(backs), short, wide_n), bf16),
            pltpu.VMEM((mixed, features // 2), bf16),
            pltpu.VMEM((mixed, features // 2), bf16),
            pltpu.VMEM((rows, mixed), bf16),
            pltpu.SemaphoreType.DMA((len(own) + len(flat),)),
            pltpu.SemaphoreType.DMA,
            pltpu.SemaphoreType.DMA((parts, len(backs) + 3)),
            pltpu.SemaphoreType.DMA((parts + 2,)),
            pltpu.SemaphoreType.DMA((mixed // 256, 2)),
        ],
        compiler_params=params(),
        cost_estimate=COST,
        name="branch",
    )(place, gain, router_weight, cotangent, hidden, payload, mixture, *backs, *own, *flat)


def input_grad_kernel(n_own, n_pairs, place, tokens, gain, grad, grad_hidden, *refs):
    own = refs[:n_own]
    flat = refs[n_own:n_own + 2 * n_pairs]
    pieces = [(flat[2 * k], flat[2 * k + 1]) for k in range(n_pairs)]
    out, local_gain, weight, normed_grad, sem = refs[n_own + 2 * n_pairs:]
    copies = piece_copies(place, own, pieces, 0, weight, sem)
    for copy in copies:
        copy.start()
    for copy in copies:
        copy.wait()
    features = tokens.shape[1]
    wide = features // 2

    @pl.loop(0, 2)
    def _(tile):
        at = pl.ds(pl.multiple_of(tile * wide, 128), wide)
        normed_grad[:, lanes(tile * wide, wide)] = mm_nt(grad[...], weight[at, :])

    value = tokens[...].astype(f32)
    inverse = lax.rsqrt(jnp.mean(value * value, axis=1, keepdims=True) + epsilon)
    grad_normed = normed_grad[...]
    along = grad_normed * value
    local_gain[...] = jnp.sum(along * inverse, axis=0, keepdims=True)
    mean = jnp.mean(along * gain[...], axis=1, keepdims=True)
    out[...] = grad_hidden[...] + inverse * (grad_normed * gain[...]) - value * (inverse * inverse * inverse * mean)


def input_grad_call(place, tokens, gain, grad, grad_hidden, own, pieces):
    rows, features = tokens.shape
    flat = [part for pair in pieces for part in pair]
    shape = jax.ShapeDtypeStruct
    return pl.pallas_call(
        functools.partial(input_grad_kernel, len(own), len(pieces)),
        out_shape=[shape((rows, features), f32), shape((1, features), f32)],
        in_specs=specs("s" + "v" * 4 + "a" * (len(own) + len(flat))),
        out_specs=specs("vv"),
        scratch_shapes=[
            pltpu.VMEM((features, grad.shape[1]), bf16),
            pltpu.VMEM((rows, features), f32),
            pltpu.SemaphoreType.DMA((len(own) + len(flat),)),
        ],
        compiler_params=params(),
        cost_estimate=COST,
        name="input_grad",
    )(place, tokens, gain, grad, grad_hidden, *own, *flat)


def fold_first_kernel(place, keep, got, keep_a, give_a, keep_b, give_b):
    rows, quart = keep_a.shape[1], keep_a.shape[2]
    high, low = lax.div(place[0], 2), lax.rem(place[0], 2)

    def total(high_bit, low_bit, first):
        at = pl.ds(pl.multiple_of((high_bit * 2 + low_bit) * rows, 16), rows)
        cols = slice(first, first + quart)
        return (keep[at, cols].astype(f32) + got[at, cols].astype(f32)).astype(bf16)

    for bit in range(2):
        keep_a[bit] = total(high, bit, 0)
        give_a[bit] = total(1 - high, bit, 0)
        keep_b[bit] = total(bit, low, quart)
        give_b[bit] = total(bit, 1 - low, quart)


def fold_first(place, keep, got, data):
    rows, quart = keep.shape[0] // data, keep.shape[1] // 2
    return pl.pallas_call(
        fold_first_kernel,
        out_shape=[jax.ShapeDtypeStruct((2, rows, quart), bf16)] * 4,
        in_specs=specs("svv"),
        out_specs=specs("vvvv"),
        compiler_params=params(),
        cost_estimate=COST,
        name="fold_first",
    )(place, keep, got)


def fold_second_kernel(place, keep_a, got_a, keep_b, got_b, next_a, give_a, next_b, give_b):
    high, low = lax.div(place[0], 2), lax.rem(place[0], 2)
    for bit, keep, got, kept, give in ((low, keep_a, got_a, next_a, give_a), (high, keep_b, got_b, next_b, give_b)):
        kept[...] = (keep[bit].astype(f32) + got[bit].astype(f32)).astype(bf16)
        give[...] = (keep[1 - bit].astype(f32) + got[1 - bit].astype(f32)).astype(bf16)


def fold_second(place, keep_a, got_a, keep_b, got_b):
    return pl.pallas_call(
        fold_second_kernel,
        out_shape=[jax.ShapeDtypeStruct(keep_a.shape[1:], bf16)] * 4,
        in_specs=specs("svvvv"),
        out_specs=specs("vvvv"),
        compiler_params=params(),
        cost_estimate=COST,
        name="fold_second",
    )(place, keep_a, got_a, keep_b, got_b)


def joined_kernel(place, mine, other, *outs):
    half = mine.shape[1]
    first = 0
    for out in outs:
        done = 0
        while done < out.shape[1]:
            at = first + done
            size = min(out.shape[1] - done, half - at % half)
            cols = slice(at % half, at % half + size)
            own = place[1] == at // half
            out[:, done:done + size] = jnp.where(own, mine[:, cols], other[:, cols]).astype(f32)
            done += size
        first += out.shape[1]


def joined(place, mine, other, widths):
    return pl.pallas_call(
        joined_kernel,
        out_shape=[jax.ShapeDtypeStruct((mine.shape[0], width), f32) for width in widths],
        in_specs=specs("svv"),
        out_specs=specs("v" * len(widths)),
        compiler_params=params(),
        cost_estimate=COST,
        name="joined",
    )(place, mine, other)


def pair_slots(routes, order_row, experts, capacity):
    pair_count = order_row.shape[0]
    place = (
        jnp.zeros((pair_count,), jnp.int32)
        .at[order_row]
        .set(jnp.arange(pair_count, dtype=jnp.int32), unique_indices=True, mode="promise_in_bounds")
        .reshape(routes.shape)
    )
    columns = jnp.arange(experts, dtype=jnp.int32)
    hit = routes[None, :, :] == columns[:, None, None]
    key = jnp.min(jnp.where(hit, place[None], pair_count), axis=2)
    rank = jnp.sum((key[:, None, :] < key[:, :, None]).astype(jnp.int32), axis=2)
    return jnp.where((key < pair_count) & (rank < capacity), rank + 1, 0).T


def body(
    tokens,
    cotangent,
    norm_attn,
    norm_moe,
    w_query,
    key_weight,
    value_weight,
    w_out,
    w_router,
    w_gate,
    w_up,
    w_down,
    document_index,
    padding_token_mask,
    routes,
    pair_order,
):
    token_rows, features = tokens.shape
    top_count = routes.shape[1]
    experts = lax.axis_size("expert")
    data = lax.axis_size("dp")
    chips = experts // 2
    half = chips // 2
    ff = w_gate.shape[2]
    capacity = 9 * token_rows * top_count // (8 * experts)
    slot_rows = (capacity + 15) // 16 * 16
    extra = tail_width(experts)
    query_width = QUERY_HEADS * HEAD_SIZE
    kv_width = KEY_VALUE_HEADS * HEAD_SIZE
    me = lax.axis_index("expert")
    my_dp = lax.axis_index("dp")
    core = lax.rem(me, 2)
    place = jnp.stack([my_dp, core]).astype(jnp.int32)
    hosted = jnp.stack([me, lax.rem(me + experts // 2, experts), my_dp]).astype(jnp.int32)

    def swap(v):
        return lax.ppermute(v, "expert", [(j, j ^ 1) for j in range(experts)])

    def shift(v, k):
        def to(j):
            chip = j // 2
            return ((chip // half) * half + (chip % half + k) % half) * 2 + j % 2

        return lax.ppermute(v, "expert", [(j, to(j)) for j in range(experts)])

    def across(v):
        return lax.ppermute(v, "expert", [(j, (j + experts // 2) % experts) for j in range(experts)])

    def chip_xor(v, step):
        return lax.ppermute(v, "expert", [(j, ((j // 2) ^ step) * 2 + j % 2) for j in range(experts)])

    def dp_xor(v, k):
        return lax.ppermute(v, "dp", [(j, j ^ k) for j in range(data)])

    def core_half(v):
        width = v.shape[1] // 2
        return jnp.where(core == 0, v[:, :width], v[:, width:])

    def after(v, *others):
        return lax.optimization_barrier((v, others))[0]

    def from_dp(v):
        return [dp_xor(v, k) for k in range(1, data)]

    def dp_part(w):
        rows = w.shape[0] // data
        return lax.dynamic_slice_in_dim(w, my_dp * rows, rows, axis=0)

    own = [w_gate[0], w_up[0], w_down[0]]
    quarter = jnp.concatenate(
        [jnp.concatenate([dp_part(own[0]), dp_part(own[1])], axis=1), dp_part(own[2])], axis=0
    )
    part_rows = quarter.shape[0] * 11 // 18
    crossed_one = across(quarter[:part_rows])

    token_half = token_rows // 2
    cot_first = [shift(cotangent[:token_half], k) for k in range(1, half)]

    qkv_own = [w_query, key_weight, value_weight]
    qkv_half = (query_width + 2 * kv_width) // 2
    mine = jnp.concatenate([core_half(jnp.concatenate(qkv_own, axis=1)), core_half(w_out)], axis=1)
    near_one, near_two = dp_xor(mine, 1), dp_xor(mine, 2)
    tall = mine.shape[0] // 2
    got = [near_one, near_two, dp_xor(near_two[:tall], 1), dp_xor(near_one[tall:], 2)]
    slots = pair_slots(routes, pair_order[0], experts, capacity)
    slot_columns = jnp.pad(
        jnp.concatenate([slots // 128, slots % 128], axis=1).astype(f32),
        ((0, 0), (3 * experts, extra - 5 * experts)),
    )
    router_weight = jnp.pad(w_router, ((0, 0), (0, extra - experts)))
    router_weight_three = jnp.pad(jnp.concatenate([w_router] * 3, axis=1), ((0, 0), (0, extra - 3 * experts)))
    gain_one = norm_attn.reshape(1, features)
    gain_two = norm_moe.reshape(1, features)
    segment_columns = document_index.reshape(token_rows, 1)
    quarter_rest, cot_rest = quarter[part_rows:], cotangent[token_half:]
    ready, gain_one, gain_two, segment_columns, quarter_rest, cot_rest = after(
        (got, gain_one, gain_two, segment_columns, quarter_rest, cot_rest),
        crossed_one, cot_first, slot_columns, router_weight, router_weight_three,
    )
    pieces = [(v, swap(v)) for v in ready]
    crossed_two = across(quarter_rest)
    cot_second = [shift(after(cot_rest, pieces), k) for k in range(1, half)]
    cot_other = swap(after(cotangent, pieces))
    cot_first_other = [swap(after(v, pieces)) for v in cot_first]
    partner_one = lax.all_gather(after(crossed_one, pieces), "dp", axis=0, tiled=True)

    normed_one, qkv, mixture, totals = attend_call(
        place, tokens, gain_one, document_index, segment_columns, padding_token_mask, qkv_own, pieces
    )
    hidden_one, payload = route_call(
        place, after(mixture, crossed_two, cot_second, cot_other, cot_first_other), tokens, gain_two, router_weight,
        slot_columns, [w_out], pieces, experts,
    )

    payload_other = swap(payload)
    payload_far_same = [shift(payload, k) for k in range(1, half)]
    total_rows = chips // 2 * 2 * slot_rows

    two = after(crossed_two, payload_other)
    partner = [partner_one, two] + from_dp(two)
    spread = tuple((0, d * part_rows, part_rows, (False, d), 0) for d in range(data))
    spread += tuple((1 + k, 0, quarter.shape[0] - part_rows, (True, k), part_rows) for k in range(data))

    def rows_of(slot, sources, weights, prev, saved, base, cost=COST):
        return expert_call(
            hosted, (slot,), sources, weights, prev, saved, base, total_rows, experts, slot_rows, data, spread, cost
        )

    one = [(payload, payload_other, (cotangent,), (cot_other,))]
    near = rows_of(0, one, own, [], [], 0)
    near_saved = near[4:]
    near = rows_of(1, one, partner, near[:4], [], 0, LONG)
    payload_far_other = [swap(after(v, near[0])) for v in payload_far_same]
    cot_second_other = [swap(after(v, near[0])) for v in cot_second]
    many = list(zip(
        payload_far_same, payload_far_other, zip(cot_first, cot_second), zip(cot_first_other, cot_second_other)
    ))
    many = [(same, other, tuple(c_same), tuple(c_other)) for same, other, c_same, c_other in many]
    far = rows_of(1, many, partner, [], near[4:], 2 * slot_rows)
    partner_local = weight_gradient_call(far[4:], data)
    far = rows_of(0, many, own, far[:4], near_saved, 2 * slot_rows)
    saved = far[4:]

    def returned(near_same, near_other, far_same, far_other):
        sums = [
            (far_same[k].astype(f32) + swap(far_other[k]).astype(f32)).astype(bf16)
            for k in range(half - 1)
        ]
        return [near_same[0], swap(near_other[0])], sums

    def scattered(v):
        return lax.psum_scatter(v, "dp", scatter_dimension=0, tiled=True)

    partner_sum = scattered(partner_local)
    backs, back_sums = returned(near[2], near[3], far[2], far[3])
    backs += [shift(v, half - 1 - k) for k, v in enumerate(back_sums)]
    outs, out_sums = returned(near[0], after(near[1], back_sums), far[0], after(far[1], back_sums))
    own_local = weight_gradient_call([after(saved[0], back_sums, out_sums), *saved[1:]], data)
    own_sum = scattered(after(own_local, partner_sum, backs))
    grad_hidden, given, out_keep, out_give, local_norm_moe, local_router = branch_call(
        place, cotangent, hidden_one, payload, gain_two, router_weight_three, mixture, backs,
        [w_out], pieces, experts,
    )

    stages = chips.bit_length() - 1

    def chip_stage(part, stage, *others):
        there = stage < stages
        step = 1 << (stage if there else 2 * stages - 1 - stage)
        bit = lax.rem(me // 2 // step, 2)
        if there:
            size = part.shape[0] // 2
            keep = lax.dynamic_slice_in_dim(part, bit * size, size, axis=0)
            give = lax.dynamic_slice_in_dim(part, (1 - bit) * size, size, axis=0)
            return (keep.astype(f32) + chip_xor(after(give, *others), step).astype(f32)).astype(bf16)
        other = chip_xor(after(part, *others), step)
        return jnp.concatenate([jnp.where(bit == 0, part, other), jnp.where(bit == 0, other, part)], axis=0)

    rows = partner_sum.shape[0]
    thirds = jnp.split(partner_sum, (11 * rows // 36, 22 * rows // 36, 31 * rows // 36), axis=0)
    arrived_one = across(after(thirds[0], backs))
    arrived_two = across(after(thirds[1], arrived_one, grad_hidden))
    given, out_give = after((given, out_give), arrived_one)
    cuts = [0, 9 * token_rows // 40, 18 * token_rows // 40, 27 * token_rows // 40, token_rows]

    def out_parts(index, *others):
        rows = slice(cuts[index], cuts[index + 1])
        return [shift(after(v[rows], *others), half - 1 - k) for k, v in enumerate(out_sums)]

    outs_one = out_parts(0, backs)
    outs_two = out_parts(1, arrived_one, grad_hidden, outs_one)
    given, out_give = after((given, out_give), outs_one)
    out_got = swap(out_give)
    grad_qkv, qkv_keep, qkv_give = attend_back_call(
        place, document_index, segment_columns, padding_token_mask, qkv, totals, given, normed_one
    )
    qkv_give, out_got = after((qkv_give, out_got), arrived_two, outs_two)
    arrived_three = across(after(thirds[2], arrived_two))
    outs_three = out_parts(2, arrived_two, outs_two)
    out_folds = fold_first(place, out_keep, out_got, data)
    out_arrived = [dp_xor(out_folds[1], 2), dp_xor(out_folds[3], 1)]
    qkv_folds = fold_first(place, qkv_keep, swap(qkv_give), data)
    qkv_arrived = [dp_xor(qkv_folds[1], 2), dp_xor(qkv_folds[3], 1)]
    grad_tokens, local_norm_attn = input_grad_call(
        place, tokens, gain_one, after(grad_qkv, qkv_folds, out_folds, arrived_three, outs_three), grad_hidden, qkv_own, pieces
    )
    arrived_four = across(after(thirds[3], arrived_three))
    qkv_arrived, out_arrived = after((qkv_arrived, out_arrived), grad_tokens)
    local_router = local_router[:3 * experts].reshape(3, experts, features).sum(0)
    small = jnp.concatenate([local_router, local_norm_attn, local_norm_moe], axis=0)
    def folded(keep_a, give_a, keep_b, give_b):
        got_a, got_b = dp_xor(give_a, 1), dp_xor(give_b, 2)
        return jnp.concatenate([
            (keep.astype(f32) + got.astype(f32)).astype(bf16) for keep, got in ((keep_a, got_a), (keep_b, got_b))
        ], axis=1)

    qkv_folds = fold_second(place, qkv_folds[0], qkv_arrived[0], qkv_folds[2], qkv_arrived[1])
    outs_four = out_parts(3, grad_tokens)
    qkv_part = folded(*qkv_folds)
    out_part = folded(*fold_second(place, out_folds[0], out_arrived[0], out_folds[2], out_arrived[1]))
    arrived = jnp.concatenate([arrived_one, arrived_two, arrived_three, arrived_four], axis=0)
    expert_sum = (own_sum.astype(f32) + arrived.astype(f32)).astype(bf16)
    expert_sum, out_part, qkv_part = after((expert_sum, out_part, qkv_part))
    whole = lax.all_gather(expert_sum, "dp", axis=0, tiled=True)
    for stage in range(2 * stages):
        ahead = chip_stage(qkv_part, stage, *([outs_four] if stage == 2 else []))
        if stage:
            out_part = chip_stage(out_part, stage - 1, qkv_part)
        qkv_part = ahead
        if stage == 1:
            small, qkv_part = after((small, qkv_part))
    outs += [jnp.concatenate(v, axis=0) for v in zip(outs_one, outs_two, outs_three, outs_four)]
    routed = outs[0].astype(f32)
    for part in outs[1:]:
        routed = routed + part.astype(f32)
    block_out = (hidden_one + routed).astype(bf16)
    out_part = chip_stage(out_part, 2 * stages - 1, qkv_part)
    qkv_other = swap(qkv_part)
    small = small + swap(small)
    arrived = [dp_xor(small, k) for k in range(1, data)]
    grad_query, grad_key, grad_value = joined(
        place, qkv_part, qkv_other, (query_width, kv_width, kv_width)
    )
    arrived, grad_query, block_out = after((arrived, grad_query, block_out))
    for value in arrived:
        small = small + value
    (grad_out,) = joined(place, out_part, swap(out_part), (features,))
    if chips <= 4:
        arrived, grad_out = after(([chip_xor(small, k) for k in range(1, chips)], grad_out))
        for value in arrived:
            small = small + value
    else:
        for step in range(stages):
            small = small + chip_xor(small, 1 << step)
    whole, small, grad_out = after((whole, small, grad_out))
    grad_gate, grad_up, grad_down = widened(whole, data)
    grad_router = small[:experts].T
    grad_norm_attn = small[experts]
    grad_norm_moe = small[experts + 1]
    return (
        block_out,
        grad_tokens,
        grad_norm_attn,
        grad_norm_moe,
        grad_query,
        grad_key,
        grad_value,
        grad_out,
        grad_router,
        grad_gate[None],
        grad_up[None],
        grad_down[None],
    )


def solution(mesh):
    rows = P(("dp", "expert"), None)
    over_dp = P("dp", None)
    over_expert = P("expert", None, None)
    return jax.shard_map(
        body,
        mesh=mesh,
        in_specs=(
            rows, rows, P(), P(), over_dp, over_dp, over_dp, over_dp, P(),
            over_expert, over_expert, over_expert, rows, rows, rows, rows,
        ),
        out_specs=(
            rows, rows, P(), P(), over_dp, over_dp, over_dp, over_dp, P(),
            over_expert, over_expert, over_expert,
        ),
        check_vma=False,
    )
```

```python
import functools

import jax
import jax.numpy as jnp
from jax import lax
from jax.experimental import pallas as pl
from jax.experimental.pallas import tpu as pltpu
from jax.sharding import PartitionSpec as P

bf16 = jnp.bfloat16
f32 = jnp.float32
MIB = 1024 * 1024
LONG = pl.CostEstimate(flops=16 << 30, bytes_accessed=30 * MIB, transcendentals=0)
COST = pl.CostEstimate(flops=1000, bytes_accessed=1000, transcendentals=0)
NT_DIMS = (((1,), (1,)), ((), ()))
TN_DIMS = (((0,), (0,)), ((), ()))


def mm(a, b):
    return jnp.dot(a, b, preferred_element_type=f32)


def mm_nt(a, b):
    return lax.dot_general(a, b, NT_DIMS, preferred_element_type=f32)


def mm_tn(a, b):
    return lax.dot_general(a, b, TN_DIMS, preferred_element_type=f32)


def split_three(v):
    high = v.astype(bf16)
    rest = v - high.astype(f32)
    middle = rest.astype(bf16)
    low = (rest - middle.astype(f32)).astype(bf16)
    return high, middle, low


def lanes(start, size):
    return pl.ds(pl.multiple_of(start, 128), size)


def specs(kinds):
    table = {"s": pltpu.SMEM, "v": pltpu.VMEM, "a": pl.ANY}
    return [pl.BlockSpec(memory_space=table[kind]) for kind in kinds]


def params():
    return pltpu.CompilerParams(vmem_limit_bytes=60 * MIB)


def expert_kernel(experts, slots, base, data, pieces, chunks, cuts, n_weights, n_prev, n_saved, rows, *refs):
    count = len(slots)
    each = 2 + 2 * len(cuts)
    hosted, sources, refs = refs[0], refs[1:1 + each * chunks], refs[1 + each * chunks:]
    sources = [sources[each * i:each * (i + 1)] for i in range(chunks)]
    weight_refs, refs = refs[:n_weights], refs[n_weights:]
    prev, refs = refs[:n_prev], refs[n_prev + n_saved:]
    po_same, po_other, pg_same, pg_other, x_out, gp_out, h_out, gg_out, gu_out = refs[:9]
    (wg, wu, wd, nbuf, cbuf, x, gp, gc, sc, h, gg, gu, dmat, dtmat, gcol, vcol, tail_t,
     w_sem, in_sem, act_sem, p_sem) = refs[9:]
    tokens, features = sources[0][0].shape[0], sources[0][2].shape[1]
    extra = sources[0][0].shape[1] - features
    ff = wg.shape[2]
    wide = features // 2
    tail = slice(features, features + extra)

    weight_copies = []
    taken = 0
    for place, slot in enumerate(slots):
        if slot == 0:
            pairs = list(zip(weight_refs[taken:taken + 3], (wg.at[place], wu.at[place], wd.at[place])))
            taken += 3
        else:
            tall_f, tall_h = features // data, ff // data
            pairs = []
            for index, begin, size, whose, first in pieces:
                ref = weight_refs[taken + index]
                source = jnp.bitwise_xor(hosted[2], whose[1]) if whose[0] else whose[1]
                wide_rows = max(0, min(size, tall_f - first))
                if wide_rows:
                    at = pl.ds(pl.multiple_of(source * tall_f + first, 16), wide_rows)
                    pairs += [
                        (ref.at[pl.ds(begin, wide_rows), pl.ds(0, ff)], wg.at[place, at]),
                        (ref.at[pl.ds(begin, wide_rows), pl.ds(ff, ff)], wu.at[place, at]),
                    ]
                if wide_rows < size:
                    at = pl.ds(pl.multiple_of(source * tall_h + first + wide_rows - tall_f, 16), size - wide_rows)
                    pairs.append((ref.at[pl.ds(begin + wide_rows, size - wide_rows)], wd.at[place, at]))
            taken += 1 + max(piece[0] for piece in pieces)
        weight_copies.append([
            pltpu.make_async_copy(source, target, w_sem.at[place, i])
            for i, (source, target) in enumerate(pairs)
        ])

    def input_copies(index, q):
        pairs = [(sources[index][q], nbuf.at[q])]
        for part, (first, size) in zip(sources[index][2 + q * len(cuts):], cuts):
            pairs.append((part, cbuf.at[q, pl.ds(first, size)]))
        return [pltpu.make_async_copy(source, target, in_sem.at[q, i]) for i, (source, target) in enumerate(pairs)]

    def act_copies(chunk, place):
        at = pl.ds(pl.multiple_of(base + chunk * 2 * rows, 16), 2 * rows)
        return [
            pltpu.make_async_copy(source.at[place], target.at[place, at], act_sem.at[place, i])
            for i, (source, target) in enumerate(
                ((x, x_out), (gp, gp_out), (h, h_out), (gg, gg_out), (gu, gu_out)))
        ]

    def partial_copies(chunk, q, tile):
        wide_cols = pl.ds(0, wide) if tile == 0 else pl.ds(wide, wide + extra)
        cols = pl.ds(tile * wide, wide)
        return (
            pltpu.make_async_copy(
                nbuf.at[q, :, wide_cols], (pg_same, pg_other)[q].at[chunk, :, wide_cols], p_sem.at[q, tile, 0]),
            pltpu.make_async_copy(cbuf.at[q, :, cols], (po_same, po_other)[q].at[chunk, :, cols], p_sem.at[q, tile, 1]),
        )

    def dispatch(q):
        columns = nbuf[q, :, tail].astype(f32)
        tail_t[...] = columns.T
        token_lane = lax.broadcasted_iota(jnp.int32, (tokens, extra), 1)
        wanted = lax.broadcasted_iota(jnp.int32, (tokens, count * rows), 1)
        slot_cols = []
        for place in range(count):
            expert = hosted[slots[place]]
            row = (tail_t[pl.ds(3 * experts + expert, 1), :] * 128.0
                   + tail_t[pl.ds(4 * experts + expert, 1), :] - 1.0).astype(jnp.int32)
            hit = lax.broadcasted_iota(jnp.int32, (rows, tokens), 0) == row
            dmat[q, place * rows:(place + 1) * rows, :] = jnp.where(hit, 1.0, 0.0).astype(bf16)
            factor = jnp.where(token_lane == 3 * experts + expert, 128.0, 0.0)
            factor = jnp.where(token_lane == 4 * experts + expert, 1.0, factor)
            slot_cols.append(jnp.sum(columns * factor, axis=1, keepdims=True).astype(jnp.int32) - 1)
        target = slot_cols[0]
        if count == 2:
            second = wanted >= rows
            target = jnp.where(second, slot_cols[1], slot_cols[0])
            wanted = jnp.where(second, wanted - rows, wanted)
        dtmat[q] = jnp.where(wanted == target, 1.0, 0.0).astype(bf16)
        parts = mm(dmat[q], nbuf[q, :, tail])
        lane = lax.broadcasted_iota(jnp.int32, (rows, extra), 1)
        for place in range(count):
            expert = hosted[slots[place]]
            mine = (lane == expert) | (lane == expert + experts) | (lane == expert + 2 * experts)
            g = jnp.sum(jnp.where(mine, parts[place * rows:(place + 1) * rows], 0.0), axis=1, keepdims=True)
            gcol[place, q * rows:(q + 1) * rows, :] = jnp.broadcast_to(g, (rows, 128))

        for tile in range(2):
            cols = slice(tile * wide, (tile + 1) * wide)
            found = mm(dmat[q], nbuf[q, :, cols]).astype(bf16)
            cot = mm(dmat[q], cbuf[q, :, cols])
            gc[q, :, cols] = cot.astype(bf16)
            for place in range(count):
                at = slice(q * rows, (q + 1) * rows)
                own = slice(place * rows, (place + 1) * rows)
                x[place, at, cols] = found[own]
                gp[place, at, cols] = (cot[own] * gcol[place, at, 0:1]).astype(bf16)

    def forward_backward(place):
        for q in range(2):
            at = slice(q * rows, (q + 1) * rows)
            gate = mm(x[place, at, :], wg[place])
            up = mm(x[place, at, :], wu[place])
            dh = mm_nt(gp[place, at, :], wd[place])
            sig = 1.0 / (1.0 + jnp.exp(-gate))
            act = gate * sig
            h[place, at, :] = (act * up).astype(bf16)
            gg[place, at, :] = (dh * up * (sig * (1.0 + gate * (1.0 - sig)))).astype(bf16)
            gu[place, at, :] = (dh * act).astype(bf16)

    def produce(place):
        vcol[place] = jnp.zeros(vcol.shape[1:], f32)

        @pl.loop(0, 2)
        def _(tile):
            cols = lanes(tile * wide, wide)
            for q in range(2):
                at = slice(q * rows, (q + 1) * rows)
                own = pl.ds(pl.multiple_of(place * rows, 16), rows)
                produced = mm(h[place, at, :], wd[place, :, cols]).astype(bf16).astype(f32)
                along = produced * gc[q, own, cols].astype(f32)
                folded = along[:, :128]
                for part in range(1, wide // 128):
                    folded = folded + along[:, part * 128:(part + 1) * 128]
                vcol[place, at, :] += folded
                sc[q, own, cols] = (produced * gcol[place, at, 0:1]).astype(bf16)
                back = mm_nt(gg[place, at, :], wg[place, cols, :]) + mm_nt(gu[place, at, :], wu[place, cols, :])
                gc[q, own, cols] = back.astype(bf16)

    def combine(chunk, q):
        at = slice(q * rows, (q + 1) * rows)
        lane = lax.broadcasted_iota(jnp.int32, (rows, extra), 1)
        payload = []
        for place in range(count):
            expert = hosted[slots[place]]
            high, middle, low = split_three(jnp.sum(vcol[place, at, :], axis=1, keepdims=True))
            part = jnp.where(lane == expert, high.astype(f32), 0.0)
            part = jnp.where(lane == expert + experts, middle.astype(f32), part)
            part = jnp.where(lane == expert + 2 * experts, low.astype(f32), part)
            payload.append(part.astype(bf16))
        payload = jnp.concatenate(payload, axis=0) if count > 1 else payload[0]
        tail_sum = mm(dtmat[q], payload)
        if n_prev:
            tail_sum = tail_sum + nbuf[q, :, tail].astype(f32)
        nbuf[q, :, tail] = tail_sum.astype(bf16)

        for tile in range(2):
            cols = slice(tile * wide, (tile + 1) * wide)
            back = mm(dtmat[q], gc[q, :, cols])
            out = mm(dtmat[q], sc[q, :, cols])
            if n_prev:
                back = back + nbuf[q, :, cols].astype(f32)
                out = out + cbuf[q, :, cols].astype(f32)
            nbuf[q, :, cols] = back.astype(bf16)
            cbuf[q, :, cols] = out.astype(bf16)
            for copy in partial_copies(chunk, q, tile):
                copy.start()

    def prev_copies(chunk):
        po0, po1, pg0, pg1 = prev
        return (
            pltpu.make_async_copy(pg0.at[chunk], nbuf.at[0], in_sem.at[0, 0]),
            pltpu.make_async_copy(pg1.at[chunk], nbuf.at[1], in_sem.at[1, 0]),
            pltpu.make_async_copy(po0.at[chunk], cbuf.at[0], in_sem.at[0, 1]),
            pltpu.make_async_copy(po1.at[chunk], cbuf.at[1], in_sem.at[1, 1]),
        )

    late = max(slots) == 0
    for copy in input_copies(0, 0):
        copy.start()
    if not late:
        for copy in input_copies(0, 1):
            copy.start()
        for copies in weight_copies:
            for copy in copies:
                copy.start()

    @pl.loop(0, chunks)
    def _(chunk):
        for copy in input_copies(0, 0):
            copy.wait()

        @pl.when((chunk == 0) & late)
        def _():
            for copy in input_copies(0, 1):
                copy.start()
            for copies in weight_copies:
                for copy in copies:
                    copy.start()

        dispatch(0)
        for copy in input_copies(0, 1):
            copy.wait()
        dispatch(1)
        if n_prev:
            for copy in prev_copies(chunk):
                copy.start()
        for place in range(count):
            @pl.when(chunk == 0)
            def _():
                for copy in weight_copies[place]:
                    copy.wait()

            forward_backward(place)
            for copy in act_copies(chunk, place):
                copy.start()
            produce(place)
        if n_prev:
            for copy in prev_copies(chunk):
                copy.wait()
        for q in range(2):
            combine(chunk, q)
        for place in range(count):
            for copy in act_copies(chunk, place):
                copy.wait()
        for q in range(2):
            for tile in range(2):
                for copy in partial_copies(chunk, q, tile):
                    copy.wait()

        for index in range(1, chunks):
            @pl.when(chunk + 1 == index)
            def _():
                for q in range(2):
                    for copy in input_copies(index, q):
                        copy.start()


def expert_call(hosted, slots, sources, weights, prev, saved, base, total, experts, rows, data, pieces, cost):
    chunks = len(sources)
    tokens, features = sources[0][0].shape[0], sources[0][2][0].shape[1]
    cuts, first = [], 0
    for part in sources[0][2]:
        cuts.append((first, part.shape[0]))
        first += part.shape[0]
    flat = [v for same, other, *parts in sources for v in (same, other, *parts[0], *parts[1])]
    ff = weights[0].shape[1] if slots[0] == 0 else weights[0].shape[1] // 2
    wide_n = sources[0][0].shape[1]
    extra = wide_n - features
    count = len(slots)
    shape = jax.ShapeDtypeStruct
    act_f = shape((count, total, features), bf16)
    act_h = shape((count, total, ff), bf16)
    out_shape = (
        [shape((chunks, tokens, features), bf16)] * 2
        + [shape((chunks, tokens, wide_n), bf16)] * 2
        + [act_f, act_f, act_h, act_h, act_h]
    )
    many = 2 * rows
    first_prev = 1 + len(flat) + len(weights)
    first_saved = first_prev + len(prev)
    return pl.pallas_call(
        functools.partial(
            expert_kernel, experts, slots, base, data, pieces, chunks, tuple(cuts), len(weights), len(prev), len(saved), rows),
        out_shape=out_shape,
        in_specs=specs("s" + "a" * (len(flat) + len(weights) + len(prev) + len(saved))),
        out_specs=specs("a" * 9),
        input_output_aliases={
            **{first_prev + i: i for i in range(len(prev))},
            **{first_saved + i: 4 + i for i in range(len(saved))},
        },
        scratch_shapes=[
            pltpu.VMEM((count, features, ff), bf16),
            pltpu.VMEM((count, features, ff), bf16),
            pltpu.VMEM((count, ff, features), bf16),
            pltpu.VMEM((2, tokens, wide_n), bf16),
            pltpu.VMEM((2, tokens, features), bf16),
            pltpu.VMEM((count, many, features), bf16),
            pltpu.VMEM((count, many, features), bf16),
            pltpu.VMEM((2, count * rows, features), bf16),
            pltpu.VMEM((2, count * rows, features), bf16),
            pltpu.VMEM((count, many, ff), bf16),
            pltpu.VMEM((count, many, ff), bf16),
            pltpu.VMEM((count, many, ff), bf16),
            pltpu.VMEM((2, count * rows, tokens), bf16),
            pltpu.VMEM((2, tokens, count * rows), bf16),
            pltpu.VMEM((count, many, 128), f32),
            pltpu.VMEM((count, many, 128), f32),
            pltpu.VMEM((extra, tokens), f32),
            pltpu.SemaphoreType.DMA((count, 3 * max(1, len(pieces)))),
            pltpu.SemaphoreType.DMA((2, 1 + len(cuts))),
            pltpu.SemaphoreType.DMA((count, 5)),
            pltpu.SemaphoreType.DMA((2, 2, 2)),
        ],
        compiler_params=params(),
        cost_estimate=cost,
        name="expert_rows",
    )(hosted, *flat, *weights, *prev, *saved)


def weight_gradient_kernel(data, x_in, gg_in, gu_in, h_in, gp_in, out, x, ggu, h, gp, wide, down, sem, out_sem):
    features, ff = x.shape[1], h.shape[1]
    tall = 512
    tall_f, tall_h = features // data, ff // data
    step = tall_f + tall_h
    loads = [
        pltpu.make_async_copy(source.at[0], target, sem.at[i])
        for i, (source, target) in enumerate((
            (gg_in, ggu.at[:, pl.ds(0, ff)]), (gu_in, ggu.at[:, pl.ds(ff, ff)]), (x_in, x), (h_in, h), (gp_in, gp)))
    ]
    for copy in loads[:3]:
        copy.start()
    stores = [
        pltpu.make_async_copy(wide.at[pl.ds(d * tall_f, tall_f)], out.at[pl.ds(d * step, tall_f)], out_sem.at[2 * d])
        for d in range(data)
    ] + [
        pltpu.make_async_copy(down.at[pl.ds(d * tall_h, tall_h)], out.at[pl.ds(d * step + tall_f, tall_h)],
                              out_sem.at[2 * d + 1])
        for d in range(data)
    ]
    for copy in loads[:3]:
        copy.wait()
    for copy in loads[3:]:
        copy.start()

    @pl.loop(0, features // tall)
    def _(tile):
        at = pl.ds(pl.multiple_of(tile * tall, tall), tall)
        wide[at, :] = mm_tn(x[:, lanes(tile * tall, tall)], ggu[...]).astype(bf16)

    for copy in stores[:data]:
        copy.start()
    for copy in loads[3:]:
        copy.wait()

    @pl.loop(0, ff // (tall // 2))
    def _(tile):
        at = pl.ds(pl.multiple_of(tile * 256, 256), 256)
        down[at, :] = mm_tn(h[:, lanes(tile * 256, 256)], gp[...]).astype(bf16)

    for copy in stores[data:]:
        copy.start()
    for copy in stores:
        copy.wait()


def weight_gradient_call(saved, data):
    x, gp, h, gg, gu = saved
    slots, features, ff = x.shape[1], x.shape[2], h.shape[2]
    return pl.pallas_call(
        functools.partial(weight_gradient_kernel, data),
        out_shape=jax.ShapeDtypeStruct((features + ff, 2 * ff), bf16),
        in_specs=specs("aaaaa"),
        out_specs=pl.BlockSpec(memory_space=pl.ANY),
        scratch_shapes=[
            pltpu.VMEM((slots, features), bf16),
            pltpu.VMEM((slots, 2 * ff), bf16),
            pltpu.VMEM((slots, ff), bf16),
            pltpu.VMEM((slots, features), bf16),
            pltpu.VMEM((features, 2 * ff), bf16),
            pltpu.VMEM((ff, features), bf16),
            pltpu.SemaphoreType.DMA((5,)),
            pltpu.SemaphoreType.DMA((2 * data,)),
        ],
        compiler_params=params(),
        cost_estimate=COST,
        name="expert_weight_gradients",
    )(x, gg, gu, h, gp)


def widened_kernel(whole, gate, up, down):
    tall, ff = gate.shape
    gate[...] = whole[:tall, :ff].astype(f32)
    up[...] = whole[:tall, ff:].astype(f32)
    down[...] = whole[tall:, :].astype(f32)


def widened(whole, data):
    rows, features = whole.shape[0] // data, whole.shape[1]
    ff = features // 2
    tall = rows * 2 // 3
    blocks = [(tall, ff), (tall, ff), (rows - tall, features)]
    return pl.pallas_call(
        widened_kernel,
        grid=(data,),
        in_specs=[pl.BlockSpec((rows, features), lambda d: (d, 0))],
        out_specs=[pl.BlockSpec(block, lambda d: (d, 0)) for block in blocks],
        out_shape=[jax.ShapeDtypeStruct((data * block[0], block[1]), f32) for block in blocks],
        compiler_params=params(),
        cost_estimate=COST,
        name="widened",
    )(whole)


epsilon = 1e-06
neg_fill = -1e30
QUERY_HEADS = 12
KEY_VALUE_HEADS = 2
HEAD_SIZE = 128
GROUP = QUERY_HEADS // KEY_VALUE_HEADS
SCORE_SCALE = HEAD_SIZE ** (-0.5)


def piece_copies(place, own, pieces, begin, weight, sem):
    rows, half = own[0].shape[0], weight.shape[1] // 2
    mine, core = place[0], place[1]
    copies = []
    column = 0
    for part in own:
        at = weight.at[pl.ds(pl.multiple_of(mine * rows, 16), rows), pl.ds(column, part.shape[1])]
        copies.append(pltpu.make_async_copy(part, at, sem.at[len(copies)]))
        column += part.shape[1]
    for (k, skip), pair in zip(((1, 0), (2, 0), (3, 0), (3, rows // 2)), pieces):
        first = pl.multiple_of(jnp.bitwise_xor(mine, k) * rows + skip, 16)
        for part, which in zip(pair, (core, 1 - core)):
            at = weight.at[pl.ds(first, part.shape[0]), lanes(which * half, half)]
            copies.append(pltpu.make_async_copy(part.at[:, pl.ds(begin, half)], at, sem.at[len(copies)]))
    return copies


def attention_mask(segment_row, segment_col, pad_row, first, size, span):
    row = first + lax.broadcasted_iota(jnp.int32, (size, span), 0)
    col = lax.broadcasted_iota(jnp.int32, (size, span), 1)
    same = segment_col[first:first + size, :] == segment_row[:, :span]
    return same & (((pad_row[:, :span] == 1) & (col < row)) | (col == row))


def stacked(ref, rows, c):
    return jnp.concatenate(
        [ref[rows, lanes((c * GROUP + g) * HEAD_SIZE, HEAD_SIZE)] for g in range(GROUP)], axis=0
    )


def attend_kernel(
    n_own, n_pairs, tokens_total, block,
    place, tokens, gain, segment_row, segment_col, pad_row, *refs,
):
    own = refs[:n_own]
    flat = refs[n_own:n_own + 2 * n_pairs]
    pieces = [(flat[2 * k], flat[2 * k + 1]) for k in range(n_pairs)]
    normed, qkv, mixture, totals, weight, sem = refs[n_own + 2 * n_pairs:]
    copies = piece_copies(place, own, pieces, 0, weight, sem)
    for copy in copies:
        copy.start()
    width = QUERY_HEADS * HEAD_SIZE
    kv_width = KEY_VALUE_HEADS * HEAD_SIZE
    source = tokens[...].astype(f32)
    inverse = lax.rsqrt(jnp.mean(source * source, axis=1, keepdims=True) + epsilon)
    normed[...] = (source * inverse * gain[...]).astype(bf16)
    for copy in copies:
        copy.wait()
    wide = 512

    @pl.loop(0, qkv.shape[1] // wide)
    def _(tile):
        cols = lanes(tile * wide, wide)
        qkv[:, cols] = mm(normed[...], weight[:, cols]).astype(bf16)

    totals[...] = jnp.zeros_like(totals)
    segment_of_row, segment_of_col, pad = segment_row[...], segment_col[...], pad_row[...]

    @pl.loop(0, KEY_VALUE_HEADS)
    def _(c):
        for first in range(0, tokens_total, block):
            span = first + block
            rows = slice(first, span)
            mask = attention_mask(segment_of_row, segment_of_col, pad, first, block, span)
            keys = qkv[:span, lanes(width + c * HEAD_SIZE, HEAD_SIZE)]
            values = qkv[:span, lanes(width + kv_width + c * HEAD_SIZE, HEAD_SIZE)]
            scores = mm_nt(stacked(qkv, rows, c), keys) * SCORE_SCALE
            lane = lax.broadcasted_iota(jnp.int32, (block, 128), 1)
            stats = totals[rows, :]
            weights = []
            for g in range(GROUP):
                part = jnp.where(mask, scores[g * block:(g + 1) * block], neg_fill)
                top = jnp.max(part, axis=1, keepdims=True)
                raised = jnp.exp(part - top)
                total = jnp.sum(raised, axis=1, keepdims=True)
                stats = jnp.where(lane == c * GROUP + g, top + jnp.log(total), stats)
                weights.append((raised * (1.0 / total)).astype(bf16))
            totals[rows, :] = stats
            mixed = mm(jnp.concatenate(weights, axis=0), values).astype(bf16)
            for g in range(GROUP):
                mixture[rows, lanes((c * GROUP + g) * HEAD_SIZE, HEAD_SIZE)] = mixed[g * block:(g + 1) * block]


def attend_call(place, tokens, gain, segments, segment_columns, pads, own, pieces):
    rows, features = tokens.shape
    width = (QUERY_HEADS + 2 * KEY_VALUE_HEADS) * HEAD_SIZE
    mixed = QUERY_HEADS * HEAD_SIZE
    flat = [part for pair in pieces for part in pair]
    shape = jax.ShapeDtypeStruct
    return pl.pallas_call(
        functools.partial(attend_kernel, len(own), len(pieces), rows, 128),
        out_shape=[
            shape((rows, features), bf16), shape((rows, width), bf16), shape((rows, mixed), bf16),
            shape((rows, 128), f32),
        ],
        in_specs=specs("s" + "v" * 5 + "a" * (len(own) + len(flat))),
        out_specs=specs("vvvv"),
        scratch_shapes=[
            pltpu.VMEM((features, width), bf16),
            pltpu.SemaphoreType.DMA((len(own) + len(flat),)),
        ],
        compiler_params=params(),
        cost_estimate=COST,
        name="attend",
    )(place, tokens, gain, segments, segment_columns, pads, *own, *flat)


def attend_back_kernel(tokens_total, block, place, segment_row, segment_col, pad_row, qkv, totals, given, normed_in,
                       grad_out, keep_out, give_out, grad_keys, grad_values, normed, grad, keep, give, sem, out_sem):
    width = QUERY_HEADS * HEAD_SIZE
    kv_width = KEY_VALUE_HEADS * HEAD_SIZE
    segment_of_row, segment_of_col, pad = segment_row[...], segment_col[...], pad_row[...]
    normed_load = pltpu.make_async_copy(normed_in, normed, sem)
    normed_load.start()

    @pl.loop(0, KEY_VALUE_HEADS)
    def _(c):
        grad_keys[...] = jnp.zeros_like(grad_keys)
        grad_values[...] = jnp.zeros_like(grad_values)
        for first in range(0, tokens_total, block):
            span = first + block
            rows = slice(first, span)
            mask = attention_mask(segment_of_row, segment_of_col, pad, first, block, span)
            keys = qkv[:span, lanes(width + c * HEAD_SIZE, HEAD_SIZE)]
            values = qkv[:span, lanes(width + kv_width + c * HEAD_SIZE, HEAD_SIZE)]
            queries = stacked(qkv, rows, c)
            arrived = stacked(given, rows, c)
            scores = mm_nt(queries, keys) * SCORE_SCALE
            grad_weights = mm_nt(arrived, values)
            lane = lax.broadcasted_iota(jnp.int32, (block, 128), 1)
            stats = totals[rows, :]
            weights, grad_scores = [], []
            for g in range(GROUP):
                at = slice(g * block, (g + 1) * block)
                total = jnp.sum(jnp.where(lane == c * GROUP + g, stats, 0.0), axis=1, keepdims=True)
                probs = jnp.exp(jnp.where(mask, scores[at], neg_fill) - total)
                weights.append(probs.astype(bf16))
                dw = grad_weights[at]
                mean = jnp.sum(probs * dw, axis=1, keepdims=True)
                grad_scores.append((probs * (dw - mean)).astype(bf16))
            weights = jnp.concatenate(weights, axis=0)
            grad_scores = jnp.concatenate(grad_scores, axis=0)
            grad_queries = (mm(grad_scores, keys) * SCORE_SCALE).astype(bf16)
            for g in range(GROUP):
                grad[rows, lanes((c * GROUP + g) * HEAD_SIZE, HEAD_SIZE)] = grad_queries[g * block:(g + 1) * block]
            grad_keys[:span, :] += mm_tn(grad_scores, queries)
            grad_values[:span, :] += mm_tn(weights, arrived)
        grad[:, lanes(width + c * HEAD_SIZE, HEAD_SIZE)] = (grad_keys[...] * SCORE_SCALE).astype(bf16)
        grad[:, lanes(width + kv_width + c * HEAD_SIZE, HEAD_SIZE)] = grad_values[...].astype(bf16)

    grad_store = pltpu.make_async_copy(grad, grad_out, out_sem.at[0])
    grad_store.start()
    normed_load.wait()
    tall = 256

    def stores(tile):
        at = pl.ds(pl.multiple_of(tile * tall, tall), tall)
        return (
            pltpu.make_async_copy(keep.at[at], keep_out.at[at], out_sem.at[1 + 2 * tile]),
            pltpu.make_async_copy(give.at[at], give_out.at[at], out_sem.at[2 + 2 * tile]),
        )

    @pl.loop(0, normed.shape[1] // tall)
    def _(tile):
        cols = lanes(tile * tall, tall)
        at = pl.ds(pl.multiple_of(tile * tall, tall), tall)
        for core, out in ((place[1], keep), (1 - place[1], give)):
            out[at, :] = mm_tn(normed[:, cols], grad[:, lanes(core * keep.shape[1], keep.shape[1])]).astype(bf16)
        for copy in stores(tile):
            copy.start()

    grad_store.wait()

    @pl.loop(0, normed.shape[1] // tall)
    def _(tile):
        for copy in stores(tile):
            copy.wait()


def attend_back_call(place, segments, segment_columns, pads, qkv, totals, given, normed):
    rows, width = qkv.shape
    features = normed.shape[1]
    shape = jax.ShapeDtypeStruct
    return pl.pallas_call(
        functools.partial(attend_back_kernel, rows, 128),
        out_shape=[shape((rows, width), bf16)] + [shape((features, width // 2), bf16)] * 2,
        in_specs=specs("s" + "v" * 6 + "a"),
        out_specs=specs("aaa"),
        scratch_shapes=[
            pltpu.VMEM((rows, HEAD_SIZE), f32),
            pltpu.VMEM((rows, HEAD_SIZE), f32),
            pltpu.VMEM((rows, features), bf16),
            pltpu.VMEM((rows, width), bf16),
            pltpu.VMEM((features, width // 2), bf16),
            pltpu.VMEM((features, width // 2), bf16),
            pltpu.SemaphoreType.DMA,
            pltpu.SemaphoreType.DMA((1 + 2 * (features // 256),)),
        ],
        compiler_params=params(),
        cost_estimate=COST,
        name="attend_back",
    )(place, segments, segment_columns, pads, qkv, totals, given, normed)


def route_kernel(experts, n_own, n_pairs, place, mixture, tokens, gain, router_weight, slots, *refs):
    own = refs[:n_own]
    flat = refs[n_own:n_own + 2 * n_pairs]
    pieces = [(flat[2 * k], flat[2 * k + 1]) for k in range(n_pairs)]
    hidden, payload, weight, sem = refs[n_own + 2 * n_pairs:]
    copies = piece_copies(place, own, pieces, (QUERY_HEADS + 2 * KEY_VALUE_HEADS) * HEAD_SIZE // 2, weight, sem)
    for copy in copies:
        copy.start()
    for copy in copies:
        copy.wait()
    features = tokens.shape[1]
    wide = features // 2

    @pl.loop(0, 2)
    def _(tile):
        cols = lanes(tile * wide, wide)
        hidden[:, cols] = tokens[:, cols].astype(f32) + mm(mixture[...], weight[:, cols])

    value = hidden[...]
    inverse = lax.rsqrt(jnp.mean(value * value, axis=1, keepdims=True) + epsilon)
    payload[:, :features] = (value * inverse * gain[...]).astype(bf16)
    extra = payload.shape[1] - features
    logits = mm(payload[:, :features], router_weight[...])
    lane = lax.broadcasted_iota(jnp.int32, logits.shape, 1)
    logits = jnp.where(lane < experts, logits, neg_fill)
    raised = jnp.exp(logits - jnp.max(logits, axis=1, keepdims=True))
    router = raised / jnp.sum(raised, axis=1, keepdims=True)
    high, middle, low = split_three(router)
    tail = high.astype(f32)
    tail = tail + pltpu.roll(middle.astype(f32), experts, 1)
    tail = tail + pltpu.roll(low.astype(f32), 2 * experts, 1)
    payload[:, features:] = (tail + slots[...]).astype(bf16)


def tail_width(experts):
    return (5 * experts + 127) // 128 * 128


def route_call(place, mixture, tokens, gain, router_weight, slots, own, pieces, experts):
    rows, features = tokens.shape
    extra = tail_width(experts)
    flat = [part for pair in pieces for part in pair]
    shape = jax.ShapeDtypeStruct
    return pl.pallas_call(
        functools.partial(route_kernel, experts, len(own), len(pieces)),
        out_shape=[shape((rows, features), f32), shape((rows, features + extra), bf16)],
        in_specs=specs("s" + "v" * 5 + "a" * (len(own) + len(flat))),
        out_specs=specs("vv"),
        scratch_shapes=[
            pltpu.VMEM((mixture.shape[1], features), bf16),
            pltpu.SemaphoreType.DMA((len(own) + len(flat),)),
        ],
        compiler_params=params(),
        cost_estimate=COST,
        name="route",
    )(place, mixture, tokens, gain, router_weight, slots, *own, *flat)


def branch_kernel(experts, n_back, n_own, n_pairs, place, gain, router_weight, cotangent, hidden, payload, mixture_in, *refs):
    backs, refs = refs[:n_back], refs[n_back:]
    own = refs[:n_own]
    flat = refs[n_own:n_own + 2 * n_pairs]
    pieces = [(flat[2 * k], flat[2 * k + 1]) for k in range(n_pairs)]
    grad_hidden, given, keep_out, give_out, local_gain, local_router = refs[n_own + 2 * n_pairs:][:6]
    (weight, branch, mixture, cot_buf, hidden_buf, payload_buf, back_buf, keep, give, given_buf,
     sem, mix_sem, in_sem, out_sem, sum_sem) = refs[n_own + 2 * n_pairs + 6:]
    parts, short = cot_buf.shape[0], cot_buf.shape[1]
    features = cot_buf.shape[2]
    extra = payload_buf.shape[2] - features
    wide_rows = mixture.shape[1]

    def loads(part):
        at = pl.ds(pl.multiple_of(part * short, 16), short)
        pairs = [(ref, back_buf.at[part, i]) for i, ref in enumerate(backs)]
        pairs += [(hidden, hidden_buf.at[part]), (payload, payload_buf.at[part]), (cotangent, cot_buf.at[part])]
        return [
            pltpu.make_async_copy(source.at[at], target, in_sem.at[part, i]) for i, (source, target) in enumerate(pairs)
        ]

    def hidden_store(part):
        at = pl.ds(pl.multiple_of(part * short, 16), short)
        return pltpu.make_async_copy(hidden_buf.at[part], grad_hidden.at[at], out_sem.at[part])

    for part in range(parts):
        for copy in loads(part):
            copy.start()
    mixture_load = pltpu.make_async_copy(mixture_in, mixture, mix_sem)
    mixture_load.start()
    copies = piece_copies(place, own, pieces, (QUERY_HEADS + 2 * KEY_VALUE_HEADS) * HEAD_SIZE // 2, weight, sem)
    for copy in copies:
        copy.start()
    local_gain[...] = jnp.zeros_like(local_gain)
    local_router[...] = jnp.zeros_like(local_router)

    def three(value):
        width = value.shape[1]
        return (value + pltpu.roll(value, width - experts, 1)
                + pltpu.roll(value, width - 2 * experts, 1))

    @pl.loop(0, parts)
    def _(part):
        for copy in loads(part):
            copy.wait()

        def arrived(cols):
            total = back_buf[part, 0, :, cols].astype(f32)
            for i in range(1, n_back):
                total = total + back_buf[part, i, :, cols].astype(f32)
            return total

        lane = lax.broadcasted_iota(jnp.int32, (short, extra), 1)
        router = jnp.where(lane < experts, three(payload_buf[part, :, features:].astype(f32)), 0.0)
        select = jnp.where(lane < experts, three(arrived(slice(features, features + extra))), 0.0)
        logits = router * (select - jnp.sum(router * select, axis=1, keepdims=True))
        high, middle, low = split_three(logits)
        packed = high.astype(f32) + pltpu.roll(middle.astype(f32), experts, 1)
        packed = (packed + pltpu.roll(low.astype(f32), 2 * experts, 1)).astype(bf16)
        grad_normed = arrived(slice(0, features)) + mm_nt(packed, router_weight[...])
        local_router[...] += mm_tn(packed, payload_buf[part, :, :features])
        value = hidden_buf[part]
        inverse = lax.rsqrt(jnp.mean(value * value, axis=1, keepdims=True) + epsilon)
        along = grad_normed * value
        local_gain[...] += jnp.sum(along * inverse, axis=0, keepdims=True)
        mean = jnp.mean(along * gain[...], axis=1, keepdims=True)
        total = (cot_buf[part].astype(f32) + inverse * (grad_normed * gain[...])
                 - value * (inverse * inverse * inverse * mean))
        hidden_buf[part] = total
        branch[pl.ds(pl.multiple_of(part * short, 16), short), :] = total.astype(bf16)
        hidden_store(part).start()

    mixture_load.wait()
    tall = 256

    def sum_stores(tile):
        at = pl.ds(pl.multiple_of(tile * tall, tall), tall)
        return (
            pltpu.make_async_copy(keep.at[at], keep_out.at[at], sum_sem.at[tile, 0]),
            pltpu.make_async_copy(give.at[at], give_out.at[at], sum_sem.at[tile, 1]),
        )

    @pl.loop(0, wide_rows // tall)
    def _(tile):
        cols = lanes(tile * tall, tall)
        at = pl.ds(pl.multiple_of(tile * tall, tall), tall)
        for core, out in ((place[1], keep), (1 - place[1], give)):
            out[at, :] = mm_tn(mixture[:, cols], branch[:, lanes(core * keep.shape[1], keep.shape[1])]).astype(bf16)
        for copy in sum_stores(tile):
            copy.start()

    for copy in copies:
        copy.wait()
    wide = wide_rows // 2

    def given_store(tile):
        cols = lanes(tile * wide, wide)
        return pltpu.make_async_copy(given_buf.at[:, cols], given.at[:, cols], out_sem.at[parts + tile])

    @pl.loop(0, 2)
    def _(tile):
        at = pl.ds(pl.multiple_of(tile * wide, 128), wide)
        given_buf[:, lanes(tile * wide, wide)] = mm_nt(branch[...], weight[at, :]).astype(bf16)
        given_store(tile).start()

    for part in range(parts):
        hidden_store(part).wait()

    @pl.loop(0, wide_rows // tall)
    def _(tile):
        for copy in sum_stores(tile):
            copy.wait()

    for tile in range(2):
        given_store(tile).wait()


def branch_call(place, cotangent, hidden, payload, gain, router_weight, mixture, backs, own, pieces, experts):
    rows, features = cotangent.shape
    wide_n = payload.shape[1]
    mixed = mixture.shape[1]
    parts = 4
    short = rows // parts
    flat = [part for pair in pieces for part in pair]
    shape = jax.ShapeDtypeStruct
    return pl.pallas_call(
        functools.partial(branch_kernel, experts, len(backs), len(own), len(pieces)),
        out_shape=[
            shape((rows, features), f32), shape((rows, mixed), bf16), shape((mixed, features // 2), bf16),
            shape((mixed, features // 2), bf16), shape((1, features), f32), shape((wide_n - features, features), f32),
        ],
        in_specs=specs("svv" + "a" * (4 + len(backs) + len(own) + len(flat))),
        out_specs=specs("aaaavv"),
        scratch_shapes=[
            pltpu.VMEM((mixed, features), bf16),
            pltpu.VMEM((rows, features), bf16),
            pltpu.VMEM((rows, mixed), bf16),
            pltpu.VMEM((parts, short, features), bf16),
            pltpu.VMEM((parts, short, features), f32),
            pltpu.VMEM((parts, short, wide_n), bf16),
            pltpu.VMEM((parts, len(backs), short, wide_n), bf16),
            pltpu.VMEM((mixed, features // 2), bf16),
            pltpu.VMEM((mixed, features // 2), bf16),
            pltpu.VMEM((rows, mixed), bf16),
            pltpu.SemaphoreType.DMA((len(own) + len(flat),)),
            pltpu.SemaphoreType.DMA,
            pltpu.SemaphoreType.DMA((parts, len(backs) + 3)),
            pltpu.SemaphoreType.DMA((parts + 2,)),
            pltpu.SemaphoreType.DMA((mixed // 256, 2)),
        ],
        compiler_params=params(),
        cost_estimate=COST,
        name="branch",
    )(place, gain, router_weight, cotangent, hidden, payload, mixture, *backs, *own, *flat)


def input_grad_kernel(n_own, n_pairs, place, tokens, gain, grad, grad_hidden, *refs):
    own = refs[:n_own]
    flat = refs[n_own:n_own + 2 * n_pairs]
    pieces = [(flat[2 * k], flat[2 * k + 1]) for k in range(n_pairs)]
    out, local_gain, weight, normed_grad, sem = refs[n_own + 2 * n_pairs:]
    copies = piece_copies(place, own, pieces, 0, weight, sem)
    for copy in copies:
        copy.start()
    for copy in copies:
        copy.wait()
    features = tokens.shape[1]
    wide = features // 2

    @pl.loop(0, 2)
    def _(tile):
        at = pl.ds(pl.multiple_of(tile * wide, 128), wide)
        normed_grad[:, lanes(tile * wide, wide)] = mm_nt(grad[...], weight[at, :])

    value = tokens[...].astype(f32)
    inverse = lax.rsqrt(jnp.mean(value * value, axis=1, keepdims=True) + epsilon)
    grad_normed = normed_grad[...]
    along = grad_normed * value
    local_gain[...] = jnp.sum(along * inverse, axis=0, keepdims=True)
    mean = jnp.mean(along * gain[...], axis=1, keepdims=True)
    out[...] = grad_hidden[...] + inverse * (grad_normed * gain[...]) - value * (inverse * inverse * inverse * mean)


def input_grad_call(place, tokens, gain, grad, grad_hidden, own, pieces):
    rows, features = tokens.shape
    flat = [part for pair in pieces for part in pair]
    shape = jax.ShapeDtypeStruct
    return pl.pallas_call(
        functools.partial(input_grad_kernel, len(own), len(pieces)),
        out_shape=[shape((rows, features), f32), shape((1, features), f32)],
        in_specs=specs("s" + "v" * 4 + "a" * (len(own) + len(flat))),
        out_specs=specs("vv"),
        scratch_shapes=[
            pltpu.VMEM((features, grad.shape[1]), bf16),
            pltpu.VMEM((rows, features), f32),
            pltpu.SemaphoreType.DMA((len(own) + len(flat),)),
        ],
        compiler_params=params(),
        cost_estimate=COST,
        name="input_grad",
    )(place, tokens, gain, grad, grad_hidden, *own, *flat)


def fold_first_kernel(place, keep, got, keep_a, give_a, keep_b, give_b):
    rows, quart = keep_a.shape[1], keep_a.shape[2]
    high, low = lax.div(place[0], 2), lax.rem(place[0], 2)

    def total(high_bit, low_bit, first):
        at = pl.ds(pl.multiple_of((high_bit * 2 + low_bit) * rows, 16), rows)
        cols = slice(first, first + quart)
        return (keep[at, cols].astype(f32) + got[at, cols].astype(f32)).astype(bf16)

    for bit in range(2):
        keep_a[bit] = total(high, bit, 0)
        give_a[bit] = total(1 - high, bit, 0)
        keep_b[bit] = total(bit, low, quart)
        give_b[bit] = total(bit, 1 - low, quart)


def fold_first(place, keep, got, data):
    rows, quart = keep.shape[0] // data, keep.shape[1] // 2
    return pl.pallas_call(
        fold_first_kernel,
        out_shape=[jax.ShapeDtypeStruct((2, rows, quart), bf16)] * 4,
        in_specs=specs("svv"),
        out_specs=specs("vvvv"),
        compiler_params=params(),
        cost_estimate=COST,
        name="fold_first",
    )(place, keep, got)


def fold_second_kernel(place, keep_a, got_a, keep_b, got_b, next_a, give_a, next_b, give_b):
    high, low = lax.div(place[0], 2), lax.rem(place[0], 2)
    for bit, keep, got, kept, give in ((low, keep_a, got_a, next_a, give_a), (high, keep_b, got_b, next_b, give_b)):
        kept[...] = (keep[bit].astype(f32) + got[bit].astype(f32)).astype(bf16)
        give[...] = (keep[1 - bit].astype(f32) + got[1 - bit].astype(f32)).astype(bf16)


def fold_second(place, keep_a, got_a, keep_b, got_b):
    return pl.pallas_call(
        fold_second_kernel,
        out_shape=[jax.ShapeDtypeStruct(keep_a.shape[1:], bf16)] * 4,
        in_specs=specs("svvvv"),
        out_specs=specs("vvvv"),
        compiler_params=params(),
        cost_estimate=COST,
        name="fold_second",
    )(place, keep_a, got_a, keep_b, got_b)


def joined_kernel(place, mine, other, *outs):
    half = mine.shape[1]
    first = 0
    for out in outs:
        done = 0
        while done < out.shape[1]:
            at = first + done
            size = min(out.shape[1] - done, half - at % half)
            cols = slice(at % half, at % half + size)
            own = place[1] == at // half
            out[:, done:done + size] = jnp.where(own, mine[:, cols], other[:, cols]).astype(f32)
            done += size
        first += out.shape[1]


def joined(place, mine, other, widths):
    return pl.pallas_call(
        joined_kernel,
        out_shape=[jax.ShapeDtypeStruct((mine.shape[0], width), f32) for width in widths],
        in_specs=specs("svv"),
        out_specs=specs("v" * len(widths)),
        compiler_params=params(),
        cost_estimate=COST,
        name="joined",
    )(place, mine, other)


def pair_slots(routes, order_row, experts, capacity):
    pair_count = order_row.shape[0]
    place = (
        jnp.zeros((pair_count,), jnp.int32)
        .at[order_row]
        .set(jnp.arange(pair_count, dtype=jnp.int32), unique_indices=True, mode="promise_in_bounds")
        .reshape(routes.shape)
    )
    columns = jnp.arange(experts, dtype=jnp.int32)
    hit = routes[None, :, :] == columns[:, None, None]
    key = jnp.min(jnp.where(hit, place[None], pair_count), axis=2)
    rank = jnp.sum((key[:, None, :] < key[:, :, None]).astype(jnp.int32), axis=2)
    return jnp.where((key < pair_count) & (rank < capacity), rank + 1, 0).T


def body(
    tokens,
    cotangent,
    norm_attn,
    norm_moe,
    w_query,
    key_weight,
    value_weight,
    w_out,
    w_router,
    w_gate,
    w_up,
    w_down,
    document_index,
    padding_token_mask,
    routes,
    pair_order,
):
    token_rows, features = tokens.shape
    top_count = routes.shape[1]
    experts = lax.axis_size("expert")
    data = lax.axis_size("dp")
    chips = experts // 2
    half = chips // 2
    ff = w_gate.shape[2]
    capacity = 9 * token_rows * top_count // (8 * experts)
    slot_rows = (capacity + 15) // 16 * 16
    extra = tail_width(experts)
    query_width = QUERY_HEADS * HEAD_SIZE
    kv_width = KEY_VALUE_HEADS * HEAD_SIZE
    me = lax.axis_index("expert")
    my_dp = lax.axis_index("dp")
    core = lax.rem(me, 2)
    place = jnp.stack([my_dp, core]).astype(jnp.int32)
    hosted = jnp.stack([me, lax.rem(me + experts // 2, experts), my_dp]).astype(jnp.int32)

    def swap(v):
        return lax.ppermute(v, "expert", [(j, j ^ 1) for j in range(experts)])

    def shift(v, k):
        def to(j):
            chip = j // 2
            return ((chip // half) * half + (chip % half + k) % half) * 2 + j % 2

        return lax.ppermute(v, "expert", [(j, to(j)) for j in range(experts)])

    def across(v):
        return lax.ppermute(v, "expert", [(j, (j + experts // 2) % experts) for j in range(experts)])

    def chip_xor(v, step):
        return lax.ppermute(v, "expert", [(j, ((j // 2) ^ step) * 2 + j % 2) for j in range(experts)])

    def dp_xor(v, k):
        return lax.ppermute(v, "dp", [(j, j ^ k) for j in range(data)])

    def core_half(v):
        width = v.shape[1] // 2
        return jnp.where(core == 0, v[:, :width], v[:, width:])

    def after(v, *others):
        return lax.optimization_barrier((v, others))[0]

    def from_dp(v):
        return [dp_xor(v, k) for k in range(1, data)]

    def dp_part(w):
        rows = w.shape[0] // data
        return lax.dynamic_slice_in_dim(w, my_dp * rows, rows, axis=0)

    own = [w_gate[0], w_up[0], w_down[0]]
    quarter = jnp.concatenate(
        [jnp.concatenate([dp_part(own[0]), dp_part(own[1])], axis=1), dp_part(own[2])], axis=0
    )
    part_rows = quarter.shape[0] * 25 // 36
    crossed_one = across(quarter[:part_rows])

    token_half = token_rows // 2
    cot_first = [shift(cotangent[:token_half], k) for k in range(1, half)]

    qkv_own = [w_query, key_weight, value_weight]
    qkv_half = (query_width + 2 * kv_width) // 2
    mine = jnp.concatenate([core_half(jnp.concatenate(qkv_own, axis=1)), core_half(w_out)], axis=1)
    near_one, near_two = dp_xor(mine, 1), dp_xor(mine, 2)
    tall = mine.shape[0] // 2
    got = [near_one, near_two, dp_xor(near_two[:tall], 1), dp_xor(near_one[tall:], 2)]
    slots = pair_slots(routes, pair_order[0], experts, capacity)
    slot_columns = jnp.pad(
        jnp.concatenate([slots // 128, slots % 128], axis=1).astype(f32),
        ((0, 0), (3 * experts, extra - 5 * experts)),
    )
    router_weight = jnp.pad(w_router, ((0, 0), (0, extra - experts)))
    router_weight_three = jnp.pad(jnp.concatenate([w_router] * 3, axis=1), ((0, 0), (0, extra - 3 * experts)))
    gain_one = norm_attn.reshape(1, features)
    gain_two = norm_moe.reshape(1, features)
    segment_columns = document_index.reshape(token_rows, 1)
    quarter_rest, cot_rest = quarter[part_rows:], cotangent[token_half:]
    ready, gain_one, gain_two, segment_columns, quarter_rest, cot_rest = after(
        (got, gain_one, gain_two, segment_columns, quarter_rest, cot_rest),
        crossed_one, cot_first, slot_columns, router_weight, router_weight_three,
    )
    pieces = [(v, swap(v)) for v in ready]
    crossed_two = across(quarter_rest)
    cot_second = [shift(after(cot_rest, pieces), k) for k in range(1, half)]
    cot_other = swap(after(cotangent, pieces))
    cot_first_other = [swap(after(v, pieces)) for v in cot_first]
    partner_one = lax.all_gather(after(crossed_one, pieces), "dp", axis=0, tiled=True)

    normed_one, qkv, mixture, totals = attend_call(
        place, tokens, gain_one, document_index, segment_columns, padding_token_mask, qkv_own, pieces
    )
    hidden_one, payload = route_call(
        place, after(mixture, crossed_two, cot_second, cot_other, cot_first_other), tokens, gain_two, router_weight,
        slot_columns, [w_out], pieces, experts,
    )

    payload_other = swap(payload)
    payload_far_same = [shift(payload, k) for k in range(1, half)]
    total_rows = chips // 2 * 2 * slot_rows

    two = after(crossed_two, payload_other)
    partner = [partner_one, two] + from_dp(two)
    spread = tuple((0, d * part_rows, part_rows, (False, d), 0) for d in range(data))
    spread += tuple((1 + k, 0, quarter.shape[0] - part_rows, (True, k), part_rows) for k in range(data))

    def rows_of(slot, sources, weights, prev, saved, base, cost=COST):
        return expert_call(
            hosted, (slot,), sources, weights, prev, saved, base, total_rows, experts, slot_rows, data, spread, cost
        )

    one = [(payload, payload_other, (cotangent,), (cot_other,))]
    near = rows_of(0, one, own, [], [], 0)
    near_saved = near[4:]
    near = rows_of(1, one, partner, near[:4], [], 0, LONG)
    payload_far_other = [swap(after(v, near[0])) for v in payload_far_same]
    cot_second_other = [swap(after(v, near[0])) for v in cot_second]
    many = list(zip(
        payload_far_same, payload_far_other, zip(cot_first, cot_second), zip(cot_first_other, cot_second_other)
    ))
    many = [(same, other, tuple(c_same), tuple(c_other)) for same, other, c_same, c_other in many]
    far = rows_of(1, many, partner, [], near[4:], 2 * slot_rows)
    partner_local = weight_gradient_call(far[4:], data)
    far = rows_of(0, many, own, far[:4], near_saved, 2 * slot_rows)
    saved = far[4:]

    def returned(near_same, near_other, far_same, far_other):
        sums = [
            (far_same[k].astype(f32) + swap(far_other[k]).astype(f32)).astype(bf16)
            for k in range(half - 1)
        ]
        return [near_same[0], swap(near_other[0])], sums

    def scattered(v):
        return lax.psum_scatter(v, "dp", scatter_dimension=0, tiled=True)

    partner_sum = scattered(partner_local)
    backs, back_sums = returned(near[2], near[3], far[2], far[3])
    backs += [shift(v, half - 1 - k) for k, v in enumerate(back_sums)]
    outs, out_sums = returned(near[0], after(near[1], back_sums), far[0], after(far[1], back_sums))
    own_local = weight_gradient_call([after(saved[0], back_sums, out_sums), *saved[1:]], data)
    own_sum = scattered(after(own_local, partner_sum, backs))
    grad_hidden, given, out_keep, out_give, local_norm_moe, local_router = branch_call(
        place, cotangent, hidden_one, payload, gain_two, router_weight_three, mixture, backs,
        [w_out], pieces, experts,
    )

    stages = chips.bit_length() - 1

    def chip_stage(part, stage, *others):
        there = stage < stages
        step = 1 << (stage if there else 2 * stages - 1 - stage)
        bit = lax.rem(me // 2 // step, 2)
        if there:
            size = part.shape[0] // 2
            keep = lax.dynamic_slice_in_dim(part, bit * size, size, axis=0)
            give = lax.dynamic_slice_in_dim(part, (1 - bit) * size, size, axis=0)
            return (keep.astype(f32) + chip_xor(after(give, *others), step).astype(f32)).astype(bf16)
        other = chip_xor(after(part, *others), step)
        return jnp.concatenate([jnp.where(bit == 0, part, other), jnp.where(bit == 0, other, part)], axis=0)

    rows = partner_sum.shape[0]
    thirds = jnp.split(partner_sum, (11 * rows // 36, 22 * rows // 36, 31 * rows // 36), axis=0)
    arrived_one = across(after(thirds[0], backs))
    arrived_two = across(after(thirds[1], arrived_one, grad_hidden))
    given, out_give = after((given, out_give), arrived_one)
    cuts = [0, 9 * token_rows // 40, 18 * token_rows // 40, 27 * token_rows // 40, token_rows]

    def out_parts(index, *others):
        rows = slice(cuts[index], cuts[index + 1])
        return [shift(after(v[rows], *others), half - 1 - k) for k, v in enumerate(out_sums)]

    outs_one = out_parts(0, backs)
    outs_two = out_parts(1, arrived_one, grad_hidden, outs_one)
    given, out_give = after((given, out_give), outs_one)
    out_got = swap(out_give)
    grad_qkv, qkv_keep, qkv_give = attend_back_call(
        place, document_index, segment_columns, padding_token_mask, qkv, totals, given, normed_one
    )
    qkv_give, out_got = after((qkv_give, out_got), arrived_two, outs_two)
    arrived_three = across(after(thirds[2], arrived_two))
    outs_three = out_parts(2, arrived_two, outs_two)
    out_folds = fold_first(place, out_keep, out_got, data)
    out_arrived = [dp_xor(out_folds[1], 2), dp_xor(out_folds[3], 1)]
    qkv_folds = fold_first(place, qkv_keep, swap(qkv_give), data)
    qkv_arrived = [dp_xor(qkv_folds[1], 2), dp_xor(qkv_folds[3], 1)]
    grad_tokens, local_norm_attn = input_grad_call(
        place, tokens, gain_one, after(grad_qkv, qkv_folds, out_folds, arrived_three, outs_three), grad_hidden, qkv_own, pieces
    )
    arrived_four = across(after(thirds[3], arrived_three))
    qkv_arrived, out_arrived = after((qkv_arrived, out_arrived), grad_tokens)
    local_router = local_router[:3 * experts].reshape(3, experts, features).sum(0)
    small = jnp.concatenate([local_router, local_norm_attn, local_norm_moe], axis=0)
    def folded(keep_a, give_a, keep_b, give_b):
        got_a, got_b = dp_xor(give_a, 1), dp_xor(give_b, 2)
        return jnp.concatenate([
            (keep.astype(f32) + got.astype(f32)).astype(bf16) for keep, got in ((keep_a, got_a), (keep_b, got_b))
        ], axis=1)

    qkv_folds = fold_second(place, qkv_folds[0], qkv_arrived[0], qkv_folds[2], qkv_arrived[1])
    outs_four = out_parts(3, grad_tokens)
    qkv_part = folded(*qkv_folds)
    out_part = folded(*fold_second(place, out_folds[0], out_arrived[0], out_folds[2], out_arrived[1]))
    arrived = jnp.concatenate([arrived_one, arrived_two, arrived_three, arrived_four], axis=0)
    expert_sum = (own_sum.astype(f32) + arrived.astype(f32)).astype(bf16)
    expert_sum, out_part, qkv_part = after((expert_sum, out_part, qkv_part))
    whole = lax.all_gather(expert_sum, "dp", axis=0, tiled=True)
    for stage in range(2 * stages):
        ahead = chip_stage(qkv_part, stage, *([outs_four] if stage == 2 else []))
        if stage:
            out_part = chip_stage(out_part, stage - 1, qkv_part)
        qkv_part = ahead
        if stage == 1:
            small, qkv_part = after((small, qkv_part))
    outs += [jnp.concatenate(v, axis=0) for v in zip(outs_one, outs_two, outs_three, outs_four)]
    routed = outs[0].astype(f32)
    for part in outs[1:]:
        routed = routed + part.astype(f32)
    block_out = (hidden_one + routed).astype(bf16)
    out_part = chip_stage(out_part, 2 * stages - 1, qkv_part)
    qkv_other = swap(qkv_part)
    small = small + swap(small)
    arrived = [dp_xor(small, k) for k in range(1, data)]
    grad_query, grad_key, grad_value = joined(
        place, qkv_part, qkv_other, (query_width, kv_width, kv_width)
    )
    arrived, grad_query, block_out = after((arrived, grad_query, block_out))
    for value in arrived:
        small = small + value
    (grad_out,) = joined(place, out_part, swap(out_part), (features,))
    if chips <= 4:
        arrived, grad_out = after(([chip_xor(small, k) for k in range(1, chips)], grad_out))
        for value in arrived:
            small = small + value
    else:
        for step in range(stages):
            small = small + chip_xor(small, 1 << step)
    whole, small, grad_out = after((whole, small, grad_out))
    grad_gate, grad_up, grad_down = widened(whole, data)
    grad_router = small[:experts].T
    grad_norm_attn = small[experts]
    grad_norm_moe = small[experts + 1]
    return (
        block_out,
        grad_tokens,
        grad_norm_attn,
        grad_norm_moe,
        grad_query,
        grad_key,
        grad_value,
        grad_out,
        grad_router,
        grad_gate[None],
        grad_up[None],
        grad_down[None],
    )


def solution(mesh):
    rows = P(("dp", "expert"), None)
    over_dp = P("dp", None)
    over_expert = P("expert", None, None)
    return jax.shard_map(
        body,
        mesh=mesh,
        in_specs=(
            rows, rows, P(), P(), over_dp, over_dp, over_dp, over_dp, P(),
            over_expert, over_expert, over_expert, rows, rows, rows, rows,
        ),
        out_specs=(
            rows, rows, P(), P(), over_dp, over_dp, over_dp, over_dp, P(),
            over_expert, over_expert, over_expert,
        ),
        check_vma=False,
    )
```

```python
import functools

import jax
import jax.numpy as jnp
from jax import lax
from jax.experimental import pallas as pl
from jax.experimental.pallas import tpu as pltpu
from jax.sharding import PartitionSpec as P

bf16 = jnp.bfloat16
f32 = jnp.float32
MIB = 1024 * 1024
LONG = pl.CostEstimate(flops=16 << 30, bytes_accessed=30 * MIB, transcendentals=0)
COST = pl.CostEstimate(flops=1000, bytes_accessed=1000, transcendentals=0)
NT_DIMS = (((1,), (1,)), ((), ()))
TN_DIMS = (((0,), (0,)), ((), ()))


def mm(a, b):
    return jnp.dot(a, b, preferred_element_type=f32)


def mm_nt(a, b):
    return lax.dot_general(a, b, NT_DIMS, preferred_element_type=f32)


def mm_tn(a, b):
    return lax.dot_general(a, b, TN_DIMS, preferred_element_type=f32)


def split_three(v):
    high = v.astype(bf16)
    rest = v - high.astype(f32)
    middle = rest.astype(bf16)
    low = (rest - middle.astype(f32)).astype(bf16)
    return high, middle, low


def lanes(start, size):
    return pl.ds(pl.multiple_of(start, 128), size)


def specs(kinds):
    table = {"s": pltpu.SMEM, "v": pltpu.VMEM, "a": pl.ANY}
    return [pl.BlockSpec(memory_space=table[kind]) for kind in kinds]


def params():
    return pltpu.CompilerParams(vmem_limit_bytes=60 * MIB)


def expert_kernel(experts, slots, base, data, pieces, chunks, cuts, n_weights, n_prev, n_saved, rows, *refs):
    count = len(slots)
    each = 2 + 2 * len(cuts)
    hosted, sources, refs = refs[0], refs[1:1 + each * chunks], refs[1 + each * chunks:]
    sources = [sources[each * i:each * (i + 1)] for i in range(chunks)]
    weight_refs, refs = refs[:n_weights], refs[n_weights:]
    prev, refs = refs[:n_prev], refs[n_prev + n_saved:]
    po_same, po_other, pg_same, pg_other, x_out, gp_out, h_out, gg_out, gu_out = refs[:9]
    (wg, wu, wd, nbuf, cbuf, x, gp, gc, sc, h, gg, gu, dmat, dtmat, gcol, vcol, tail_t,
     w_sem, in_sem, act_sem, p_sem) = refs[9:]
    tokens, features = sources[0][0].shape[0], sources[0][2].shape[1]
    extra = sources[0][0].shape[1] - features
    ff = wg.shape[2]
    wide = features // 2
    tail = slice(features, features + extra)

    weight_copies = []
    taken = 0
    for place, slot in enumerate(slots):
        if slot == 0:
            pairs = list(zip(weight_refs[taken:taken + 3], (wg.at[place], wu.at[place], wd.at[place])))
            taken += 3
        else:
            tall_f, tall_h = features // data, ff // data
            pairs = []
            for index, begin, size, whose, first in pieces:
                ref = weight_refs[taken + index]
                source = jnp.bitwise_xor(hosted[2], whose[1]) if whose[0] else whose[1]
                wide_rows = max(0, min(size, tall_f - first))
                if wide_rows:
                    at = pl.ds(pl.multiple_of(source * tall_f + first, 16), wide_rows)
                    pairs += [
                        (ref.at[pl.ds(begin, wide_rows), pl.ds(0, ff)], wg.at[place, at]),
                        (ref.at[pl.ds(begin, wide_rows), pl.ds(ff, ff)], wu.at[place, at]),
                    ]
                if wide_rows < size:
                    at = pl.ds(pl.multiple_of(source * tall_h + first + wide_rows - tall_f, 16), size - wide_rows)
                    pairs.append((ref.at[pl.ds(begin + wide_rows, size - wide_rows)], wd.at[place, at]))
            taken += 1 + max(piece[0] for piece in pieces)
        weight_copies.append([
            pltpu.make_async_copy(source, target, w_sem.at[place, i])
            for i, (source, target) in enumerate(pairs)
        ])

    def input_copies(index, q):
        pairs = [(sources[index][q], nbuf.at[q])]
        for part, (first, size) in zip(sources[index][2 + q * len(cuts):], cuts):
            pairs.append((part, cbuf.at[q, pl.ds(first, size)]))
        return [pltpu.make_async_copy(source, target, in_sem.at[q, i]) for i, (source, target) in enumerate(pairs)]

    def act_copies(chunk, place):
        at = pl.ds(pl.multiple_of(base + chunk * 2 * rows, 16), 2 * rows)
        return [
            pltpu.make_async_copy(source.at[place], target.at[place, at], act_sem.at[place, i])
            for i, (source, target) in enumerate(
                ((x, x_out), (gp, gp_out), (h, h_out), (gg, gg_out), (gu, gu_out)))
        ]

    def partial_copies(chunk, q, tile):
        wide_cols = pl.ds(0, wide) if tile == 0 else pl.ds(wide, wide + extra)
        cols = pl.ds(tile * wide, wide)
        return (
            pltpu.make_async_copy(
                nbuf.at[q, :, wide_cols], (pg_same, pg_other)[q].at[chunk, :, wide_cols], p_sem.at[q, tile, 0]),
            pltpu.make_async_copy(cbuf.at[q, :, cols], (po_same, po_other)[q].at[chunk, :, cols], p_sem.at[q, tile, 1]),
        )

    def dispatch(q):
        columns = nbuf[q, :, tail].astype(f32)
        tail_t[...] = columns.T
        token_lane = lax.broadcasted_iota(jnp.int32, (tokens, extra), 1)
        wanted = lax.broadcasted_iota(jnp.int32, (tokens, count * rows), 1)
        slot_cols = []
        for place in range(count):
            expert = hosted[slots[place]]
            row = (tail_t[pl.ds(3 * experts + expert, 1), :] * 128.0
                   + tail_t[pl.ds(4 * experts + expert, 1), :] - 1.0).astype(jnp.int32)
            hit = lax.broadcasted_iota(jnp.int32, (rows, tokens), 0) == row
            dmat[q, place * rows:(place + 1) * rows, :] = jnp.where(hit, 1.0, 0.0).astype(bf16)
            factor = jnp.where(token_lane == 3 * experts + expert, 128.0, 0.0)
            factor = jnp.where(token_lane == 4 * experts + expert, 1.0, factor)
            slot_cols.append(jnp.sum(columns * factor, axis=1, keepdims=True).astype(jnp.int32) - 1)
        target = slot_cols[0]
        if count == 2:
            second = wanted >= rows
            target = jnp.where(second, slot_cols[1], slot_cols[0])
            wanted = jnp.where(second, wanted - rows, wanted)
        dtmat[q] = jnp.where(wanted == target, 1.0, 0.0).astype(bf16)
        parts = mm(dmat[q], nbuf[q, :, tail])
        lane = lax.broadcasted_iota(jnp.int32, (rows, extra), 1)
        for place in range(count):
            expert = hosted[slots[place]]
            mine = (lane == expert) | (lane == expert + experts) | (lane == expert + 2 * experts)
            g = jnp.sum(jnp.where(mine, parts[place * rows:(place + 1) * rows], 0.0), axis=1, keepdims=True)
            gcol[place, q * rows:(q + 1) * rows, :] = jnp.broadcast_to(g, (rows, 128))

        for tile in range(2):
            cols = slice(tile * wide, (tile + 1) * wide)
            found = mm(dmat[q], nbuf[q, :, cols]).astype(bf16)
            cot = mm(dmat[q], cbuf[q, :, cols])
            gc[q, :, cols] = cot.astype(bf16)
            for place in range(count):
                at = slice(q * rows, (q + 1) * rows)
                own = slice(place * rows, (place + 1) * rows)
                x[place, at, cols] = found[own]
                gp[place, at, cols] = (cot[own] * gcol[place, at, 0:1]).astype(bf16)

    def forward_backward(place):
        for q in range(2):
            at = slice(q * rows, (q + 1) * rows)
            gate = mm(x[place, at, :], wg[place])
            up = mm(x[place, at, :], wu[place])
            dh = mm_nt(gp[place, at, :], wd[place])
            sig = 1.0 / (1.0 + jnp.exp(-gate))
            act = gate * sig
            h[place, at, :] = (act * up).astype(bf16)
            gg[place, at, :] = (dh * up * (sig * (1.0 + gate * (1.0 - sig)))).astype(bf16)
            gu[place, at, :] = (dh * act).astype(bf16)

    def produce(place):
        vcol[place] = jnp.zeros(vcol.shape[1:], f32)

        @pl.loop(0, 2)
        def _(tile):
            cols = lanes(tile * wide, wide)
            for q in range(2):
                at = slice(q * rows, (q + 1) * rows)
                own = pl.ds(pl.multiple_of(place * rows, 16), rows)
                produced = mm(h[place, at, :], wd[place, :, cols]).astype(bf16).astype(f32)
                along = produced * gc[q, own, cols].astype(f32)
                folded = along[:, :128]
                for part in range(1, wide // 128):
                    folded = folded + along[:, part * 128:(part + 1) * 128]
                vcol[place, at, :] += folded
                sc[q, own, cols] = (produced * gcol[place, at, 0:1]).astype(bf16)
                back = mm_nt(gg[place, at, :], wg[place, cols, :]) + mm_nt(gu[place, at, :], wu[place, cols, :])
                gc[q, own, cols] = back.astype(bf16)

    def combine(chunk, q):
        at = slice(q * rows, (q + 1) * rows)
        lane = lax.broadcasted_iota(jnp.int32, (rows, extra), 1)
        payload = []
        for place in range(count):
            expert = hosted[slots[place]]
            high, middle, low = split_three(jnp.sum(vcol[place, at, :], axis=1, keepdims=True))
            part = jnp.where(lane == expert, high.astype(f32), 0.0)
            part = jnp.where(lane == expert + experts, middle.astype(f32), part)
            part = jnp.where(lane == expert + 2 * experts, low.astype(f32), part)
            payload.append(part.astype(bf16))
        payload = jnp.concatenate(payload, axis=0) if count > 1 else payload[0]
        tail_sum = mm(dtmat[q], payload)
        if n_prev:
            tail_sum = tail_sum + nbuf[q, :, tail].astype(f32)
        nbuf[q, :, tail] = tail_sum.astype(bf16)

        for tile in range(2):
            cols = slice(tile * wide, (tile + 1) * wide)
            back = mm(dtmat[q], gc[q, :, cols])
            out = mm(dtmat[q], sc[q, :, cols])
            if n_prev:
                back = back + nbuf[q, :, cols].astype(f32)
                out = out + cbuf[q, :, cols].astype(f32)
            nbuf[q, :, cols] = back.astype(bf16)
            cbuf[q, :, cols] = out.astype(bf16)
            for copy in partial_copies(chunk, q, tile):
                copy.start()

    def prev_copies(chunk):
        po0, po1, pg0, pg1 = prev
        return (
            pltpu.make_async_copy(pg0.at[chunk], nbuf.at[0], in_sem.at[0, 0]),
            pltpu.make_async_copy(pg1.at[chunk], nbuf.at[1], in_sem.at[1, 0]),
            pltpu.make_async_copy(po0.at[chunk], cbuf.at[0], in_sem.at[0, 1]),
            pltpu.make_async_copy(po1.at[chunk], cbuf.at[1], in_sem.at[1, 1]),
        )

    late = max(slots) == 0
    for copy in input_copies(0, 0):
        copy.start()
    if not late:
        for copy in input_copies(0, 1):
            copy.start()
        for copies in weight_copies:
            for copy in copies:
                copy.start()

    @pl.loop(0, chunks)
    def _(chunk):
        for copy in input_copies(0, 0):
            copy.wait()

        @pl.when((chunk == 0) & late)
        def _():
            for copy in input_copies(0, 1):
                copy.start()
            for copies in weight_copies:
                for copy in copies:
                    copy.start()

        dispatch(0)
        for copy in input_copies(0, 1):
            copy.wait()
        dispatch(1)
        if n_prev:
            for copy in prev_copies(chunk):
                copy.start()
        for place in range(count):
            @pl.when(chunk == 0)
            def _():
                for copy in weight_copies[place]:
                    copy.wait()

            forward_backward(place)
            for copy in act_copies(chunk, place):
                copy.start()
            produce(place)
        if n_prev:
            for copy in prev_copies(chunk):
                copy.wait()
        for q in range(2):
            combine(chunk, q)
        for place in range(count):
            for copy in act_copies(chunk, place):
                copy.wait()
        for q in range(2):
            for tile in range(2):
                for copy in partial_copies(chunk, q, tile):
                    copy.wait()

        for index in range(1, chunks):
            @pl.when(chunk + 1 == index)
            def _():
                for q in range(2):
                    for copy in input_copies(index, q):
                        copy.start()


def expert_call(hosted, slots, sources, weights, prev, saved, base, total, experts, rows, data, pieces, cost):
    chunks = len(sources)
    tokens, features = sources[0][0].shape[0], sources[0][2][0].shape[1]
    cuts, first = [], 0
    for part in sources[0][2]:
        cuts.append((first, part.shape[0]))
        first += part.shape[0]
    flat = [v for same, other, *parts in sources for v in (same, other, *parts[0], *parts[1])]
    ff = weights[0].shape[1] if slots[0] == 0 else weights[0].shape[1] // 2
    wide_n = sources[0][0].shape[1]
    extra = wide_n - features
    count = len(slots)
    shape = jax.ShapeDtypeStruct
    act_f = shape((count, total, features), bf16)
    act_h = shape((count, total, ff), bf16)
    out_shape = (
        [shape((chunks, tokens, features), bf16)] * 2
        + [shape((chunks, tokens, wide_n), bf16)] * 2
        + [act_f, act_f, act_h, act_h, act_h]
    )
    many = 2 * rows
    first_prev = 1 + len(flat) + len(weights)
    first_saved = first_prev + len(prev)
    return pl.pallas_call(
        functools.partial(
            expert_kernel, experts, slots, base, data, pieces, chunks, tuple(cuts), len(weights), len(prev), len(saved), rows),
        out_shape=out_shape,
        in_specs=specs("s" + "a" * (len(flat) + len(weights) + len(prev) + len(saved))),
        out_specs=specs("a" * 9),
        input_output_aliases={
            **{first_prev + i: i for i in range(len(prev))},
            **{first_saved + i: 4 + i for i in range(len(saved))},
        },
        scratch_shapes=[
            pltpu.VMEM((count, features, ff), bf16),
            pltpu.VMEM((count, features, ff), bf16),
            pltpu.VMEM((count, ff, features), bf16),
            pltpu.VMEM((2, tokens, wide_n), bf16),
            pltpu.VMEM((2, tokens, features), bf16),
            pltpu.VMEM((count, many, features), bf16),
            pltpu.VMEM((count, many, features), bf16),
            pltpu.VMEM((2, count * rows, features), bf16),
            pltpu.VMEM((2, count * rows, features), bf16),
            pltpu.VMEM((count, many, ff), bf16),
            pltpu.VMEM((count, many, ff), bf16),
            pltpu.VMEM((count, many, ff), bf16),
            pltpu.VMEM((2, count * rows, tokens), bf16),
            pltpu.VMEM((2, tokens, count * rows), bf16),
            pltpu.VMEM((count, many, 128), f32),
            pltpu.VMEM((count, many, 128), f32),
            pltpu.VMEM((extra, tokens), f32),
            pltpu.SemaphoreType.DMA((count, 3 * max(1, len(pieces)))),
            pltpu.SemaphoreType.DMA((2, 1 + len(cuts))),
            pltpu.SemaphoreType.DMA((count, 5)),
            pltpu.SemaphoreType.DMA((2, 2, 2)),
        ],
        compiler_params=params(),
        cost_estimate=cost,
        name="expert_rows",
    )(hosted, *flat, *weights, *prev, *saved)


def weight_gradient_kernel(data, x_in, gg_in, gu_in, h_in, gp_in, out, x, ggu, h, gp, wide, down, sem, out_sem):
    features, ff = x.shape[1], h.shape[1]
    tall = 512
    tall_f, tall_h = features // data, ff // data
    step = tall_f + tall_h
    loads = [
        pltpu.make_async_copy(source.at[0], target, sem.at[i])
        for i, (source, target) in enumerate((
            (gg_in, ggu.at[:, pl.ds(0, ff)]), (gu_in, ggu.at[:, pl.ds(ff, ff)]), (x_in, x), (h_in, h), (gp_in, gp)))
    ]
    for copy in loads[:3]:
        copy.start()
    stores = [
        pltpu.make_async_copy(wide.at[pl.ds(d * tall_f, tall_f)], out.at[pl.ds(d * step, tall_f)], out_sem.at[2 * d])
        for d in range(data)
    ] + [
        pltpu.make_async_copy(down.at[pl.ds(d * tall_h, tall_h)], out.at[pl.ds(d * step + tall_f, tall_h)],
                              out_sem.at[2 * d + 1])
        for d in range(data)
    ]
    for copy in loads[:3]:
        copy.wait()
    for copy in loads[3:]:
        copy.start()

    @pl.loop(0, features // tall)
    def _(tile):
        at = pl.ds(pl.multiple_of(tile * tall, tall), tall)
        wide[at, :] = mm_tn(x[:, lanes(tile * tall, tall)], ggu[...]).astype(bf16)

    for copy in stores[:data]:
        copy.start()
    for copy in loads[3:]:
        copy.wait()

    @pl.loop(0, ff // (tall // 2))
    def _(tile):
        at = pl.ds(pl.multiple_of(tile * 256, 256), 256)
        down[at, :] = mm_tn(h[:, lanes(tile * 256, 256)], gp[...]).astype(bf16)

    for copy in stores[data:]:
        copy.start()
    for copy in stores:
        copy.wait()


def weight_gradient_call(saved, data):
    x, gp, h, gg, gu = saved
    slots, features, ff = x.shape[1], x.shape[2], h.shape[2]
    return pl.pallas_call(
        functools.partial(weight_gradient_kernel, data),
        out_shape=jax.ShapeDtypeStruct((features + ff, 2 * ff), bf16),
        in_specs=specs("aaaaa"),
        out_specs=pl.BlockSpec(memory_space=pl.ANY),
        scratch_shapes=[
            pltpu.VMEM((slots, features), bf16),
            pltpu.VMEM((slots, 2 * ff), bf16),
            pltpu.VMEM((slots, ff), bf16),
            pltpu.VMEM((slots, features), bf16),
            pltpu.VMEM((features, 2 * ff), bf16),
            pltpu.VMEM((ff, features), bf16),
            pltpu.SemaphoreType.DMA((5,)),
            pltpu.SemaphoreType.DMA((2 * data,)),
        ],
        compiler_params=params(),
        cost_estimate=COST,
        name="expert_weight_gradients",
    )(x, gg, gu, h, gp)


def widened_kernel(whole, gate, up, down):
    ff = gate.shape[1]
    third = lax.rem(pl.program_id(0), 3)

    @pl.when(third < 2)
    def _():
        gate[...] = whole[:, :ff].astype(f32)
        up[...] = whole[:, ff:].astype(f32)

    @pl.when(third == 2)
    def _():
        down[...] = whole[...].astype(f32)


def widened(whole, data):
    rows, features = whole.shape[0] // data, whole.shape[1]
    ff = features // 2
    unit = rows // 3

    def wide_block(i):
        return (i // 3 * 2 + jnp.minimum(i % 3, 1), 0)

    return pl.pallas_call(
        widened_kernel,
        grid=(3 * data,),
        in_specs=[pl.BlockSpec((unit, features), lambda i: (i, 0))],
        out_specs=[
            pl.BlockSpec((unit, ff), wide_block),
            pl.BlockSpec((unit, ff), wide_block),
            pl.BlockSpec((unit, features), lambda i: (i // 3, 0)),
        ],
        out_shape=[
            jax.ShapeDtypeStruct((2 * data * unit, ff), f32),
            jax.ShapeDtypeStruct((2 * data * unit, ff), f32),
            jax.ShapeDtypeStruct((data * unit, features), f32),
        ],
        compiler_params=params(),
        cost_estimate=COST,
        name="widened",
    )(whole)


epsilon = 1e-06
neg_fill = -1e30
QUERY_HEADS = 12
KEY_VALUE_HEADS = 2
HEAD_SIZE = 128
GROUP = QUERY_HEADS // KEY_VALUE_HEADS
SCORE_SCALE = HEAD_SIZE ** (-0.5)


def piece_copies(place, own, pieces, begin, weight, sem):
    rows, half = own[0].shape[0], weight.shape[1] // 2
    mine, core = place[0], place[1]
    copies = []
    column = 0
    for part in own:
        at = weight.at[pl.ds(pl.multiple_of(mine * rows, 16), rows), pl.ds(column, part.shape[1])]
        copies.append(pltpu.make_async_copy(part, at, sem.at[len(copies)]))
        column += part.shape[1]
    for (k, skip), pair in zip(((1, 0), (2, 0), (3, 0), (3, rows // 2)), pieces):
        first = pl.multiple_of(jnp.bitwise_xor(mine, k) * rows + skip, 16)
        for part, which in zip(pair, (core, 1 - core)):
            at = weight.at[pl.ds(first, part.shape[0]), lanes(which * half, half)]
            copies.append(pltpu.make_async_copy(part.at[:, pl.ds(begin, half)], at, sem.at[len(copies)]))
    return copies


def attention_mask(segment_row, segment_col, pad_row, first, size, span):
    row = first + lax.broadcasted_iota(jnp.int32, (size, span), 0)
    col = lax.broadcasted_iota(jnp.int32, (size, span), 1)
    same = segment_col[first:first + size, :] == segment_row[:, :span]
    return same & (((pad_row[:, :span] == 1) & (col < row)) | (col == row))


def stacked(ref, rows, c):
    return jnp.concatenate(
        [ref[rows, lanes((c * GROUP + g) * HEAD_SIZE, HEAD_SIZE)] for g in range(GROUP)], axis=0
    )


def attend_kernel(
    n_own, n_pairs, tokens_total, block,
    place, tokens, gain, segment_row, segment_col, pad_row, *refs,
):
    own = refs[:n_own]
    flat = refs[n_own:n_own + 2 * n_pairs]
    pieces = [(flat[2 * k], flat[2 * k + 1]) for k in range(n_pairs)]
    normed, qkv, mixture, totals, weight, sem = refs[n_own + 2 * n_pairs:]
    copies = piece_copies(place, own, pieces, 0, weight, sem)
    for copy in copies:
        copy.start()
    width = QUERY_HEADS * HEAD_SIZE
    kv_width = KEY_VALUE_HEADS * HEAD_SIZE
    source = tokens[...].astype(f32)
    inverse = lax.rsqrt(jnp.mean(source * source, axis=1, keepdims=True) + epsilon)
    normed[...] = (source * inverse * gain[...]).astype(bf16)
    for copy in copies:
        copy.wait()
    wide = 512

    @pl.loop(0, qkv.shape[1] // wide)
    def _(tile):
        cols = lanes(tile * wide, wide)
        qkv[:, cols] = mm(normed[...], weight[:, cols]).astype(bf16)

    totals[...] = jnp.zeros_like(totals)
    segment_of_row, segment_of_col, pad = segment_row[...], segment_col[...], pad_row[...]

    @pl.loop(0, KEY_VALUE_HEADS)
    def _(c):
        for first in range(0, tokens_total, block):
            span = first + block
            rows = slice(first, span)
            mask = attention_mask(segment_of_row, segment_of_col, pad, first, block, span)
            keys = qkv[:span, lanes(width + c * HEAD_SIZE, HEAD_SIZE)]
            values = qkv[:span, lanes(width + kv_width + c * HEAD_SIZE, HEAD_SIZE)]
            scores = mm_nt(stacked(qkv, rows, c), keys) * SCORE_SCALE
            lane = lax.broadcasted_iota(jnp.int32, (block, 128), 1)
            stats = totals[rows, :]
            weights = []
            for g in range(GROUP):
                part = jnp.where(mask, scores[g * block:(g + 1) * block], neg_fill)
                top = jnp.max(part, axis=1, keepdims=True)
                raised = jnp.exp(part - top)
                total = jnp.sum(raised, axis=1, keepdims=True)
                stats = jnp.where(lane == c * GROUP + g, top + jnp.log(total), stats)
                weights.append((raised * (1.0 / total)).astype(bf16))
            totals[rows, :] = stats
            mixed = mm(jnp.concatenate(weights, axis=0), values).astype(bf16)
            for g in range(GROUP):
                mixture[rows, lanes((c * GROUP + g) * HEAD_SIZE, HEAD_SIZE)] = mixed[g * block:(g + 1) * block]


def attend_call(place, tokens, gain, segments, segment_columns, pads, own, pieces):
    rows, features = tokens.shape
    width = (QUERY_HEADS + 2 * KEY_VALUE_HEADS) * HEAD_SIZE
    mixed = QUERY_HEADS * HEAD_SIZE
    flat = [part for pair in pieces for part in pair]
    shape = jax.ShapeDtypeStruct
    return pl.pallas_call(
        functools.partial(attend_kernel, len(own), len(pieces), rows, 128),
        out_shape=[
            shape((rows, features), bf16), shape((rows, width), bf16), shape((rows, mixed), bf16),
            shape((rows, 128), f32),
        ],
        in_specs=specs("s" + "v" * 5 + "a" * (len(own) + len(flat))),
        out_specs=specs("vvvv"),
        scratch_shapes=[
            pltpu.VMEM((features, width), bf16),
            pltpu.SemaphoreType.DMA((len(own) + len(flat),)),
        ],
        compiler_params=params(),
        cost_estimate=COST,
        name="attend",
    )(place, tokens, gain, segments, segment_columns, pads, *own, *flat)


def attend_back_kernel(tokens_total, block, place, segment_row, segment_col, pad_row, qkv, totals, given, normed_in,
                       grad_out, keep_out, give_out, grad_keys, grad_values, normed, grad, keep, give, sem, out_sem):
    width = QUERY_HEADS * HEAD_SIZE
    kv_width = KEY_VALUE_HEADS * HEAD_SIZE
    segment_of_row, segment_of_col, pad = segment_row[...], segment_col[...], pad_row[...]
    normed_load = pltpu.make_async_copy(normed_in, normed, sem)
    normed_load.start()

    @pl.loop(0, KEY_VALUE_HEADS)
    def _(c):
        grad_keys[...] = jnp.zeros_like(grad_keys)
        grad_values[...] = jnp.zeros_like(grad_values)
        for first in range(0, tokens_total, block):
            span = first + block
            rows = slice(first, span)
            mask = attention_mask(segment_of_row, segment_of_col, pad, first, block, span)
            keys = qkv[:span, lanes(width + c * HEAD_SIZE, HEAD_SIZE)]
            values = qkv[:span, lanes(width + kv_width + c * HEAD_SIZE, HEAD_SIZE)]
            queries = stacked(qkv, rows, c)
            arrived = stacked(given, rows, c)
            scores = mm_nt(queries, keys) * SCORE_SCALE
            grad_weights = mm_nt(arrived, values)
            lane = lax.broadcasted_iota(jnp.int32, (block, 128), 1)
            stats = totals[rows, :]
            weights, grad_scores = [], []
            for g in range(GROUP):
                at = slice(g * block, (g + 1) * block)
                total = jnp.sum(jnp.where(lane == c * GROUP + g, stats, 0.0), axis=1, keepdims=True)
                probs = jnp.exp(jnp.where(mask, scores[at], neg_fill) - total)
                weights.append(probs.astype(bf16))
                dw = grad_weights[at]
                mean = jnp.sum(probs * dw, axis=1, keepdims=True)
                grad_scores.append((probs * (dw - mean)).astype(bf16))
            weights = jnp.concatenate(weights, axis=0)
            grad_scores = jnp.concatenate(grad_scores, axis=0)
            grad_queries = (mm(grad_scores, keys) * SCORE_SCALE).astype(bf16)
            for g in range(GROUP):
                grad[rows, lanes((c * GROUP + g) * HEAD_SIZE, HEAD_SIZE)] = grad_queries[g * block:(g + 1) * block]
            grad_keys[:span, :] += mm_tn(grad_scores, queries)
            grad_values[:span, :] += mm_tn(weights, arrived)
        grad[:, lanes(width + c * HEAD_SIZE, HEAD_SIZE)] = (grad_keys[...] * SCORE_SCALE).astype(bf16)
        grad[:, lanes(width + kv_width + c * HEAD_SIZE, HEAD_SIZE)] = grad_values[...].astype(bf16)

    grad_store = pltpu.make_async_copy(grad, grad_out, out_sem.at[0])
    grad_store.start()
    normed_load.wait()
    tall = 256

    def stores(tile):
        at = pl.ds(pl.multiple_of(tile * tall, tall), tall)
        return (
            pltpu.make_async_copy(keep.at[at], keep_out.at[at], out_sem.at[1 + 2 * tile]),
            pltpu.make_async_copy(give.at[at], give_out.at[at], out_sem.at[2 + 2 * tile]),
        )

    @pl.loop(0, normed.shape[1] // tall)
    def _(tile):
        cols = lanes(tile * tall, tall)
        at = pl.ds(pl.multiple_of(tile * tall, tall), tall)
        for core, out in ((place[1], keep), (1 - place[1], give)):
            out[at, :] = mm_tn(normed[:, cols], grad[:, lanes(core * keep.shape[1], keep.shape[1])]).astype(bf16)
        for copy in stores(tile):
            copy.start()

    grad_store.wait()

    @pl.loop(0, normed.shape[1] // tall)
    def _(tile):
        for copy in stores(tile):
            copy.wait()


def attend_back_call(place, segments, segment_columns, pads, qkv, totals, given, normed):
    rows, width = qkv.shape
    features = normed.shape[1]
    shape = jax.ShapeDtypeStruct
    return pl.pallas_call(
        functools.partial(attend_back_kernel, rows, 128),
        out_shape=[shape((rows, width), bf16)] + [shape((features, width // 2), bf16)] * 2,
        in_specs=specs("s" + "v" * 6 + "a"),
        out_specs=specs("aaa"),
        scratch_shapes=[
            pltpu.VMEM((rows, HEAD_SIZE), f32),
            pltpu.VMEM((rows, HEAD_SIZE), f32),
            pltpu.VMEM((rows, features), bf16),
            pltpu.VMEM((rows, width), bf16),
            pltpu.VMEM((features, width // 2), bf16),
            pltpu.VMEM((features, width // 2), bf16),
            pltpu.SemaphoreType.DMA,
            pltpu.SemaphoreType.DMA((1 + 2 * (features // 256),)),
        ],
        compiler_params=params(),
        cost_estimate=COST,
        name="attend_back",
    )(place, segments, segment_columns, pads, qkv, totals, given, normed)


def route_kernel(experts, n_own, n_pairs, place, mixture, tokens, gain, router_weight, slots, *refs):
    own = refs[:n_own]
    flat = refs[n_own:n_own + 2 * n_pairs]
    pieces = [(flat[2 * k], flat[2 * k + 1]) for k in range(n_pairs)]
    hidden, payload, weight, sem = refs[n_own + 2 * n_pairs:]
    copies = piece_copies(place, own, pieces, (QUERY_HEADS + 2 * KEY_VALUE_HEADS) * HEAD_SIZE // 2, weight, sem)
    for copy in copies:
        copy.start()
    for copy in copies:
        copy.wait()
    features = tokens.shape[1]
    wide = features // 2

    @pl.loop(0, 2)
    def _(tile):
        cols = lanes(tile * wide, wide)
        hidden[:, cols] = tokens[:, cols].astype(f32) + mm(mixture[...], weight[:, cols])

    value = hidden[...]
    inverse = lax.rsqrt(jnp.mean(value * value, axis=1, keepdims=True) + epsilon)
    payload[:, :features] = (value * inverse * gain[...]).astype(bf16)
    extra = payload.shape[1] - features
    logits = mm(payload[:, :features], router_weight[...])
    lane = lax.broadcasted_iota(jnp.int32, logits.shape, 1)
    logits = jnp.where(lane < experts, logits, neg_fill)
    raised = jnp.exp(logits - jnp.max(logits, axis=1, keepdims=True))
    router = raised / jnp.sum(raised, axis=1, keepdims=True)
    high, middle, low = split_three(router)
    tail = high.astype(f32)
    tail = tail + pltpu.roll(middle.astype(f32), experts, 1)
    tail = tail + pltpu.roll(low.astype(f32), 2 * experts, 1)
    payload[:, features:] = (tail + slots[...]).astype(bf16)


def tail_width(experts):
    return (5 * experts + 127) // 128 * 128


def route_call(place, mixture, tokens, gain, router_weight, slots, own, pieces, experts):
    rows, features = tokens.shape
    extra = tail_width(experts)
    flat = [part for pair in pieces for part in pair]
    shape = jax.ShapeDtypeStruct
    return pl.pallas_call(
        functools.partial(route_kernel, experts, len(own), len(pieces)),
        out_shape=[shape((rows, features), f32), shape((rows, features + extra), bf16)],
        in_specs=specs("s" + "v" * 5 + "a" * (len(own) + len(flat))),
        out_specs=specs("vv"),
        scratch_shapes=[
            pltpu.VMEM((mixture.shape[1], features), bf16),
            pltpu.SemaphoreType.DMA((len(own) + len(flat),)),
        ],
        compiler_params=params(),
        cost_estimate=COST,
        name="route",
    )(place, mixture, tokens, gain, router_weight, slots, *own, *flat)


def branch_kernel(experts, n_back, n_own, n_pairs, place, gain, router_weight, cotangent, hidden, payload, mixture_in, *refs):
    backs, refs = refs[:n_back], refs[n_back:]
    own = refs[:n_own]
    flat = refs[n_own:n_own + 2 * n_pairs]
    pieces = [(flat[2 * k], flat[2 * k + 1]) for k in range(n_pairs)]
    grad_hidden, given, keep_out, give_out, local_gain, local_router = refs[n_own + 2 * n_pairs:][:6]
    (weight, branch, mixture, cot_buf, hidden_buf, payload_buf, back_buf, keep, give, given_buf,
     sem, mix_sem, in_sem, out_sem, sum_sem) = refs[n_own + 2 * n_pairs + 6:]
    parts, short = cot_buf.shape[0], cot_buf.shape[1]
    features = cot_buf.shape[2]
    extra = payload_buf.shape[2] - features
    wide_rows = mixture.shape[1]

    def loads(part):
        at = pl.ds(pl.multiple_of(part * short, 16), short)
        pairs = [(ref, back_buf.at[part, i]) for i, ref in enumerate(backs)]
        pairs += [(hidden, hidden_buf.at[part]), (payload, payload_buf.at[part]), (cotangent, cot_buf.at[part])]
        return [
            pltpu.make_async_copy(source.at[at], target, in_sem.at[part, i]) for i, (source, target) in enumerate(pairs)
        ]

    def hidden_store(part):
        at = pl.ds(pl.multiple_of(part * short, 16), short)
        return pltpu.make_async_copy(hidden_buf.at[part], grad_hidden.at[at], out_sem.at[part])

    for part in range(parts):
        for copy in loads(part):
            copy.start()
    mixture_load = pltpu.make_async_copy(mixture_in, mixture, mix_sem)
    mixture_load.start()
    copies = piece_copies(place, own, pieces, (QUERY_HEADS + 2 * KEY_VALUE_HEADS) * HEAD_SIZE // 2, weight, sem)
    for copy in copies:
        copy.start()
    local_gain[...] = jnp.zeros_like(local_gain)
    local_router[...] = jnp.zeros_like(local_router)

    def three(value):
        width = value.shape[1]
        return (value + pltpu.roll(value, width - experts, 1)
                + pltpu.roll(value, width - 2 * experts, 1))

    @pl.loop(0, parts)
    def _(part):
        for copy in loads(part):
            copy.wait()

        def arrived(cols):
            total = back_buf[part, 0, :, cols].astype(f32)
            for i in range(1, n_back):
                total = total + back_buf[part, i, :, cols].astype(f32)
            return total

        lane = lax.broadcasted_iota(jnp.int32, (short, extra), 1)
        router = jnp.where(lane < experts, three(payload_buf[part, :, features:].astype(f32)), 0.0)
        select = jnp.where(lane < experts, three(arrived(slice(features, features + extra))), 0.0)
        logits = router * (select - jnp.sum(router * select, axis=1, keepdims=True))
        high, middle, low = split_three(logits)
        packed = high.astype(f32) + pltpu.roll(middle.astype(f32), experts, 1)
        packed = (packed + pltpu.roll(low.astype(f32), 2 * experts, 1)).astype(bf16)
        grad_normed = arrived(slice(0, features)) + mm_nt(packed, router_weight[...])
        local_router[...] += mm_tn(packed, payload_buf[part, :, :features])
        value = hidden_buf[part]
        inverse = lax.rsqrt(jnp.mean(value * value, axis=1, keepdims=True) + epsilon)
        along = grad_normed * value
        local_gain[...] += jnp.sum(along * inverse, axis=0, keepdims=True)
        mean = jnp.mean(along * gain[...], axis=1, keepdims=True)
        total = (cot_buf[part].astype(f32) + inverse * (grad_normed * gain[...])
                 - value * (inverse * inverse * inverse * mean))
        hidden_buf[part] = total
        branch[pl.ds(pl.multiple_of(part * short, 16), short), :] = total.astype(bf16)
        hidden_store(part).start()

    mixture_load.wait()
    tall = 256

    def sum_stores(tile):
        at = pl.ds(pl.multiple_of(tile * tall, tall), tall)
        return (
            pltpu.make_async_copy(keep.at[at], keep_out.at[at], sum_sem.at[tile, 0]),
            pltpu.make_async_copy(give.at[at], give_out.at[at], sum_sem.at[tile, 1]),
        )

    @pl.loop(0, wide_rows // tall)
    def _(tile):
        cols = lanes(tile * tall, tall)
        at = pl.ds(pl.multiple_of(tile * tall, tall), tall)
        for core, out in ((place[1], keep), (1 - place[1], give)):
            out[at, :] = mm_tn(mixture[:, cols], branch[:, lanes(core * keep.shape[1], keep.shape[1])]).astype(bf16)
        for copy in sum_stores(tile):
            copy.start()

    for copy in copies:
        copy.wait()
    wide = wide_rows // 2

    def given_store(tile):
        cols = lanes(tile * wide, wide)
        return pltpu.make_async_copy(given_buf.at[:, cols], given.at[:, cols], out_sem.at[parts + tile])

    @pl.loop(0, 2)
    def _(tile):
        at = pl.ds(pl.multiple_of(tile * wide, 128), wide)
        given_buf[:, lanes(tile * wide, wide)] = mm_nt(branch[...], weight[at, :]).astype(bf16)
        given_store(tile).start()

    for part in range(parts):
        hidden_store(part).wait()

    @pl.loop(0, wide_rows // tall)
    def _(tile):
        for copy in sum_stores(tile):
            copy.wait()

    for tile in range(2):
        given_store(tile).wait()


def branch_call(place, cotangent, hidden, payload, gain, router_weight, mixture, backs, own, pieces, experts):
    rows, features = cotangent.shape
    wide_n = payload.shape[1]
    mixed = mixture.shape[1]
    parts = 4
    short = rows // parts
    flat = [part for pair in pieces for part in pair]
    shape = jax.ShapeDtypeStruct
    return pl.pallas_call(
        functools.partial(branch_kernel, experts, len(backs), len(own), len(pieces)),
        out_shape=[
            shape((rows, features), f32), shape((rows, mixed), bf16), shape((mixed, features // 2), bf16),
            shape((mixed, features // 2), bf16), shape((1, features), f32), shape((wide_n - features, features), f32),
        ],
        in_specs=specs("svv" + "a" * (4 + len(backs) + len(own) + len(flat))),
        out_specs=specs("aaaavv"),
        scratch_shapes=[
            pltpu.VMEM((mixed, features), bf16),
            pltpu.VMEM((rows, features), bf16),
            pltpu.VMEM((rows, mixed), bf16),
            pltpu.VMEM((parts, short, features), bf16),
            pltpu.VMEM((parts, short, features), f32),
            pltpu.VMEM((parts, short, wide_n), bf16),
            pltpu.VMEM((parts, len(backs), short, wide_n), bf16),
            pltpu.VMEM((mixed, features // 2), bf16),
            pltpu.VMEM((mixed, features // 2), bf16),
            pltpu.VMEM((rows, mixed), bf16),
            pltpu.SemaphoreType.DMA((len(own) + len(flat),)),
            pltpu.SemaphoreType.DMA,
            pltpu.SemaphoreType.DMA((parts, len(backs) + 3)),
            pltpu.SemaphoreType.DMA((parts + 2,)),
            pltpu.SemaphoreType.DMA((mixed // 256, 2)),
        ],
        compiler_params=params(),
        cost_estimate=COST,
        name="branch",
    )(place, gain, router_weight, cotangent, hidden, payload, mixture, *backs, *own, *flat)


def input_grad_kernel(n_own, n_pairs, place, tokens, gain, grad, grad_hidden, *refs):
    own = refs[:n_own]
    flat = refs[n_own:n_own + 2 * n_pairs]
    pieces = [(flat[2 * k], flat[2 * k + 1]) for k in range(n_pairs)]
    out, local_gain, weight, normed_grad, sem = refs[n_own + 2 * n_pairs:]
    copies = piece_copies(place, own, pieces, 0, weight, sem)
    for copy in copies:
        copy.start()
    for copy in copies:
        copy.wait()
    features = tokens.shape[1]
    wide = features // 2

    @pl.loop(0, 2)
    def _(tile):
        at = pl.ds(pl.multiple_of(tile * wide, 128), wide)
        normed_grad[:, lanes(tile * wide, wide)] = mm_nt(grad[...], weight[at, :])

    value = tokens[...].astype(f32)
    inverse = lax.rsqrt(jnp.mean(value * value, axis=1, keepdims=True) + epsilon)
    grad_normed = normed_grad[...]
    along = grad_normed * value
    local_gain[...] = jnp.sum(along * inverse, axis=0, keepdims=True)
    mean = jnp.mean(along * gain[...], axis=1, keepdims=True)
    out[...] = grad_hidden[...] + inverse * (grad_normed * gain[...]) - value * (inverse * inverse * inverse * mean)


def input_grad_call(place, tokens, gain, grad, grad_hidden, own, pieces):
    rows, features = tokens.shape
    flat = [part for pair in pieces for part in pair]
    shape = jax.ShapeDtypeStruct
    return pl.pallas_call(
        functools.partial(input_grad_kernel, len(own), len(pieces)),
        out_shape=[shape((rows, features), f32), shape((1, features), f32)],
        in_specs=specs("s" + "v" * 4 + "a" * (len(own) + len(flat))),
        out_specs=specs("vv"),
        scratch_shapes=[
            pltpu.VMEM((features, grad.shape[1]), bf16),
            pltpu.VMEM((rows, features), f32),
            pltpu.SemaphoreType.DMA((len(own) + len(flat),)),
        ],
        compiler_params=params(),
        cost_estimate=COST,
        name="input_grad",
    )(place, tokens, gain, grad, grad_hidden, *own, *flat)


def fold_first_kernel(place, keep, got, keep_a, give_a, keep_b, give_b):
    rows, quart = keep_a.shape[1], keep_a.shape[2]
    high, low = lax.div(place[0], 2), lax.rem(place[0], 2)

    def total(high_bit, low_bit, first):
        at = pl.ds(pl.multiple_of((high_bit * 2 + low_bit) * rows, 16), rows)
        cols = slice(first, first + quart)
        return (keep[at, cols].astype(f32) + got[at, cols].astype(f32)).astype(bf16)

    for bit in range(2):
        keep_a[bit] = total(high, bit, 0)
        give_a[bit] = total(1 - high, bit, 0)
        keep_b[bit] = total(bit, low, quart)
        give_b[bit] = total(bit, 1 - low, quart)


def fold_first(place, keep, got, data):
    rows, quart = keep.shape[0] // data, keep.shape[1] // 2
    return pl.pallas_call(
        fold_first_kernel,
        out_shape=[jax.ShapeDtypeStruct((2, rows, quart), bf16)] * 4,
        in_specs=specs("svv"),
        out_specs=specs("vvvv"),
        compiler_params=params(),
        cost_estimate=COST,
        name="fold_first",
    )(place, keep, got)


def fold_second_kernel(place, keep_a, got_a, keep_b, got_b, next_a, give_a, next_b, give_b):
    high, low = lax.div(place[0], 2), lax.rem(place[0], 2)
    for bit, keep, got, kept, give in ((low, keep_a, got_a, next_a, give_a), (high, keep_b, got_b, next_b, give_b)):
        kept[...] = (keep[bit].astype(f32) + got[bit].astype(f32)).astype(bf16)
        give[...] = (keep[1 - bit].astype(f32) + got[1 - bit].astype(f32)).astype(bf16)


def fold_second(place, keep_a, got_a, keep_b, got_b):
    return pl.pallas_call(
        fold_second_kernel,
        out_shape=[jax.ShapeDtypeStruct(keep_a.shape[1:], bf16)] * 4,
        in_specs=specs("svvvv"),
        out_specs=specs("vvvv"),
        compiler_params=params(),
        cost_estimate=COST,
        name="fold_second",
    )(place, keep_a, got_a, keep_b, got_b)


def joined_kernel(place, mine, other, *outs):
    half = mine.shape[1]
    first = 0
    for out in outs:
        done = 0
        while done < out.shape[1]:
            at = first + done
            size = min(out.shape[1] - done, half - at % half)
            cols = slice(at % half, at % half + size)
            own = place[1] == at // half
            out[:, done:done + size] = jnp.where(own, mine[:, cols], other[:, cols]).astype(f32)
            done += size
        first += out.shape[1]


def joined(place, mine, other, widths):
    return pl.pallas_call(
        joined_kernel,
        out_shape=[jax.ShapeDtypeStruct((mine.shape[0], width), f32) for width in widths],
        in_specs=specs("svv"),
        out_specs=specs("v" * len(widths)),
        compiler_params=params(),
        cost_estimate=COST,
        name="joined",
    )(place, mine, other)


def pair_slots(routes, order_row, experts, capacity):
    pair_count = order_row.shape[0]
    place = (
        jnp.zeros((pair_count,), jnp.int32)
        .at[order_row]
        .set(jnp.arange(pair_count, dtype=jnp.int32), unique_indices=True, mode="promise_in_bounds")
        .reshape(routes.shape)
    )
    columns = jnp.arange(experts, dtype=jnp.int32)
    hit = routes[None, :, :] == columns[:, None, None]
    key = jnp.min(jnp.where(hit, place[None], pair_count), axis=2)
    rank = jnp.sum((key[:, None, :] < key[:, :, None]).astype(jnp.int32), axis=2)
    return jnp.where((key < pair_count) & (rank < capacity), rank + 1, 0).T


def body(
    tokens,
    cotangent,
    norm_attn,
    norm_moe,
    w_query,
    key_weight,
    value_weight,
    w_out,
    w_router,
    w_gate,
    w_up,
    w_down,
    document_index,
    padding_token_mask,
    routes,
    pair_order,
):
    token_rows, features = tokens.shape
    top_count = routes.shape[1]
    experts = lax.axis_size("expert")
    data = lax.axis_size("dp")
    chips = experts // 2
    half = chips // 2
    ff = w_gate.shape[2]
    capacity = 9 * token_rows * top_count // (8 * experts)
    slot_rows = (capacity + 15) // 16 * 16
    extra = tail_width(experts)
    query_width = QUERY_HEADS * HEAD_SIZE
    kv_width = KEY_VALUE_HEADS * HEAD_SIZE
    me = lax.axis_index("expert")
    my_dp = lax.axis_index("dp")
    core = lax.rem(me, 2)
    place = jnp.stack([my_dp, core]).astype(jnp.int32)
    hosted = jnp.stack([me, lax.rem(me + experts // 2, experts), my_dp]).astype(jnp.int32)

    def swap(v):
        return lax.ppermute(v, "expert", [(j, j ^ 1) for j in range(experts)])

    def shift(v, k):
        def to(j):
            chip = j // 2
            return ((chip // half) * half + (chip % half + k) % half) * 2 + j % 2

        return lax.ppermute(v, "expert", [(j, to(j)) for j in range(experts)])

    def across(v):
        return lax.ppermute(v, "expert", [(j, (j + experts // 2) % experts) for j in range(experts)])

    def chip_xor(v, step):
        return lax.ppermute(v, "expert", [(j, ((j // 2) ^ step) * 2 + j % 2) for j in range(experts)])

    def dp_xor(v, k):
        return lax.ppermute(v, "dp", [(j, j ^ k) for j in range(data)])

    def core_half(v):
        width = v.shape[1] // 2
        return jnp.where(core == 0, v[:, :width], v[:, width:])

    def after(v, *others):
        return lax.optimization_barrier((v, others))[0]

    def from_dp(v):
        return [dp_xor(v, k) for k in range(1, data)]

    def dp_part(w):
        rows = w.shape[0] // data
        return lax.dynamic_slice_in_dim(w, my_dp * rows, rows, axis=0)

    own = [w_gate[0], w_up[0], w_down[0]]
    quarter = jnp.concatenate(
        [jnp.concatenate([dp_part(own[0]), dp_part(own[1])], axis=1), dp_part(own[2])], axis=0
    )
    part_rows = quarter.shape[0] * 25 // 36
    crossed_one = across(quarter[:part_rows])

    token_half = token_rows // 2
    cot_first = [shift(cotangent[:token_half], k) for k in range(1, half)]

    qkv_own = [w_query, key_weight, value_weight]
    qkv_half = (query_width + 2 * kv_width) // 2
    mine = jnp.concatenate([core_half(jnp.concatenate(qkv_own, axis=1)), core_half(w_out)], axis=1)
    near_one, near_two = dp_xor(mine, 1), dp_xor(mine, 2)
    tall = mine.shape[0] // 2
    got = [near_one, near_two, dp_xor(near_two[:tall], 1), dp_xor(near_one[tall:], 2)]
    slots = pair_slots(routes, pair_order[0], experts, capacity)
    slot_columns = jnp.pad(
        jnp.concatenate([slots // 128, slots % 128], axis=1).astype(f32),
        ((0, 0), (3 * experts, extra - 5 * experts)),
    )
    router_weight = jnp.pad(w_router, ((0, 0), (0, extra - experts)))
    router_weight_three = jnp.pad(jnp.concatenate([w_router] * 3, axis=1), ((0, 0), (0, extra - 3 * experts)))
    gain_one = norm_attn.reshape(1, features)
    gain_two = norm_moe.reshape(1, features)
    segment_columns = document_index.reshape(token_rows, 1)
    quarter_rest, cot_rest = quarter[part_rows:], cotangent[token_half:]
    ready, gain_one, gain_two, segment_columns, quarter_rest, cot_rest = after(
        (got, gain_one, gain_two, segment_columns, quarter_rest, cot_rest),
        crossed_one, cot_first, slot_columns, router_weight, router_weight_three,
    )
    pieces = [(v, swap(v)) for v in ready]
    crossed_two = across(quarter_rest)
    cot_second = [shift(after(cot_rest, pieces), k) for k in range(1, half)]
    cot_other = swap(after(cotangent, pieces))
    cot_first_other = [swap(after(v, pieces)) for v in cot_first]
    partner_one = lax.all_gather(after(crossed_one, pieces), "dp", axis=0, tiled=True)

    normed_one, qkv, mixture, totals = attend_call(
        place, tokens, gain_one, document_index, segment_columns, padding_token_mask, qkv_own, pieces
    )
    hidden_one, payload = route_call(
        place, after(mixture, crossed_two, cot_second, cot_other, cot_first_other), tokens, gain_two, router_weight,
        slot_columns, [w_out], pieces, experts,
    )

    payload_other = swap(payload)
    payload_far_same = [shift(payload, k) for k in range(1, half)]
    total_rows = chips // 2 * 2 * slot_rows

    two = after(crossed_two, payload_other)
    partner = [partner_one, two] + from_dp(two)
    spread = tuple((0, d * part_rows, part_rows, (False, d), 0) for d in range(data))
    spread += tuple((1 + k, 0, quarter.shape[0] - part_rows, (True, k), part_rows) for k in range(data))

    def rows_of(slot, sources, weights, prev, saved, base, cost=COST):
        return expert_call(
            hosted, (slot,), sources, weights, prev, saved, base, total_rows, experts, slot_rows, data, spread, cost
        )

    one = [(payload, payload_other, (cotangent,), (cot_other,))]
    near = rows_of(0, one, own, [], [], 0)
    near_saved = near[4:]
    near = rows_of(1, one, partner, near[:4], [], 0, LONG)
    payload_far_other = [swap(after(v, near[0])) for v in payload_far_same]
    cot_second_other = [swap(after(v, near[0])) for v in cot_second]
    many = list(zip(
        payload_far_same, payload_far_other, zip(cot_first, cot_second), zip(cot_first_other, cot_second_other)
    ))
    many = [(same, other, tuple(c_same), tuple(c_other)) for same, other, c_same, c_other in many]
    far = rows_of(1, many, partner, [], near[4:], 2 * slot_rows)
    partner_local = weight_gradient_call(far[4:], data)
    far = rows_of(0, many, own, far[:4], near_saved, 2 * slot_rows)
    saved = far[4:]

    def returned(near_same, near_other, far_same, far_other):
        sums = [
            (far_same[k].astype(f32) + swap(far_other[k]).astype(f32)).astype(bf16)
            for k in range(half - 1)
        ]
        return [near_same[0], swap(near_other[0])], sums

    def scattered(v):
        return lax.psum_scatter(v, "dp", scatter_dimension=0, tiled=True)

    partner_sum = scattered(partner_local)
    backs, back_sums = returned(near[2], near[3], far[2], far[3])
    backs += [shift(v, half - 1 - k) for k, v in enumerate(back_sums)]
    outs, out_sums = returned(near[0], after(near[1], back_sums), far[0], after(far[1], back_sums))
    own_local = weight_gradient_call([after(saved[0], back_sums, out_sums), *saved[1:]], data)
    own_sum = scattered(after(own_local, partner_sum, backs))
    grad_hidden, given, out_keep, out_give, local_norm_moe, local_router = branch_call(
        place, cotangent, hidden_one, payload, gain_two, router_weight_three, mixture, backs,
        [w_out], pieces, experts,
    )

    stages = chips.bit_length() - 1

    def chip_stage(part, stage, *others):
        there = stage < stages
        step = 1 << (stage if there else 2 * stages - 1 - stage)
        bit = lax.rem(me // 2 // step, 2)
        if there:
            size = part.shape[0] // 2
            keep = lax.dynamic_slice_in_dim(part, bit * size, size, axis=0)
            give = lax.dynamic_slice_in_dim(part, (1 - bit) * size, size, axis=0)
            return (keep.astype(f32) + chip_xor(after(give, *others), step).astype(f32)).astype(bf16)
        other = chip_xor(after(part, *others), step)
        return jnp.concatenate([jnp.where(bit == 0, part, other), jnp.where(bit == 0, other, part)], axis=0)

    rows = partner_sum.shape[0]
    thirds = jnp.split(partner_sum, (11 * rows // 36, 22 * rows // 36, 31 * rows // 36), axis=0)
    arrived_one = across(after(thirds[0], backs))
    arrived_two = across(after(thirds[1], arrived_one, grad_hidden))
    given, out_give = after((given, out_give), arrived_one)
    cuts = [0, 9 * token_rows // 40, 18 * token_rows // 40, 27 * token_rows // 40, token_rows]

    def out_parts(index, *others):
        rows = slice(cuts[index], cuts[index + 1])
        return [shift(after(v[rows], *others), half - 1 - k) for k, v in enumerate(out_sums)]

    outs_one = out_parts(0, backs)
    outs_two = out_parts(1, arrived_one, grad_hidden, outs_one)
    given, out_give = after((given, out_give), outs_one)
    out_got = swap(out_give)
    grad_qkv, qkv_keep, qkv_give = attend_back_call(
        place, document_index, segment_columns, padding_token_mask, qkv, totals, given, normed_one
    )
    qkv_give, out_got = after((qkv_give, out_got), arrived_two, outs_two)
    arrived_three = across(after(thirds[2], arrived_two))
    outs_three = out_parts(2, arrived_two, outs_two)
    out_folds = fold_first(place, out_keep, out_got, data)
    out_arrived = [dp_xor(out_folds[1], 2), dp_xor(out_folds[3], 1)]
    qkv_folds = fold_first(place, qkv_keep, swap(qkv_give), data)
    qkv_arrived = [dp_xor(qkv_folds[1], 2), dp_xor(qkv_folds[3], 1)]
    grad_tokens, local_norm_attn = input_grad_call(
        place, tokens, gain_one, after(grad_qkv, qkv_folds, out_folds, arrived_three, outs_three), grad_hidden, qkv_own, pieces
    )
    arrived_four = across(after(thirds[3], arrived_three))
    qkv_arrived, out_arrived = after((qkv_arrived, out_arrived), grad_tokens)
    local_router = local_router[:3 * experts].reshape(3, experts, features).sum(0)
    small = jnp.concatenate([local_router, local_norm_attn, local_norm_moe], axis=0)
    def folded(keep_a, give_a, keep_b, give_b):
        got_a, got_b = dp_xor(give_a, 1), dp_xor(give_b, 2)
        return jnp.concatenate([
            (keep.astype(f32) + got.astype(f32)).astype(bf16) for keep, got in ((keep_a, got_a), (keep_b, got_b))
        ], axis=1)

    qkv_folds = fold_second(place, qkv_folds[0], qkv_arrived[0], qkv_folds[2], qkv_arrived[1])
    outs_four = out_parts(3, grad_tokens)
    qkv_part = folded(*qkv_folds)
    out_part = folded(*fold_second(place, out_folds[0], out_arrived[0], out_folds[2], out_arrived[1]))
    arrived = jnp.concatenate([arrived_one, arrived_two, arrived_three, arrived_four], axis=0)
    expert_sum = (own_sum.astype(f32) + arrived.astype(f32)).astype(bf16)
    expert_sum, out_part, qkv_part = after((expert_sum, out_part, qkv_part))
    whole = lax.all_gather(expert_sum, "dp", axis=0, tiled=True)
    for stage in range(2 * stages):
        ahead = chip_stage(qkv_part, stage, *([outs_four] if stage == 2 else []))
        if stage:
            out_part = chip_stage(out_part, stage - 1, qkv_part)
        qkv_part = ahead
        if stage == 1:
            small, qkv_part = after((small, qkv_part))
    outs += [jnp.concatenate(v, axis=0) for v in zip(outs_one, outs_two, outs_three, outs_four)]
    routed = outs[0].astype(f32)
    for part in outs[1:]:
        routed = routed + part.astype(f32)
    block_out = (hidden_one + routed).astype(bf16)
    out_part = chip_stage(out_part, 2 * stages - 1, qkv_part)
    qkv_other = swap(qkv_part)
    small = small + swap(small)
    arrived = [dp_xor(small, k) for k in range(1, data)]
    grad_query, grad_key, grad_value = joined(
        place, qkv_part, qkv_other, (query_width, kv_width, kv_width)
    )
    arrived, grad_query, block_out = after((arrived, grad_query, block_out))
    for value in arrived:
        small = small + value
    (grad_out,) = joined(place, out_part, swap(out_part), (features,))
    if chips <= 4:
        arrived, grad_out = after(([chip_xor(small, k) for k in range(1, chips)], grad_out))
        for value in arrived:
            small = small + value
    else:
        for step in range(stages):
            small = small + chip_xor(small, 1 << step)
    whole, small, grad_out = after((whole, small, grad_out))
    grad_gate, grad_up, grad_down = widened(whole, data)
    grad_router = small[:experts].T
    grad_norm_attn = small[experts]
    grad_norm_moe = small[experts + 1]
    return (
        block_out,
        grad_tokens,
        grad_norm_attn,
        grad_norm_moe,
        grad_query,
        grad_key,
        grad_value,
        grad_out,
        grad_router,
        grad_gate[None],
        grad_up[None],
        grad_down[None],
    )


def solution(mesh):
    rows = P(("dp", "expert"), None)
    over_dp = P("dp", None)
    over_expert = P("expert", None, None)
    return jax.shard_map(
        body,
        mesh=mesh,
        in_specs=(
            rows, rows, P(), P(), over_dp, over_dp, over_dp, over_dp, P(),
            over_expert, over_expert, over_expert, rows, rows, rows, rows,
        ),
        out_specs=(
            rows, rows, P(), P(), over_dp, over_dp, over_dp, over_dp, P(),
            over_expert, over_expert, over_expert,
        ),
        check_vma=False,
    )
```
